32 devices in a mesh: groups: 2 (over y), wide: 16 (over z, x, core), narrow: 1.
Axes of the slice: x: 2, y: 2, z: 4, core: 2. Of those that a mesh axis runs over, the one named last changes fastest.
Arguments:
- tokens: bfloat16 [4096, 8192], P(('groups', 'wide'), 'narrow'), parts along dimension 0, may hold values from -6 to 6
- adapter_down_weight: bfloat16 [16, 2, 4096, 128], P(None, 'narrow', 'wide'), may hold values from -0.0625 to 0.0625
- adapter_up_weight: bfloat16 [16, 2, 512, 128], P(None, 'narrow', 'wide'), may hold values from -0.75 to 0.75
- adapter_entry: int32 [16], replicated, may hold values from 0 to 15, each once
- adapter_of_request: int32 [8], P('groups'), parts along dimension 0, may hold values from 0 to 15
- token_blocks_per_request: int32 [8], P('groups'), parts along dimension 0, may hold values from 1 to 8, 16 in all
Outputs:
- key_delta: bfloat16 [4096, 1024], P(('groups', 'wide'), 'narrow'), parts along dimension 0
- value_delta: bfloat16 [4096, 1024], P(('groups', 'wide'), 'narrow'), parts along dimension 0
The draws below stay inside these ranges and needn't reach their ends.
There are 2 independent parts, one for each index of `groups`. The reference program is written for one: setup_inputs(seed, part) draws one part's arguments, and reference() takes and returns one part's arrays. A program takes and returns all parts, laid end to end along the dimension named above; an argument that names none is the same for every part. Nothing has to cross between parts.
Inputs may be any that keep to these rules, and one draw needn't show every extreme that they name: `adapter_entry`: each table entry holds exactly one adapter. `token_blocks_per_request`: the counts sum to 16.
All inputs are finite; a program needn't handle non-finite values.
Results may differ from the reference program's by a relative error of at most 0.0049.
Values may be sent and summed in bfloat16 or wider, within the bound.
No kernel may reach another device: no remote copies, remote signals or barrier semaphores. Data moves between devices by JAX's collectives and lax.ppermute only.
A program may use at most 64 MiB of HBM per device.

```python
import math
import jax
import jax.numpy as jnp
import numpy as np
from jax import lax

MODEL_WIDTH = 8192
KEY_VALUE_WIDTH = 1024
ADAPTER_RANK = 64
BLK = 128
BLOCKS = 16
TOKENS = 2048
ADAPTER_TOTAL = 16
REQUESTS = 4
MOST = 8


def place_ends(result, rng, low, top_value):
    spot = [jax.random.randint(jax.random.fold_in(rng, axis), (), 0, length) for axis, length in enumerate(result.shape)]
    longest = result.shape.index(max(result.shape))
    beside = spot[:longest] + [(spot[longest] + 1) % result.shape[longest]] + spot[longest + 1:]
    return result.at[tuple(spot)].set(low).at[tuple(beside)].set(top_value)


def steps_of(own_key, extent, pieces, low, high):
    def one(position, shards_of):
        draws = jax.random.uniform(jax.random.fold_in(jax.random.fold_in(own_key, 6), position), (shards_of,), jnp.float32, low / len(pieces), high / len(pieces))
        return jnp.repeat(jnp.exp(draws), extent[position] // shards_of).reshape((-1,) + (1,) * (len(extent) - position - 1))

    factor_of = one(*pieces[0])
    for cut in pieces[1:]:
        factor_of = factor_of * one(*cut)
    return factor_of


def rank_bounds(count, skew):
    weights = [(1 << 20) // math.isqrt(rank ** skew) + 1 for rank in range(1, count + 1)]
    scale = 1 + sum(weights) // (1 << 30)
    return np.cumsum(np.array([max(1, weight // scale) for weight in weights]))


def ranked(stream_key, dims, count, lean):
    listing = rank_bounds(count, lean)
    lot = jax.random.randint(jax.random.fold_in(stream_key, 1), dims, 0, int(listing[count - 1]))
    rank = jnp.searchsorted(jnp.asarray(listing, jnp.int32), lot, side="right")
    return jax.random.permutation(jax.random.fold_in(stream_key, 2), count)[rank].astype(jnp.int32)


def split_up(count, total, reach, lean):
    loads = [(1 << 20) // math.isqrt(standing ** lean) + 1 for standing in range(2, count + 1)]
    rest, holding = total - reach - (count - 1), [1] * (count - 1)
    while rest > 0:
        movable = [i for i in range(count - 1) if holding[i] < reach]
        pool, left = sum([loads[i] for i in movable]), rest
        for i in movable:
            more = min(reach - holding[i], max(1, left * loads[i] // pool), rest)
            holding[i] = holding[i] + more
            rest = rest - more
    return np.array([reach] + holding)


def uneven_parts(rng, amount, total, bound, slope):
    if amount == 2:
        one = jax.random.randint(rng, (), max(1, total - bound), min(bound, total - 1) + 1)
        return jnp.stack([one, total - one])
    lengths = jnp.asarray(split_up(amount, total, bound, slope), jnp.int32)
    twos = (amount - 1) // 2
    source_of, sink = lengths[1:1 + 2 * twos:2], lengths[2:2 + 2 * twos:2]
    margin = jnp.minimum(source_of - 1, bound - sink)
    moved = jax.random.randint(jax.random.fold_in(rng, 1), (twos,), 0, 1 << 20) % (margin + 1)
    lengths = lengths.at[1:1 + 2 * twos:2].set(source_of - moved).at[2:2 + 2 * twos:2].set(sink + moved)
    return lengths[jax.random.permutation(jax.random.fold_in(rng, 2), amount)]


def normal_values(key, shape, width, most, cuts=(), held_as=jnp.bfloat16):
    loudness = steps_of(key, shape, cuts, -0.22, 0.18) if cuts else 1.0
    entries = jax.random.normal(key, shape, jnp.float32) * width * loudness
    return jnp.minimum(jnp.maximum(entries, -most), most).astype(held_as)


def setup_inputs(seed: int = 0, part: int = 0) -> dict:
    splits = jax.random.split(jax.random.key(seed), 7)
    part_keys = jax.random.split(jax.random.fold_in(splits[6], part), 7)
    return {
        "tokens": normal_values(part_keys[0], (TOKENS, MODEL_WIDTH), 1.0, 6.0, ((0, 16),)),
        "adapter_down_weight": normal_values(splits[1], (ADAPTER_TOTAL, 2, MODEL_WIDTH // 2, 2 * ADAPTER_RANK), MODEL_WIDTH ** -0.5, 0.0625, ((2, 16),)),
        "adapter_up_weight": normal_values(splits[2], (ADAPTER_TOTAL, 2, KEY_VALUE_WIDTH // 2, 2 * ADAPTER_RANK), ADAPTER_RANK ** -0.5, 0.75, ((2, 16),)),
        "adapter_entry": jax.random.permutation(splits[3], ADAPTER_TOTAL).astype(jnp.int32),
        "adapter_of_request": place_ends(ranked(part_keys[4], (REQUESTS,), ADAPTER_TOTAL, 2), jax.random.fold_in(part_keys[4], 3), 0, ADAPTER_TOTAL - 1).astype(jnp.int32),
        "token_blocks_per_request": uneven_parts(part_keys[5], REQUESTS, BLOCKS, MOST, 2).astype(jnp.int32),
    }


def block_tables(adapter_entry, adapter_of_request, token_blocks_per_request, block_count, request_count, adapter_count):
    request_ends = jnp.cumsum(token_blocks_per_request).astype(jnp.int32)
    block_index = jnp.arange(block_count, dtype=jnp.int32)
    request = jnp.sum((request_ends[None, :] <= block_index[:, None]).astype(jnp.int32), axis=1)
    pick_table = (request[:, None] == jnp.arange(request_count, dtype=jnp.int32)[None, :]).astype(jnp.int32)
    adapter = jnp.sum(pick_table * adapter_of_request[None, :], axis=1)
    slot_table = (adapter[:, None] == jnp.arange(adapter_count, dtype=jnp.int32)[None, :]).astype(jnp.int32)
    return jnp.sum(slot_table * adapter_entry[None, :], axis=1).astype(jnp.int32)


def reference(tokens, adapter_down_weight, adapter_up_weight, adapter_entry, adapter_of_request, token_blocks_per_request):
    slot_ids = block_tables(adapter_entry, adapter_of_request, token_blocks_per_request, BLOCKS, REQUESTS, ADAPTER_TOTAL)
    down_complete = adapter_down_weight.reshape(ADAPTER_TOTAL, MODEL_WIDTH, 2 * ADAPTER_RANK)
    up_complete = adapter_up_weight.reshape(ADAPTER_TOTAL, KEY_VALUE_WIDTH, 2 * ADAPTER_RANK)
    block_rows = tokens.reshape(BLOCKS, BLK, MODEL_WIDTH)

    def one_block(inputs_pair):
        rows_here, slot_here = inputs_pair
        down_block = down_complete[slot_here]
        up_block = up_complete[slot_here]
        shrink = jnp.dot(rows_here, down_block, preferred_element_type=jnp.float32)
        low_rank = shrink.astype(jnp.bfloat16)
        delta_key = jnp.dot(low_rank[:, :ADAPTER_RANK], up_block[:, :ADAPTER_RANK].T, preferred_element_type=jnp.float32)
        delta_value = jnp.dot(low_rank[:, ADAPTER_RANK:], up_block[:, ADAPTER_RANK:].T, preferred_element_type=jnp.float32)
        return delta_key.astype(jnp.bfloat16), delta_value.astype(jnp.bfloat16)

    key_delta, value_delta = lax.map(one_block, (block_rows, slot_ids))
    return key_delta.reshape(TOKENS, KEY_VALUE_WIDTH), value_delta.reshape(TOKENS, KEY_VALUE_WIDTH)
```

```python
import jax
import jax.numpy as jnp
from jax import lax
from jax.experimental import pallas as pl
from jax.experimental.pallas import tpu as pltpu
from jax.sharding import PartitionSpec as P

BLK = 128
PLANE = 4
SLOTS = 3


def block_tables(
    adapter_entry,
    adapter_of_request,
    token_blocks_per_request,
    block_count,
    request_count,
    adapter_count,
):
    request_ends = jnp.cumsum(token_blocks_per_request)
    block_index = jnp.arange(block_count, dtype=jnp.int32)
    request = jnp.sum((request_ends[None, :] <= block_index[:, None]).astype(jnp.int32), axis=1)
    pick_table = (request[:, None] == jnp.arange(request_count, dtype=jnp.int32)[None, :]).astype(
        jnp.int32
    )
    adapter = jnp.sum(pick_table * adapter_of_request[None, :], axis=1)
    slot_table = (adapter[:, None] == jnp.arange(adapter_count, dtype=jnp.int32)[None, :]).astype(
        jnp.int32
    )
    return jnp.sum(slot_table * adapter_entry[None, :], axis=1)


def direct_body(
    tokens,
    adapter_down_weight,
    adapter_up_weight,
    adapter_entry,
    adapter_of_request,
    token_blocks_per_request,
):
    wide_count = lax.axis_size("wide")
    blocks_dev = tokens.shape[0] // BLK
    local_width = tokens.shape[1]
    paired_ranks = adapter_down_weight.shape[3]
    rank_count = paired_ranks // 2
    slot_ids = block_tables(
        adapter_entry,
        adapter_of_request,
        token_blocks_per_request,
        blocks_dev * wide_count,
        token_blocks_per_request.shape[0],
        adapter_entry.shape[0],
    )
    needed_adapters = slot_ids.reshape(wide_count, blocks_dev).T
    down_outgoing = adapter_down_weight[needed_adapters]
    up_outgoing = adapter_up_weight[needed_adapters]
    got_down, got_up = (
        lax.all_to_all(down_outgoing, "wide", split_axis=1, concat_axis=3, tiled=True),
        lax.all_to_all(up_outgoing, "wide", split_axis=1, concat_axis=3, tiled=True),
    )
    got_down = got_down.reshape(blocks_dev, local_width, paired_ranks)
    block_rows = tokens.reshape(blocks_dev, BLK, local_width)
    shrink = jnp.einsum("btd,bdr->btr", block_rows, got_down, preferred_element_type=jnp.float32)
    low_rank = lax.psum(shrink, "narrow").astype(jnp.bfloat16)
    got_up = got_up.reshape(blocks_dev, -1, paired_ranks)
    delta_key = jnp.einsum(
        "btr,bjr->btj",
        low_rank[..., :rank_count],
        got_up[..., :rank_count],
        preferred_element_type=jnp.float32,
    )
    delta_value = jnp.einsum(
        "btr,bjr->btj",
        low_rank[..., rank_count:],
        got_up[..., rank_count:],
        preferred_element_type=jnp.float32,
    )
    out_cols = got_up.shape[1]
    key_delta = delta_key.reshape(blocks_dev * BLK, out_cols).astype(jnp.bfloat16)
    value_delta = delta_value.reshape(blocks_dev * BLK, out_cols).astype(jnp.bfloat16)
    return (key_delta, value_delta)


def swap(value, step):
    count = lax.axis_size("wide")
    return lax.ppermute(value, "wide", [(i, i ^ step) for i in range(count)])


def pick(index, values):
    got = values[0]
    for i in range(1, len(values)):
        got = jnp.where(index == i, values[i], got)
    return got


def prepare_kernel(
    planes,
    entry_ref,
    adapter_ref,
    counts_ref,
    tokens_ref,
    down_ref,
    up_ref,
    table_ref,
    *refs,
):
    others = planes - 1
    factors_out = refs[:others]
    tokens_out = refs[others : others + PLANE - 1]
    tokens_sem, down_sem, up_sem = refs[others + PLANE - 1 :]
    me = lax.axis_index("wide")
    column, plane = lax.rem(me, PLANE), lax.div(me, PLANE)
    run, up_run = down_ref.shape[2], up_ref.shape[2]
    copies = []
    for k in range(1, PLANE):
        for piece in range(2 * planes):
            start = piece * PLANE * run + (column ^ k) * run
            copies.append(
                pltpu.make_async_copy(
                    tokens_ref.at[:, pl.ds(pl.multiple_of(start, run), run)],
                    tokens_out[k - 1].at[piece],
                    tokens_sem.at[k - 1, piece],
                )
            )
            copies[-1].start()

    requests = counts_ref.shape[0]
    ends, total = [], 0
    for q in range(requests):
        total = total + counts_ref[q]
        ends.append(total)
    entries = [entry_ref[adapter_ref[q]] for q in range(requests)]
    slots, places, most = [], [], jnp.int32(1)
    for p in range(planes):
        ids = []
        for i in range(PLANE):
            got = entries[0]
            for q in range(1, requests):
                got = jnp.where(ends[q - 1] <= p * PLANE + i, entries[q], got)
            ids.append(got)
        place, held, count = [jnp.int32(0)], [ids[0]] * SLOTS, jnp.int32(1)
        for i in range(1, PLANE):
            found = count
            for j in range(i):
                found = jnp.where(ids[i] == ids[j], place[j], found)
            place.append(found)
            held = [jnp.where(found == s, ids[i], held[s]) for s in range(SLOTS)]
            count = jnp.maximum(count, found + 1)
        slots.append(held)
        places.append(place)
        most = jnp.maximum(most, count)
    for k in range(1, planes):
        there = plane ^ k
        for s in range(SLOTS):
            slot = pick(there, [slots[p][s] for p in range(planes)])
            copies.append(
                pltpu.make_async_copy(
                    down_ref.at[slot],
                    factors_out[k - 1].at[s, :, pl.ds(0, run)],
                    down_sem.at[k - 1, s],
                )
            )
            copies[-1].start()
            copies.append(
                pltpu.make_async_copy(
                    up_ref.at[slot],
                    factors_out[k - 1].at[s, :, pl.ds(run, up_run)],
                    up_sem.at[k - 1, s],
                )
            )
            copies[-1].start()
    here = [pick(plane, [places[p][i] for p in range(planes)]) for i in range(PLANE)]
    for k in range(PLANE):
        table_ref[k] = pick(column ^ k, here)
    for s in range(SLOTS):
        table_ref[PLANE + s] = pick(plane, [slots[p][s] for p in range(planes)])
    table_ref[PLANE + SLOTS] = most
    for copy in copies:
        copy.wait()


def prepare(planes, tokens, down, up, entry, adapter, counts):
    run, ranks = down.shape[2:]
    hbm = pl.BlockSpec(memory_space=pl.ANY)
    smem = pl.BlockSpec(memory_space=pltpu.SMEM)
    others = planes - 1
    factors = jax.ShapeDtypeStruct((SLOTS, 2, run + up.shape[2], ranks), down.dtype)
    return pl.pallas_call(
        lambda *refs: prepare_kernel(planes, *refs),
        out_shape=[jax.ShapeDtypeStruct((PLANE + SLOTS + 1,), jnp.int32)]
        + [factors] * others
        + [jax.ShapeDtypeStruct((2 * planes, BLK, run), tokens.dtype)] * (PLANE - 1),
        in_specs=[smem] * 3 + [hbm] * 3,
        out_specs=[smem] + [hbm] * (others + PLANE - 1),
        scratch_shapes=[
            pltpu.SemaphoreType.DMA((PLANE - 1, 2 * planes)),
            pltpu.SemaphoreType.DMA((others, SLOTS)),
            pltpu.SemaphoreType.DMA((others, SLOTS)),
        ],
        compiler_params=pltpu.CompilerParams(vmem_limit_bytes=2**20),
        name="prepare",
    )(entry, adapter, counts, tokens, down, up)


def shrink_kernel(planes, table_ref, tokens_ref, down_ref, up_ref, *refs):
    others = planes - 1
    got_tokens = refs[: PLANE - 1]
    got_factors = refs[PLANE - 1 : PLANE - 1 + others]
    own_ref, *sends, ups = refs[PLANE - 1 + others : 2 * PLANE + others]
    rows, factors, rows_sem, factors_sem, up_sem = refs[2 * PLANE + others :]
    me = lax.axis_index("wide")
    column, plane = lax.rem(me, PLANE), lax.div(me, PLANE)
    run, up_run = down_ref.shape[2], up_ref.shape[2]
    slots = factors.shape[0]
    copies = []
    for piece in range(2 * planes):
        start = piece * PLANE * run + column * run
        copies.append(
            pltpu.make_async_copy(
                tokens_ref.at[:, pl.ds(pl.multiple_of(start, run), run)],
                rows.at[0, piece],
                rows_sem.at[0, piece],
            )
        )
    for k in range(1, PLANE):
        copies.append(pltpu.make_async_copy(got_tokens[k - 1], rows.at[k], rows_sem.at[k, 0]))
    for s in range(slots):
        slot = table_ref[PLANE + s]
        copies.append(
            pltpu.make_async_copy(
                down_ref.at[slot], factors.at[s, plane, :, pl.ds(0, run)], factors_sem.at[0, s]
            )
        )
        copies.append(
            pltpu.make_async_copy(
                up_ref.at[slot], factors.at[s, plane, :, pl.ds(run, up_run)], up_sem.at[s]
            )
        )
        for d in range(1, planes):
            copies.append(
                pltpu.make_async_copy(
                    got_factors[d - 1].at[s], factors.at[s, plane ^ d], factors_sem.at[d, s]
                )
            )
    for copy in copies:
        copy.start()
    for copy in copies:
        copy.wait()
    for k in range(PLANE):
        place = table_ref[k]
        total = jnp.zeros(own_ref.shape, jnp.float32)
        for half in range(2):
            for p in range(planes):
                total += jnp.dot(
                    rows[k, half * planes + p],
                    factors[place, p, half, pl.ds(0, run)],
                    preferred_element_type=jnp.float32,
                )
        up_rows = factors[place, :, :, pl.ds(run, up_run)]
        if k == 0:
            own_ref[...] = total
            ups[...] = up_rows
        else:
            sends[k - 1][pl.ds(0, BLK)] = total.astype(sends[k - 1].dtype)
            sends[k - 1][pl.ds(BLK, 2 * planes * up_run)] = up_rows.reshape(-1, up_rows.shape[-1])


def shrink(planes, slots, table, tokens, down, up, got_tokens, got_factors):
    hbm = pl.BlockSpec(memory_space=pl.ANY)
    vmem = pl.BlockSpec(memory_space=pltpu.VMEM)
    run, ranks = down.shape[2:]
    up_run = up.shape[2]
    send = jax.ShapeDtypeStruct((BLK + 2 * planes * up_run, ranks), tokens.dtype)
    return pl.pallas_call(
        lambda *refs: shrink_kernel(planes, *refs),
        out_shape=[jax.ShapeDtypeStruct((BLK, ranks), jnp.float32)] + [send] * (PLANE - 1)
        + [jax.ShapeDtypeStruct((planes, 2, up_run, ranks), up.dtype)],
        in_specs=[pl.BlockSpec(memory_space=pltpu.SMEM)] + [hbm] * (planes + PLANE + 1),
        out_specs=[vmem] * (PLANE + 1),
        scratch_shapes=[
            pltpu.VMEM((PLANE, 2 * planes, BLK, run), tokens.dtype),
            pltpu.VMEM((slots, planes, 2, run + up_run, ranks), down.dtype),
            pltpu.SemaphoreType.DMA((PLANE, 2 * planes)),
            pltpu.SemaphoreType.DMA((planes, slots)),
            pltpu.SemaphoreType.DMA((slots,)),
        ],
        compiler_params=pltpu.CompilerParams(vmem_limit_bytes=8 * 2**20),
        name="shrink",
    )(table, tokens, down, up, *got_tokens, *got_factors)


def expand_kernel(own_ref, up_ref, *refs):
    got = refs[: PLANE - 1]
    key_ref, value_ref, factor = refs[PLANE - 1 :]
    column = lax.rem(lax.axis_index("wide"), PLANE)
    planes, _, up_run, ranks = up_ref.shape
    total = own_ref[...]
    factor[:, :, column] = up_ref[...]
    for k in range(1, PLANE):
        total += got[k - 1][pl.ds(0, BLK)].astype(jnp.float32)
        factor[:, :, column ^ k] = got[k - 1][pl.ds(BLK, 2 * planes * up_run)].reshape(up_ref.shape)
    low_rank = total.astype(jnp.bfloat16)
    is_key = lax.broadcasted_iota(jnp.int32, low_rank.shape, 1) < ranks // 2
    zero = jnp.zeros_like(low_rank)
    both = jnp.concatenate(
        [jnp.where(is_key, low_rank, zero), jnp.where(is_key, zero, low_rank)], axis=0
    )
    for half in range(2):
        for p in range(planes):
            delta = lax.dot_general(
                both,
                factor[p, half].reshape(PLANE * up_run, ranks),
                (((1,), (1,)), ((), ())),
                preferred_element_type=jnp.float32,
            ).astype(jnp.bfloat16)
            columns = pl.ds((half * planes + p) * PLANE * up_run, PLANE * up_run)
            key_ref[:, columns] = delta[:BLK]
            value_ref[:, columns] = delta[BLK:]


def expand(own, up, got):
    planes, _, up_run, ranks = up.shape
    columns = 2 * planes * PLANE * up_run
    vmem = pl.BlockSpec(memory_space=pltpu.VMEM)
    return pl.pallas_call(
        expand_kernel,
        out_shape=[jax.ShapeDtypeStruct((BLK, columns), jnp.bfloat16)] * 2,
        in_specs=[vmem] * (PLANE + 1),
        out_specs=[vmem] * 2,
        scratch_shapes=[pltpu.VMEM((planes, 2, PLANE, up_run, ranks), jnp.bfloat16)],
        compiler_params=pltpu.CompilerParams(vmem_limit_bytes=4 * 2**20),
        name="expand",
    )(own, up, *got)


def plane_body(
    tokens,
    adapter_down_weight,
    adapter_up_weight,
    adapter_entry,
    adapter_of_request,
    token_blocks_per_request,
):
    planes = lax.axis_size("wide") // PLANE
    others = planes - 1
    table, *sends = prepare(
        planes,
        tokens,
        adapter_down_weight,
        adapter_up_weight,
        adapter_entry,
        adapter_of_request,
        token_blocks_per_request,
    )

    def rest(slots, table, tokens, down, up, factors_sends, tokens_sends):
        got_factors = [swap(factors_sends[d - 1][:slots], d * PLANE) for d in range(1, planes)]
        got_tokens = [swap(tokens_sends[k - 1], k) for k in range(1, PLANE)]
        own, *sends, ups = shrink(planes, slots, table, tokens, down, up, got_tokens, got_factors)
        got = [swap(sends[k - 1], k) for k in range(1, PLANE)]
        return tuple(expand(own, ups, got))

    return lax.cond(
        table[PLANE + SLOTS] > 2,
        lambda *operands: rest(3, *operands),
        lambda *operands: rest(2, *operands),
        table,
        tokens,
        adapter_down_weight,
        adapter_up_weight,
        sends[:others],
        sends[others:],
    )


def solution(mesh):
    by_plane = mesh.shape["wide"] == 16 and mesh.shape["narrow"] == 1
    return jax.shard_map(
        plane_body if by_plane else direct_body,
        mesh=mesh,
        in_specs=(
            P(("groups", "wide"), "narrow"),
            P(None, "narrow", "wide", None),
            P(None, "narrow", "wide", None),
            P(),
            P("groups"),
            P("groups"),
        ),
        out_specs=(P(("groups", "wide"), "narrow"), P(("groups", "wide"), "narrow")),
        check_vma=False,
    )
```

```python
import jax
import jax.numpy as jnp
from jax import lax
from jax.experimental import pallas as pl
from jax.experimental.pallas import tpu as pltpu
from jax.sharding import PartitionSpec as P

BLK = 128
PLANE = 4
SLOTS = 3
USUAL = 2


def block_tables(
    adapter_entry,
    adapter_of_request,
    token_blocks_per_request,
    block_count,
    request_count,
    adapter_count,
):
    request_ends = jnp.cumsum(token_blocks_per_request)
    block_index = jnp.arange(block_count, dtype=jnp.int32)
    request = jnp.sum((request_ends[None, :] <= block_index[:, None]).astype(jnp.int32), axis=1)
    pick_table = (request[:, None] == jnp.arange(request_count, dtype=jnp.int32)[None, :]).astype(
        jnp.int32
    )
    adapter = jnp.sum(pick_table * adapter_of_request[None, :], axis=1)
    slot_table = (adapter[:, None] == jnp.arange(adapter_count, dtype=jnp.int32)[None, :]).astype(
        jnp.int32
    )
    return jnp.sum(slot_table * adapter_entry[None, :], axis=1)


def direct_body(
    tokens,
    adapter_down_weight,
    adapter_up_weight,
    adapter_entry,
    adapter_of_request,
    token_blocks_per_request,
):
    wide_count = lax.axis_size("wide")
    blocks_dev = tokens.shape[0] // BLK
    local_width = tokens.shape[1]
    paired_ranks = adapter_down_weight.shape[3]
    rank_count = paired_ranks // 2
    slot_ids = block_tables(
        adapter_entry,
        adapter_of_request,
        token_blocks_per_request,
        blocks_dev * wide_count,
        token_blocks_per_request.shape[0],
        adapter_entry.shape[0],
    )
    needed_adapters = slot_ids.reshape(wide_count, blocks_dev).T
    down_outgoing = adapter_down_weight[needed_adapters]
    up_outgoing = adapter_up_weight[needed_adapters]
    got_down, got_up = (
        lax.all_to_all(down_outgoing, "wide", split_axis=1, concat_axis=3, tiled=True),
        lax.all_to_all(up_outgoing, "wide", split_axis=1, concat_axis=3, tiled=True),
    )
    got_down = got_down.reshape(blocks_dev, local_width, paired_ranks)
    block_rows = tokens.reshape(blocks_dev, BLK, local_width)
    shrink = jnp.einsum("btd,bdr->btr", block_rows, got_down, preferred_element_type=jnp.float32)
    low_rank = lax.psum(shrink, "narrow").astype(jnp.bfloat16)
    got_up = got_up.reshape(blocks_dev, -1, paired_ranks)
    delta_key = jnp.einsum(
        "btr,bjr->btj",
        low_rank[..., :rank_count],
        got_up[..., :rank_count],
        preferred_element_type=jnp.float32,
    )
    delta_value = jnp.einsum(
        "btr,bjr->btj",
        low_rank[..., rank_count:],
        got_up[..., rank_count:],
        preferred_element_type=jnp.float32,
    )
    out_cols = got_up.shape[1]
    key_delta = delta_key.reshape(blocks_dev * BLK, out_cols).astype(jnp.bfloat16)
    value_delta = delta_value.reshape(blocks_dev * BLK, out_cols).astype(jnp.bfloat16)
    return (key_delta, value_delta)


def swap(value, step):
    count = lax.axis_size("wide")
    return lax.ppermute(value, "wide", [(i, i ^ step) for i in range(count)])


def pick(index, values):
    got = values[0]
    for i in range(1, len(values)):
        got = jnp.where(index == i, values[i], got)
    return got


def prepare_kernel(
    planes,
    entry_hbm,
    adapter_hbm,
    counts_hbm,
    tokens_ref,
    down_ref,
    up_ref,
    places_ref,
    many_ref,
    *refs,
):
    factors_out = refs[:planes]
    tokens_out = refs[planes : planes + PLANE]
    entry_ref, adapter_ref, counts_ref = refs[planes + PLANE : planes + PLANE + 3]
    small_sem, tokens_sem, down_sem, up_sem = refs[planes + PLANE + 3 :]
    me = lax.axis_index("wide")
    column, plane = lax.rem(me, PLANE), lax.div(me, PLANE)
    run, up_run = down_ref.shape[2], up_ref.shape[2]
    small = [
        pltpu.make_async_copy(entry_hbm, entry_ref, small_sem.at[0]),
        pltpu.make_async_copy(adapter_hbm, adapter_ref, small_sem.at[1]),
        pltpu.make_async_copy(counts_hbm, counts_ref, small_sem.at[2]),
    ]
    for copy in small:
        copy.start()
    copies = []
    for k in range(PLANE):
        for piece in range(2 * planes):
            start = piece * PLANE * run + (column ^ k) * run
            copies.append(
                pltpu.make_async_copy(
                    tokens_ref.at[:, pl.ds(pl.multiple_of(start, run), run)],
                    tokens_out[k].at[piece],
                    tokens_sem.at[k, piece],
                )
            )
            copies[-1].start()
    for copy in small:
        copy.wait()

    requests = counts_ref.shape[0]
    ends, total = [], 0
    for q in range(requests):
        total = total + counts_ref[q]
        ends.append(total)
    entries = [entry_ref[adapter_ref[q]] for q in range(requests)]
    slots, places, most = [], [], jnp.int32(1)
    for p in range(planes):
        ids = []
        for i in range(PLANE):
            got = entries[0]
            for q in range(1, requests):
                got = jnp.where(ends[q - 1] <= p * PLANE + i, entries[q], got)
            ids.append(got)
        place, held, count = [jnp.int32(0)], [ids[0]] * SLOTS, jnp.int32(1)
        for i in range(1, PLANE):
            found = count
            for j in range(i):
                found = jnp.where(ids[i] == ids[j], place[j], found)
            place.append(found)
            held = [jnp.where(found == s, ids[i], held[s]) for s in range(SLOTS)]
            count = jnp.maximum(count, found + 1)
        slots.append(held)
        places.append(place)
        most = jnp.maximum(most, count)

    def send_rows(k, s):
        slot = pick(plane ^ k, [held[s] for held in slots])
        out = factors_out[k].at[s]
        return (
            pltpu.make_async_copy(down_ref.at[slot], out.at[:, pl.ds(0, run)], down_sem.at[k, s]),
            pltpu.make_async_copy(up_ref.at[slot], out.at[:, pl.ds(run, up_run)], up_sem.at[k, s]),
        )

    for k in range(planes):
        for s in range(USUAL):
            for copy in send_rows(k, s):
                copy.start()
                copies.append(copy)
    here = [pick(plane, [place[i] for place in places]) for i in range(PLANE)]
    for k in range(PLANE):
        places_ref[k] = pick(column ^ k, here)
    many_ref[0] = jnp.where(most > USUAL, 1, 0)

    @pl.when(most > USUAL)
    def _():
        more = [copy for k in range(planes) for s in range(USUAL, SLOTS) for copy in send_rows(k, s)]
        for copy in more:
            copy.start()
        for copy in more:
            copy.wait()

    for copy in copies:
        copy.wait()


def prepare(planes, tokens, down, up, entry, adapter, counts):
    run, ranks = down.shape[2:]
    hbm = pl.BlockSpec(memory_space=pltpu.HBM)
    smem = pl.BlockSpec(memory_space=pltpu.SMEM)
    factors = jax.ShapeDtypeStruct((SLOTS, 2, run + up.shape[2], ranks), down.dtype)
    rows = jax.ShapeDtypeStruct((2 * planes, BLK, run), tokens.dtype)
    return pl.pallas_call(
        lambda *refs: prepare_kernel(planes, *refs),
        out_shape=[jax.ShapeDtypeStruct((PLANE,), jnp.int32), jax.ShapeDtypeStruct((1,), jnp.int32)]
        + [factors] * planes
        + [rows] * PLANE,
        in_specs=[hbm] * 6,
        out_specs=[smem] * 2 + [pl.BlockSpec(memory_space=pltpu.VMEM)] * (planes + PLANE),
        scratch_shapes=[
            pltpu.SMEM(entry.shape, jnp.int32),
            pltpu.SMEM(adapter.shape, jnp.int32),
            pltpu.SMEM(counts.shape, jnp.int32),
            pltpu.SemaphoreType.DMA((3,)),
            pltpu.SemaphoreType.DMA((PLANE, 2 * planes)),
            pltpu.SemaphoreType.DMA((planes, SLOTS)),
            pltpu.SemaphoreType.DMA((planes, SLOTS)),
        ],
        compiler_params=pltpu.CompilerParams(vmem_limit_bytes=59 * 2**20),
        name="prepare",
    )(entry, adapter, counts, tokens, down, up)


def shrink_kernel(planes, slots, run, places_ref, *refs):
    rows = refs[:PLANE]
    factors = refs[PLANE : PLANE + planes]
    own_ref, *sends, ups = refs[PLANE + planes :]
    plane = lax.div(lax.axis_index("wide"), PLANE)
    up_run, ranks = ups.shape[2:]
    places = [places_ref[k] for k in range(PLANE)]
    for k in range(PLANE):
        for d in range(planes):
            for half in range(2):
                up_rows = factors[d][places[k], half, pl.ds(run, up_run)]
                if k == 0:
                    ups[plane ^ d, half] = up_rows
                else:
                    start = BLK + ((plane ^ d) * 2 + half) * up_run
                    sends[k - 1][pl.ds(pl.multiple_of(start, up_run), up_run)] = up_rows
    total = jnp.zeros((PLANE * BLK, slots * ranks), jnp.float32)
    for d in range(planes):
        for half in range(2):
            total += jnp.dot(
                jnp.concatenate([rows[k][half * planes + (plane ^ d)] for k in range(PLANE)], axis=0),
                jnp.concatenate([factors[d][s, half, pl.ds(0, run)] for s in range(slots)], axis=1),
                preferred_element_type=jnp.float32,
            )
    for k in range(PLANE):
        of_block = total[k * BLK : (k + 1) * BLK]
        mine = pick(places[k], [of_block[:, s * ranks : (s + 1) * ranks] for s in range(slots)])
        if k == 0:
            own_ref[...] = mine
        else:
            sends[k - 1][pl.ds(0, BLK)] = mine.astype(sends[k - 1].dtype)


def shrink(planes, slots, places, rows, factors, up_run):
    vmem = pl.BlockSpec(memory_space=pltpu.VMEM)
    run, ranks = factors[0].shape[2] - up_run, factors[0].shape[3]
    send = jax.ShapeDtypeStruct((BLK + 2 * planes * up_run, ranks), rows[0].dtype)
    return pl.pallas_call(
        lambda *refs: shrink_kernel(planes, slots, run, *refs),
        out_shape=[jax.ShapeDtypeStruct((BLK, ranks), jnp.float32)]
        + [send] * (PLANE - 1)
        + [jax.ShapeDtypeStruct((planes, 2, up_run, ranks), factors[0].dtype)],
        in_specs=[pl.BlockSpec(memory_space=pltpu.SMEM)] + [vmem] * (PLANE + planes),
        out_specs=[vmem] * (PLANE + 1),
        compiler_params=pltpu.CompilerParams(vmem_limit_bytes=10 * 2**20),
        name="shrink",
    )(places, *rows, *factors)


def expand_kernel(own_ref, up_ref, *refs):
    got = refs[: PLANE - 1]
    key_ref, value_ref, factor = refs[PLANE - 1 :]
    column = lax.rem(lax.axis_index("wide"), PLANE)
    planes, _, up_run, ranks = up_ref.shape
    total = own_ref[...]
    factor[:, :, column] = up_ref[...]
    for k in range(1, PLANE):
        total += got[k - 1][pl.ds(0, BLK)].astype(jnp.float32)
        factor[:, :, column ^ k] = got[k - 1][pl.ds(BLK, 2 * planes * up_run)].reshape(up_ref.shape)
    low_rank = total.astype(jnp.bfloat16)
    is_key = lax.broadcasted_iota(jnp.int32, low_rank.shape, 1) < ranks // 2
    zero = jnp.zeros_like(low_rank)
    both = jnp.concatenate(
        [jnp.where(is_key, low_rank, zero), jnp.where(is_key, zero, low_rank)], axis=0
    )
    for half in range(2):
        for p in range(planes):
            delta = lax.dot_general(
                both,
                factor[p, half].reshape(PLANE * up_run, ranks),
                (((1,), (1,)), ((), ())),
                preferred_element_type=jnp.float32,
            ).astype(jnp.bfloat16)
            columns = pl.ds((half * planes + p) * PLANE * up_run, PLANE * up_run)
            key_ref[:, columns] = delta[:BLK]
            value_ref[:, columns] = delta[BLK:]


def expand(own, up, got):
    planes, _, up_run, ranks = up.shape
    columns = 2 * planes * PLANE * up_run
    vmem = pl.BlockSpec(memory_space=pltpu.VMEM)
    return pl.pallas_call(
        expand_kernel,
        out_shape=[jax.ShapeDtypeStruct((BLK, columns), jnp.bfloat16)] * 2,
        in_specs=[vmem] * (PLANE + 1),
        out_specs=[vmem] * 2,
        scratch_shapes=[pltpu.VMEM((planes, 2, PLANE, up_run, ranks), jnp.bfloat16)],
        compiler_params=pltpu.CompilerParams(vmem_limit_bytes=4 * 2**20),
        name="expand",
    )(own, up, *got)


def plane_body(
    tokens,
    adapter_down_weight,
    adapter_up_weight,
    adapter_entry,
    adapter_of_request,
    token_blocks_per_request,
):
    planes = lax.axis_size("wide") // PLANE
    places, many, *sends = prepare(
        planes,
        tokens,
        adapter_down_weight,
        adapter_up_weight,
        adapter_entry,
        adapter_of_request,
        token_blocks_per_request,
    )
    factors, rows = sends[:planes], sends[planes:]
    beside = swap(rows[1], 1)

    def rest(slots, places, factors, rows, beside):
        factors = [factors[0]] + [swap(factors[d][:slots], d * PLANE) for d in range(1, planes)]
        rows = [rows[0], beside] + [swap(rows[k], k) for k in range(2, PLANE)]
        own, *sends, ups = shrink(planes, slots, places, rows, factors, adapter_up_weight.shape[2])
        got = [swap(sends[k - 1], k) for k in range(1, PLANE)]
        return tuple(expand(own, ups, got))

    return lax.switch(
        many[0],
        [lambda *operands: rest(USUAL, *operands), lambda *operands: rest(SLOTS, *operands)],
        places,
        factors,
        rows,
        beside,
    )


def solution(mesh):
    by_plane = mesh.shape["wide"] == 16 and mesh.shape["narrow"] == 1
    return jax.shard_map(
        plane_body if by_plane else direct_body,
        mesh=mesh,
        in_specs=(
            P(("groups", "wide"), "narrow"),
            P(None, "narrow", "wide", None),
            P(None, "narrow", "wide", None),
            P(),
            P("groups"),
            P("groups"),
        ),
        out_specs=(P(("groups", "wide"), "narrow"), P(("groups", "wide"), "narrow")),
        check_vma=False,
    )
```

```python
import jax
import jax.numpy as jnp
from jax import lax
from jax.experimental import pallas as pl
from jax.experimental.pallas import tpu as pltpu
from jax.sharding import PartitionSpec as P

BLK = 128
PLANE = 4
SLOTS = 3
USUAL = 2


def block_tables(
    adapter_entry,
    adapter_of_request,
    token_blocks_per_request,
    block_count,
    request_count,
    adapter_count,
):
    request_ends = jnp.cumsum(token_blocks_per_request)
    block_index = jnp.arange(block_count, dtype=jnp.int32)
    request = jnp.sum((request_ends[None, :] <= block_index[:, None]).astype(jnp.int32), axis=1)
    pick_table = (request[:, None] == jnp.arange(request_count, dtype=jnp.int32)[None, :]).astype(
        jnp.int32
    )
    adapter = jnp.sum(pick_table * adapter_of_request[None, :], axis=1)
    slot_table = (adapter[:, None] == jnp.arange(adapter_count, dtype=jnp.int32)[None, :]).astype(
        jnp.int32
    )
    return jnp.sum(slot_table * adapter_entry[None, :], axis=1)


def direct_body(
    tokens,
    adapter_down_weight,
    adapter_up_weight,
    adapter_entry,
    adapter_of_request,
    token_blocks_per_request,
):
    wide_count = lax.axis_size("wide")
    blocks_dev = tokens.shape[0] // BLK
    local_width = tokens.shape[1]
    paired_ranks = adapter_down_weight.shape[3]
    rank_count = paired_ranks // 2
    slot_ids = block_tables(
        adapter_entry,
        adapter_of_request,
        token_blocks_per_request,
        blocks_dev * wide_count,
        token_blocks_per_request.shape[0],
        adapter_entry.shape[0],
    )
    needed_adapters = slot_ids.reshape(wide_count, blocks_dev).T
    down_outgoing = adapter_down_weight[needed_adapters]
    up_outgoing = adapter_up_weight[needed_adapters]
    got_down, got_up = (
        lax.all_to_all(down_outgoing, "wide", split_axis=1, concat_axis=3, tiled=True),
        lax.all_to_all(up_outgoing, "wide", split_axis=1, concat_axis=3, tiled=True),
    )
    got_down = got_down.reshape(blocks_dev, local_width, paired_ranks)
    block_rows = tokens.reshape(blocks_dev, BLK, local_width)
    shrink = jnp.einsum("btd,bdr->btr", block_rows, got_down, preferred_element_type=jnp.float32)
    low_rank = lax.psum(shrink, "narrow").astype(jnp.bfloat16)
    got_up = got_up.reshape(blocks_dev, -1, paired_ranks)
    delta_key = jnp.einsum(
        "btr,bjr->btj",
        low_rank[..., :rank_count],
        got_up[..., :rank_count],
        preferred_element_type=jnp.float32,
    )
    delta_value = jnp.einsum(
        "btr,bjr->btj",
        low_rank[..., rank_count:],
        got_up[..., rank_count:],
        preferred_element_type=jnp.float32,
    )
    out_cols = got_up.shape[1]
    key_delta = delta_key.reshape(blocks_dev * BLK, out_cols).astype(jnp.bfloat16)
    value_delta = delta_value.reshape(blocks_dev * BLK, out_cols).astype(jnp.bfloat16)
    return (key_delta, value_delta)


def swap(value, step):
    count = lax.axis_size("wide")
    return lax.ppermute(value, "wide", [(i, i ^ step) for i in range(count)])


def pick(index, values):
    got = values[0]
    for i in range(1, len(values)):
        got = jnp.where(index == i, values[i], got)
    return got


def prepare_kernel(
    planes,
    entry_hbm,
    adapter_hbm,
    counts_hbm,
    tokens_ref,
    down_ref,
    up_ref,
    places_ref,
    many_ref,
    *refs,
):
    factors_out = refs[:planes]
    tokens_out = refs[planes : planes + PLANE]
    entry_ref, adapter_ref, counts_ref = refs[planes + PLANE : planes + PLANE + 3]
    small_sem, tokens_sem, down_sem, up_sem = refs[planes + PLANE + 3 :]
    me = lax.axis_index("wide")
    column, plane = lax.rem(me, PLANE), lax.div(me, PLANE)
    run, up_run = down_ref.shape[2], up_ref.shape[2]
    small = [
        pltpu.make_async_copy(entry_hbm, entry_ref, small_sem.at[0]),
        pltpu.make_async_copy(adapter_hbm, adapter_ref, small_sem.at[1]),
        pltpu.make_async_copy(counts_hbm, counts_ref, small_sem.at[2]),
    ]
    for copy in small:
        copy.start()
    copies = []
    for k in range(PLANE):
        for piece in range(2 * planes):
            start = piece * PLANE * run + (column ^ k) * run
            copies.append(
                pltpu.make_async_copy(
                    tokens_ref.at[:, pl.ds(pl.multiple_of(start, run), run)],
                    tokens_out[k].at[piece],
                    tokens_sem.at[k, piece],
                )
            )
            copies[-1].start()
    for copy in small:
        copy.wait()

    requests = counts_ref.shape[0]
    ends, total = [], 0
    for q in range(requests):
        total = total + counts_ref[q]
        ends.append(total)
    entries = [entry_ref[adapter_ref[q]] for q in range(requests)]
    slots, places, most = [], [], jnp.int32(1)
    for p in range(planes):
        ids = []
        for i in range(PLANE):
            got = entries[0]
            for q in range(1, requests):
                got = jnp.where(ends[q - 1] <= p * PLANE + i, entries[q], got)
            ids.append(got)
        order = range(PLANE) if p % 2 == 0 else range(PLANE - 1, -1, -1)
        ids = [ids[i] for i in order]
        place, held, count = [jnp.int32(0)], [ids[0]] * SLOTS, jnp.int32(1)
        for i in range(1, PLANE):
            found = count
            for j in range(i):
                found = jnp.where(ids[i] == ids[j], place[j], found)
            place.append(found)
            held = [jnp.where(found == s, ids[i], held[s]) for s in range(SLOTS)]
            count = jnp.maximum(count, found + 1)
        place = [place[i] for i in order]
        slots.append(held)
        places.append(place)
        most = jnp.maximum(most, count)

    kept = [out.shape[0] for out in factors_out]

    def send_rows(k, s):
        slot = pick(plane ^ k, [held[s] for held in slots])
        out = factors_out[k].at[s]
        return (
            pltpu.make_async_copy(down_ref.at[slot], out.at[:, pl.ds(0, run)], down_sem.at[k, s]),
            pltpu.make_async_copy(up_ref.at[slot], out.at[:, pl.ds(run, up_run)], up_sem.at[k, s]),
        )

    for k in reversed(range(planes)):
        for s in range(kept[k]):
            for copy in send_rows(k, s):
                copy.start()
                copies.append(copy)
    here = [pick(plane, [place[i] for place in places]) for i in range(PLANE)]
    for k in range(PLANE):
        places_ref[k] = pick(column ^ k, here)
    many_ref[0] = jnp.where(most > USUAL, 1, 0)

    for copy in copies:
        copy.wait()


def prepare(planes, tokens, down, up, entry, adapter, counts):
    run, ranks = down.shape[2:]
    hbm = pl.BlockSpec(memory_space=pltpu.HBM)
    smem = pl.BlockSpec(memory_space=pltpu.SMEM)
    rows_of = (2, run + up.shape[2], ranks)
    factors = [
        jax.ShapeDtypeStruct((SLOTS if k < 2 else USUAL,) + rows_of, down.dtype) for k in range(planes)
    ]
    rows = jax.ShapeDtypeStruct((2 * planes, BLK, run), tokens.dtype)
    return pl.pallas_call(
        lambda *refs: prepare_kernel(planes, *refs),
        out_shape=[jax.ShapeDtypeStruct((PLANE,), jnp.int32), jax.ShapeDtypeStruct((1,), jnp.int32)]
        + factors
        + [rows] * PLANE,
        in_specs=[hbm] * 6,
        out_specs=[smem] * 2 + [pl.BlockSpec(memory_space=pltpu.VMEM)] * (planes + PLANE),
        scratch_shapes=[
            pltpu.SMEM(entry.shape, jnp.int32),
            pltpu.SMEM(adapter.shape, jnp.int32),
            pltpu.SMEM(counts.shape, jnp.int32),
            pltpu.SemaphoreType.DMA((3,)),
            pltpu.SemaphoreType.DMA((PLANE, 2 * planes)),
            pltpu.SemaphoreType.DMA((planes, SLOTS)),
            pltpu.SemaphoreType.DMA((planes, SLOTS)),
        ],
        compiler_params=pltpu.CompilerParams(vmem_limit_bytes=59 * 2**20),
        name="prepare",
    )(entry, adapter, counts, tokens, down, up)


def shrink_kernel(planes, slots, run, up_run, blocks, distances, add, places_ref, *refs):
    rows = refs[: len(blocks)]
    factors = dict(zip(distances, refs[len(blocks) :]))
    refs = refs[len(blocks) + len(distances) :]
    held, outs = (refs[0], refs[1:]) if add else (None, refs)
    plane = lax.div(lax.axis_index("wide"), PLANE)
    ranks = factors[distances[-1]].shape[3]
    places = [places_ref[k] for k in blocks]
    last = len(outs) == len(blocks)
    if last:
        for place, out in zip(places, outs):
            for d in range(planes):
                for half in range(2):
                    start = BLK + ((plane ^ d) * 2 + half) * up_run
                    out[pl.ds(pl.multiple_of(start, up_run), up_run)] = factors[d][
                        place, half, pl.ds(run, up_run)
                    ]
    total = jnp.zeros((len(blocks) * BLK, slots * ranks), jnp.float32)
    for d in distances:
        if last and add and d == 0:
            continue
        for half in range(2):
            total += jnp.dot(
                jnp.concatenate([part[half * planes + (plane ^ d)] for part in rows], axis=0),
                jnp.concatenate([factors[d][s, half, pl.ds(0, run)] for s in range(slots)], axis=1),
                preferred_element_type=jnp.float32,
            )
    for i, place in enumerate(places):
        span = pl.ds(i * BLK, BLK)
        of_block = total[i * BLK : (i + 1) * BLK]
        mine = pick(place, [of_block[:, s * ranks : (s + 1) * ranks] for s in range(slots)])
        if not last:
            outs[0][span] = mine
        else:
            mine = mine + held[span] if add else mine
            outs[i][pl.ds(0, BLK)] = mine.astype(outs[i].dtype)


def shrink(planes, slots, blocks, distances, places, rows, factors, up_run, held=None, last=True, flops=None):
    vmem = pl.BlockSpec(memory_space=pltpu.VMEM)
    run, ranks = factors[0].shape[2] - up_run, factors[0].shape[3]
    if last:
        outs = [jax.ShapeDtypeStruct((BLK + 2 * planes * up_run, ranks), rows[0].dtype)] * len(blocks)
    else:
        outs = [jax.ShapeDtypeStruct((len(blocks) * BLK, ranks), jnp.float32)]
    add = [] if held is None else [held]
    cost = None
    if flops is not None:
        cost = pl.CostEstimate(flops=flops, bytes_accessed=0, transcendentals=0)
    return pl.pallas_call(
        lambda *refs: shrink_kernel(planes, slots, run, up_run, blocks, distances, bool(add), *refs),
        out_shape=outs,
        in_specs=[pl.BlockSpec(memory_space=pltpu.SMEM)]
        + [vmem] * (len(blocks) + len(distances) + len(add)),
        out_specs=[vmem] * len(outs),
        compiler_params=pltpu.CompilerParams(vmem_limit_bytes=10 * 2**20),
        cost_estimate=cost,
        name="shrink",
    )(places, *[rows[k] for k in blocks], *[factors[d] for d in distances], *add)


def expand_kernel(planes, up_run, *refs):
    got = refs[:PLANE]
    key_ref, value_ref, factor = refs[PLANE:]
    column = lax.rem(lax.axis_index("wide"), PLANE)
    ranks = factor.shape[4]
    total = jnp.zeros((BLK, ranks), jnp.float32)
    for k in range(PLANE):
        total += got[k][pl.ds(0, BLK)].astype(jnp.float32)
        rows = got[k][pl.ds(BLK, 2 * planes * up_run)]
        factor[:, :, column ^ k] = rows.reshape(planes, 2, up_run, ranks)
    low_rank = total.astype(jnp.bfloat16)
    is_key = lax.broadcasted_iota(jnp.int32, low_rank.shape, 1) < ranks // 2
    zero = jnp.zeros_like(low_rank)
    both = jnp.concatenate(
        [jnp.where(is_key, low_rank, zero), jnp.where(is_key, zero, low_rank)], axis=0
    )
    for half in range(2):
        for p in range(planes):
            delta = lax.dot_general(
                both,
                factor[p, half].reshape(PLANE * up_run, ranks),
                (((1,), (1,)), ((), ())),
                preferred_element_type=jnp.float32,
            ).astype(jnp.bfloat16)
            columns = pl.ds((half * planes + p) * PLANE * up_run, PLANE * up_run)
            key_ref[:, columns] = delta[:BLK]
            value_ref[:, columns] = delta[BLK:]


def expand(planes, up_run, got):
    ranks = got[0].shape[1]
    columns = 2 * planes * PLANE * up_run
    vmem = pl.BlockSpec(memory_space=pltpu.VMEM)
    return pl.pallas_call(
        lambda *refs: expand_kernel(planes, up_run, *refs),
        out_shape=[jax.ShapeDtypeStruct((BLK, columns), jnp.bfloat16)] * 2,
        in_specs=[vmem] * PLANE,
        out_specs=[vmem] * 2,
        scratch_shapes=[pltpu.VMEM((planes, 2, PLANE, up_run, ranks), jnp.bfloat16)],
        compiler_params=pltpu.CompilerParams(vmem_limit_bytes=4 * 2**20),
        name="expand",
    )(*got)


def plane_body(
    tokens,
    adapter_down_weight,
    adapter_up_weight,
    adapter_entry,
    adapter_of_request,
    token_blocks_per_request,
):
    planes = lax.axis_size("wide") // PLANE
    places, many, *sends = prepare(
        planes,
        tokens,
        adapter_down_weight,
        adapter_up_weight,
        adapter_entry,
        adapter_of_request,
        token_blocks_per_request,
    )
    factors, rows = sends[:planes], sends[planes:]
    up_run = adapter_up_weight.shape[2]
    factors = [factors[0]] + [swap(factors[d], d * PLANE) for d in range(1, planes)]
    rows = [rows[0]] + [swap(rows[k], k) for k in range(1, PLANE)]
    whole = tuple(range(planes))
    (own,) = shrink(
        planes, SLOTS, (0, 1), (0,), places, rows, factors, up_run, last=False, flops=3*10**10
    )
    first = shrink(planes, USUAL, (0, 1), whole, places, rows, factors, up_run, held=own, flops=3*10**10)

    def finish(sums):
        got = [sums[0]] + [swap(sums[k], k) for k in range(1, PLANE)]
        return tuple(expand(planes, up_run, got))

    def usual(places, factors, rows, first):
        return finish([*first, *shrink(planes, USUAL, (2, 3), whole, places, rows, factors, up_run)])

    def more(places, factors, rows, first):
        third = [swap(factors[d ^ 1][:1], PLANE) for d in range(2, planes)]
        factors = factors[:2] + [jnp.concatenate([factors[d], third[d - 2]]) for d in range(2, planes)]
        return finish(shrink(planes, SLOTS, tuple(range(PLANE)), whole, places, rows, factors, up_run))

    return lax.switch(many[0], [usual, more], places, factors, rows, first)


def solution(mesh):
    by_plane = mesh.shape["wide"] == 16 and mesh.shape["narrow"] == 1
    return jax.shard_map(
        plane_body if by_plane else direct_body,
        mesh=mesh,
        in_specs=(
            P(("groups", "wide"), "narrow"),
            P(None, "narrow", "wide", None),
            P(None, "narrow", "wide", None),
            P(),
            P("groups"),
            P("groups"),
        ),
        out_specs=(P(("groups", "wide"), "narrow"), P(("groups", "wide"), "narrow")),
        check_vma=False,
    )
```

```python
import jax
import jax.numpy as jnp
from jax import lax
from jax.experimental import pallas as pl
from jax.experimental.pallas import tpu as pltpu
from jax.sharding import PartitionSpec as P

BLK = 128
PLANE = 4
SLOTS = 3
USUAL = 2


def block_tables(
    adapter_entry,
    adapter_of_request,
    token_blocks_per_request,
    block_count,
    request_count,
    adapter_count,
):
    request_ends = jnp.cumsum(token_blocks_per_request)
    block_index = jnp.arange(block_count, dtype=jnp.int32)
    request = jnp.sum((request_ends[None, :] <= block_index[:, None]).astype(jnp.int32), axis=1)
    pick_table = (request[:, None] == jnp.arange(request_count, dtype=jnp.int32)[None, :]).astype(
        jnp.int32
    )
    adapter = jnp.sum(pick_table * adapter_of_request[None, :], axis=1)
    slot_table = (adapter[:, None] == jnp.arange(adapter_count, dtype=jnp.int32)[None, :]).astype(
        jnp.int32
    )
    return jnp.sum(slot_table * adapter_entry[None, :], axis=1)


def direct_body(
    tokens,
    adapter_down_weight,
    adapter_up_weight,
    adapter_entry,
    adapter_of_request,
    token_blocks_per_request,
):
    wide_count = lax.axis_size("wide")
    blocks_dev = tokens.shape[0] // BLK
    local_width = tokens.shape[1]
    paired_ranks = adapter_down_weight.shape[3]
    rank_count = paired_ranks // 2
    slot_ids = block_tables(
        adapter_entry,
        adapter_of_request,
        token_blocks_per_request,
        blocks_dev * wide_count,
        token_blocks_per_request.shape[0],
        adapter_entry.shape[0],
    )
    needed_adapters = slot_ids.reshape(wide_count, blocks_dev).T
    down_outgoing = adapter_down_weight[needed_adapters]
    up_outgoing = adapter_up_weight[needed_adapters]
    got_down, got_up = (
        lax.all_to_all(down_outgoing, "wide", split_axis=1, concat_axis=3, tiled=True),
        lax.all_to_all(up_outgoing, "wide", split_axis=1, concat_axis=3, tiled=True),
    )
    got_down = got_down.reshape(blocks_dev, local_width, paired_ranks)
    block_rows = tokens.reshape(blocks_dev, BLK, local_width)
    shrink = jnp.einsum("btd,bdr->btr", block_rows, got_down, preferred_element_type=jnp.float32)
    low_rank = lax.psum(shrink, "narrow").astype(jnp.bfloat16)
    got_up = got_up.reshape(blocks_dev, -1, paired_ranks)
    delta_key = jnp.einsum(
        "btr,bjr->btj",
        low_rank[..., :rank_count],
        got_up[..., :rank_count],
        preferred_element_type=jnp.float32,
    )
    delta_value = jnp.einsum(
        "btr,bjr->btj",
        low_rank[..., rank_count:],
        got_up[..., rank_count:],
        preferred_element_type=jnp.float32,
    )
    out_cols = got_up.shape[1]
    key_delta = delta_key.reshape(blocks_dev * BLK, out_cols).astype(jnp.bfloat16)
    value_delta = delta_value.reshape(blocks_dev * BLK, out_cols).astype(jnp.bfloat16)
    return (key_delta, value_delta)


def swap(value, step):
    count = lax.axis_size("wide")
    return lax.ppermute(value, "wide", [(i, i ^ step) for i in range(count)])


def swap_cores(value):
    count = lax.axis_size("wide")
    pairs = [[i, i + 1] for i in range(0, count, 2)]
    return lax.all_to_all(value, "wide", 0, 0, axis_index_groups=pairs, tiled=True)


def pick(index, values):
    got = values[0]
    for i in range(1, len(values)):
        got = jnp.where(index == i, values[i], got)
    return got


def slices(tokens_ref, column, run, out, sem):
    return [
        pltpu.make_async_copy(
            tokens_ref.at[:, pl.ds(pl.multiple_of((piece * PLANE + column) * run, run), run)],
            out.at[piece],
            sem.at[piece],
        )
        for piece in range(out.shape[0])
    ]


def choose_kernel(
    planes, entry_hbm, adapter_hbm, counts_hbm, tokens_ref, down_ref, up_ref, table_ref, *refs
):
    others = planes - 2
    sends, tokens_out = refs[:others], refs[others : others + PLANE - 2]
    entry_ref, adapter_ref, counts_ref, small_sem, tokens_sem, sem = refs[others + PLANE - 2 :]
    me = lax.axis_index("wide")
    column, plane = lax.rem(me, PLANE), lax.div(me, PLANE)
    run, up_run = down_ref.shape[2], up_ref.shape[2]
    small = [
        pltpu.make_async_copy(entry_hbm, entry_ref, small_sem.at[0]),
        pltpu.make_async_copy(adapter_hbm, adapter_ref, small_sem.at[1]),
        pltpu.make_async_copy(counts_hbm, counts_ref, small_sem.at[2]),
    ]
    for copy in small:
        copy.start()
    copies = []
    for k, out in enumerate(tokens_out):
        copies += slices(tokens_ref, column ^ (k + 2), run, out, tokens_sem.at[k])
    for copy in copies:
        copy.start()
    for copy in small:
        copy.wait()

    requests = counts_ref.shape[0]
    ends, total = [], 0
    for q in range(requests):
        total = total + counts_ref[q]
        ends.append(total)
    entries = [entry_ref[adapter_ref[q]] for q in range(requests)]

    def listed(p):
        ids = []
        for i in range(PLANE):
            block = p * PLANE + jnp.where(p % 2 == 0, i, PLANE - 1 - i)
            got = entries[0]
            for q in range(1, requests):
                got = jnp.where(ends[q - 1] <= block, entries[q], got)
            ids.append(got)
        place, held, count = [jnp.int32(0)], [ids[0]] * SLOTS, jnp.int32(1)
        for i in range(1, PLANE):
            found = count
            for j in range(i):
                found = jnp.where(ids[i] == ids[j], place[j], found)
            place.append(found)
            held = [jnp.where(found == s, ids[i], held[s]) for s in range(SLOTS)]
            count = jnp.maximum(count, found + 1)
        return held, place, count

    most = jnp.int32(1)
    for d in reversed(range(planes)):
        held, place, count = listed(plane ^ d)
        most = jnp.maximum(most, count)
        if d > 1:
            for s in range(USUAL):
                out = sends[d - 2].at[s]
                for part, (ref, at) in enumerate(
                    ((down_ref, pl.ds(0, run)), (up_ref, pl.ds(run, up_run)))
                ):
                    copies.append(
                        pltpu.make_async_copy(ref.at[held[s]], out.at[:, at], sem.at[d - 2, s, part])
                    )
                    copies[-1].start()
        else:
            for s in range(SLOTS):
                table_ref[PLANE + d * SLOTS + s] = held[s]
    for k in range(PLANE):
        i = column ^ k
        table_ref[k] = pick(jnp.where(plane % 2 == 0, i, PLANE - 1 - i), place)
    table_ref[PLANE + 2 * SLOTS] = jnp.where(most > USUAL, 1, 0)
    for copy in copies:
        copy.wait()


def choose(planes, tokens, down, up, entry, adapter, counts):
    hbm = pl.BlockSpec(memory_space=pltpu.HBM)
    others = planes - 2
    send = jax.ShapeDtypeStruct((USUAL, 2, down.shape[2] + up.shape[2], down.shape[3]), down.dtype)
    return pl.pallas_call(
        lambda *refs: choose_kernel(planes, *refs),
        out_shape=[jax.ShapeDtypeStruct((PLANE + 2 * SLOTS + 1,), jnp.int32)]
        + [send] * others
        + [jax.ShapeDtypeStruct((2 * planes, BLK, down.shape[2]), tokens.dtype)] * (PLANE - 2),
        in_specs=[hbm] * 6,
        out_specs=[pl.BlockSpec(memory_space=pltpu.SMEM)]
        + [pl.BlockSpec(memory_space=pltpu.VMEM)] * (others + PLANE - 2),
        scratch_shapes=[
            pltpu.SMEM(entry.shape, jnp.int32),
            pltpu.SMEM(adapter.shape, jnp.int32),
            pltpu.SMEM(counts.shape, jnp.int32),
            pltpu.SemaphoreType.DMA((3,)),
            pltpu.SemaphoreType.DMA((PLANE - 2, 2 * planes)),
            pltpu.SemaphoreType.DMA((others, USUAL, 2)),
        ],
        compiler_params=pltpu.CompilerParams(vmem_limit_bytes=57 * 2**20),
        name="choose",
    )(entry, adapter, counts, tokens, down, up)


def gather_kernel(planes, table_ref, tokens_ref, down_ref, up_ref, own_ref, near_ref, pair_ref, tokens_sem, sem):
    column = lax.rem(lax.axis_index("wide"), PLANE)
    run, up_run = down_ref.shape[2], up_ref.shape[2]
    copies = []
    for core in range(2):
        at = lax.div(column, 2) * 2 + core
        copies += slices(tokens_ref, at, run, pair_ref.at[core], tokens_sem.at[core])
    for d, out in enumerate((own_ref, near_ref)):
        for s in range(out.shape[0]):
            slot = table_ref[PLANE + d * SLOTS + s]
            copies.append(
                pltpu.make_async_copy(
                    down_ref.at[slot], out.at[s, :, pl.ds(0, run)], sem.at[d, s, 0]
                )
            )
            copies.append(
                pltpu.make_async_copy(
                    up_ref.at[slot], out.at[s, :, pl.ds(run, up_run)], sem.at[d, s, 1]
                )
            )
    for copy in copies:
        copy.start()
    for copy in copies:
        copy.wait()


def gather(planes, table, tokens, down, up):
    run = down.shape[2]
    hbm = pl.BlockSpec(memory_space=pltpu.HBM)
    rows = (2, run + up.shape[2], down.shape[3])
    return pl.pallas_call(
        lambda *refs: gather_kernel(planes, *refs),
        out_shape=[
            jax.ShapeDtypeStruct((SLOTS,) + rows, down.dtype),
            jax.ShapeDtypeStruct((USUAL,) + rows, down.dtype),
        ]
        + [jax.ShapeDtypeStruct((2, 2 * planes, BLK, run), tokens.dtype)],
        in_specs=[pl.BlockSpec(memory_space=pltpu.SMEM)] + [hbm] * 3,
        out_specs=[pl.BlockSpec(memory_space=pltpu.VMEM)] * 3,
        scratch_shapes=[
            pltpu.SemaphoreType.DMA((2, 2 * planes)),
            pltpu.SemaphoreType.DMA((2, SLOTS, 2)),
        ],
        compiler_params=pltpu.CompilerParams(vmem_limit_bytes=57 * 2**20),
        cost_estimate=pl.CostEstimate(flops=10**10, bytes_accessed=0, transcendentals=0),
        name="gather",
    )(table, tokens, down, up)


def up_rows(factors, distances, place):
    rows = []
    for d in distances:
        slot = jnp.minimum(place, factors[d].shape[0] - 1)
        rows += [factors[d][slot, half] for half in range(2)]
    return rows


def shrink(planes, slots, run, blocks, near, far, places, rows, factors, held=(), ups=None, flops=None, kept=(), flag=False):
    vmem = pl.BlockSpec(memory_space=pltpu.VMEM)
    up_run, ranks = factors[0].shape[2] - run, factors[0].shape[3]

    def kernel(places_ref, *refs):
        row_refs, refs = refs[: len(rows)], refs[len(rows) :]
        factor_refs, refs = refs[: len(factors)], refs[len(factors) :]
        held_refs, outs = list(refs[: len(held)]), refs[len(held) + len(kept) :]
        me = lax.axis_index("wide")
        core, plane = lax.rem(me, 2), lax.div(me, PLANE)
        at = [places_ref[k] for k in blocks]
        views = [ref.at[:, :, pl.ds(run, up_run)] for ref in factor_refs]

        def rows_at(k, piece):
            return row_refs[0][core ^ k, piece] if k < 2 else row_refs[k - 1][piece]

        def sums_of(chosen, distances):
            total = jnp.zeros((len(chosen) * BLK, slots * ranks), jnp.float32)
            for d in distances:
                for half in range(2):
                    piece = half * planes + (plane ^ d)
                    total += jnp.dot(
                        jnp.concatenate([rows_at(blocks[i], piece) for i in chosen], axis=0),
                        jnp.concatenate(
                            [factor_refs[d][s, half, pl.ds(0, run)] for s in range(slots)], axis=1
                        ),
                        preferred_element_type=jnp.float32,
                    )
            parts = [total[j * BLK : (j + 1) * BLK] for j in range(len(chosen))]
            return {
                i: pick(at[i], [part[:, s * ranks : (s + 1) * ranks] for s in range(slots)])
                for i, part in zip(chosen, parts)
            }

        if flag:
            *outs, flag_ref = outs
            flag_ref[0] = places_ref[PLANE + 2 * SLOTS]
        every = range(len(blocks))
        mine = sums_of(every, far) if far else {}
        here = [i for i in every if blocks[i] in near]
        for i, part in (sums_of(here, (0,)) if here else {}).items():
            mine[i] = mine[i] + part if far else part
        for i in every:
            if i not in here:
                mine[i] = mine[i] + held_refs.pop(0)[...]
            outs[i][pl.ds(0, BLK)] = mine[i].astype(outs[i].dtype)
            for j, part in enumerate(up_rows(views, ups or (), at[i])):
                outs[i][pl.ds(BLK + j * up_run, up_run)] = part.astype(outs[i].dtype)

    height = BLK + len(ups or ()) * 2 * up_run
    exact = [ups is None or k == 0 for k in blocks]
    cost = None
    if flops is not None:
        cost = pl.CostEstimate(flops=flops, bytes_accessed=0, transcendentals=0)
    return pl.pallas_call(
        kernel,
        out_shape=[
            jax.ShapeDtypeStruct((height, ranks), jnp.float32 if full else rows[0].dtype)
            for full in exact
        ]
        + [jax.ShapeDtypeStruct((1,), jnp.int32)] * flag,
        in_specs=[pl.BlockSpec(memory_space=pltpu.SMEM)]
        + [vmem] * (len(rows) + len(factors) + len(held))
        + [pl.BlockSpec(memory_space=pl.ANY)] * len(kept),
        out_specs=[vmem] * len(blocks) + [pl.BlockSpec(memory_space=pltpu.SMEM)] * flag,
        compiler_params=pltpu.CompilerParams(vmem_limit_bytes=10 * 2**20),
        cost_estimate=cost,
        name="shrink",
    )(places, *rows, *factors, *held, *kept)


def expand(planes, up_run, sums):
    ranks = sums[0].shape[1]
    columns = 2 * planes * PLANE * up_run
    vmem = pl.BlockSpec(memory_space=pltpu.VMEM)
    span = 2 * up_run

    def kernel(*refs):
        sum_refs = refs[:PLANE]
        key_ref, value_ref, factor = refs[PLANE:]
        me = lax.axis_index("wide")
        column, plane = lax.rem(me, PLANE), lax.div(me, PLANE)
        total = jnp.zeros((BLK, ranks), jnp.float32)
        for k in range(PLANE):
            total += sum_refs[k][pl.ds(0, BLK)].astype(jnp.float32)
            for d in range(planes):
                rows = sum_refs[k][pl.ds(BLK + d * span, span)]
                factor[plane ^ d, :, column ^ k] = rows.astype(factor.dtype).reshape(2, up_run, ranks)
        low_rank = total.astype(jnp.bfloat16)
        is_key = lax.broadcasted_iota(jnp.int32, low_rank.shape, 1) < ranks // 2
        zero = jnp.zeros_like(low_rank)
        both = jnp.concatenate(
            [jnp.where(is_key, low_rank, zero), jnp.where(is_key, zero, low_rank)], axis=0
        )
        for half in range(2):
            for p in range(planes):
                delta = lax.dot_general(
                    both,
                    factor[p, half].reshape(PLANE * up_run, ranks),
                    (((1,), (1,)), ((), ())),
                    preferred_element_type=jnp.float32,
                ).astype(jnp.bfloat16)
                at = pl.ds((half * planes + p) * PLANE * up_run, PLANE * up_run)
                key_ref[:, at] = delta[:BLK]
                value_ref[:, at] = delta[BLK:]

    return pl.pallas_call(
        kernel,
        out_shape=[jax.ShapeDtypeStruct((BLK, columns), jnp.bfloat16)] * 2,
        in_specs=[vmem] * PLANE,
        out_specs=[vmem] * 2,
        scratch_shapes=[pltpu.VMEM((planes, 2, PLANE, up_run, ranks), jnp.bfloat16)],
        compiler_params=pltpu.CompilerParams(vmem_limit_bytes=4 * 2**20),
        name="expand",
    )(*sums)


def plane_body(
    tokens,
    adapter_down_weight,
    adapter_up_weight,
    adapter_entry,
    adapter_of_request,
    token_blocks_per_request,
):
    planes = lax.axis_size("wide") // PLANE
    places, *sends = choose(
        planes,
        tokens,
        adapter_down_weight,
        adapter_up_weight,
        adapter_entry,
        adapter_of_request,
        token_blocks_per_request,
    )
    far, across = sends[: planes - 2], sends[planes - 2 :]
    own_factors, near, pair = gather(planes, places, tokens, adapter_down_weight, adapter_up_weight)
    sends = sends + [near, pair]
    run, up_run = adapter_down_weight.shape[2], adapter_up_weight.shape[2]
    whole, blocks = tuple(range(planes)), tuple(range(PLANE))
    far = [swap(far[d - 2], d * PLANE) for d in range(2, planes)]
    factors = [own_factors, swap(near, PLANE)] + far
    rows = [swap_cores(pair)] + [swap(across[k - 2], k) for k in range(2, PLANE)]
    *held, many = shrink(
        planes, SLOTS, run, (0, 1), (0, 1), (), places, rows[:1], factors[:1], flops=None, flag=True
    )

    def finish(sums):
        sums = [sums[0]] + [swap(sums[k], k) for k in range(1, PLANE)]
        return tuple(expand(planes, up_run, sums))

    def usual(places, factors, rows, held, kept):
        sums = shrink(
            planes, USUAL, run, blocks, (2, 3), whole[1:], places, rows, factors, held, whole
        )
        return finish(sums)

    def more(places, factors, rows, held, kept):
        third = swap(jnp.concatenate([factors[d ^ 1][:1] for d in whole[1:]]), PLANE)
        factors = [factors[0]] + [
            jnp.concatenate([factors[d], third[d - 1 : d]]) for d in whole[1:]
        ]
        sums = shrink(
            planes, SLOTS, run, blocks, (2, 3), whole[1:], places, rows, factors, held, whole, kept=kept
        )
        return finish(sums)

    return lax.switch(many[0], [usual, more], places, factors, rows, held, sends)


def solution(mesh):
    by_plane = mesh.shape["wide"] == 16 and mesh.shape["narrow"] == 1
    return jax.shard_map(
        plane_body if by_plane else direct_body,
        mesh=mesh,
        in_specs=(
            P(("groups", "wide"), "narrow"),
            P(None, "narrow", "wide", None),
            P(None, "narrow", "wide", None),
            P(),
            P("groups"),
            P("groups"),
        ),
        out_specs=(P(("groups", "wide"), "narrow"), P(("groups", "wide"), "narrow")),
        check_vma=False,
    )
```

```python
import jax
import jax.numpy as jnp
from jax import lax
from jax.experimental import pallas as pl
from jax.experimental.pallas import tpu as pltpu
from jax.sharding import PartitionSpec as P

BLK = 128
PLANE = 4
SLOTS = 3
USUAL = 2


def block_tables(
    adapter_entry,
    adapter_of_request,
    token_blocks_per_request,
    block_count,
    request_count,
    adapter_count,
):
    request_ends = jnp.cumsum(token_blocks_per_request)
    block_index = jnp.arange(block_count, dtype=jnp.int32)
    request = jnp.sum((request_ends[None, :] <= block_index[:, None]).astype(jnp.int32), axis=1)
    pick_table = (request[:, None] == jnp.arange(request_count, dtype=jnp.int32)[None, :]).astype(
        jnp.int32
    )
    adapter = jnp.sum(pick_table * adapter_of_request[None, :], axis=1)
    slot_table = (adapter[:, None] == jnp.arange(adapter_count, dtype=jnp.int32)[None, :]).astype(
        jnp.int32
    )
    return jnp.sum(slot_table * adapter_entry[None, :], axis=1)


def direct_body(
    tokens,
    adapter_down_weight,
    adapter_up_weight,
    adapter_entry,
    adapter_of_request,
    token_blocks_per_request,
):
    wide_count = lax.axis_size("wide")
    blocks_dev = tokens.shape[0] // BLK
    local_width = tokens.shape[1]
    paired_ranks = adapter_down_weight.shape[3]
    rank_count = paired_ranks // 2
    slot_ids = block_tables(
        adapter_entry,
        adapter_of_request,
        token_blocks_per_request,
        blocks_dev * wide_count,
        token_blocks_per_request.shape[0],
        adapter_entry.shape[0],
    )
    needed_adapters = slot_ids.reshape(wide_count, blocks_dev).T
    down_outgoing = adapter_down_weight[needed_adapters]
    up_outgoing = adapter_up_weight[needed_adapters]
    got_down, got_up = (
        lax.all_to_all(down_outgoing, "wide", split_axis=1, concat_axis=3, tiled=True),
        lax.all_to_all(up_outgoing, "wide", split_axis=1, concat_axis=3, tiled=True),
    )
    got_down = got_down.reshape(blocks_dev, local_width, paired_ranks)
    block_rows = tokens.reshape(blocks_dev, BLK, local_width)
    shrink = jnp.einsum("btd,bdr->btr", block_rows, got_down, preferred_element_type=jnp.float32)
    low_rank = lax.psum(shrink, "narrow").astype(jnp.bfloat16)
    got_up = got_up.reshape(blocks_dev, -1, paired_ranks)
    delta_key = jnp.einsum(
        "btr,bjr->btj",
        low_rank[..., :rank_count],
        got_up[..., :rank_count],
        preferred_element_type=jnp.float32,
    )
    delta_value = jnp.einsum(
        "btr,bjr->btj",
        low_rank[..., rank_count:],
        got_up[..., rank_count:],
        preferred_element_type=jnp.float32,
    )
    out_cols = got_up.shape[1]
    key_delta = delta_key.reshape(blocks_dev * BLK, out_cols).astype(jnp.bfloat16)
    value_delta = delta_value.reshape(blocks_dev * BLK, out_cols).astype(jnp.bfloat16)
    return (key_delta, value_delta)


def swap(value, step):
    count = lax.axis_size("wide")
    return lax.ppermute(value, "wide", [(i, i ^ step) for i in range(count)])


def swap_cores(value):
    count = lax.axis_size("wide")
    pairs = [[i, i + 1] for i in range(0, count, 2)]
    return lax.all_to_all(value, "wide", 0, 0, axis_index_groups=pairs, tiled=True)


def pick(index, values):
    got = values[0]
    for i in range(1, len(values)):
        got = jnp.where(index == i, values[i], got)
    return got


def slices(tokens_ref, column, run, out, sem):
    return [
        pltpu.make_async_copy(
            tokens_ref.at[:, pl.ds(pl.multiple_of((piece * PLANE + column) * run, run), run)],
            out.at[piece],
            sem.at[piece],
        )
        for piece in range(out.shape[0])
    ]


def choose_kernel(
    planes, entry_hbm, adapter_hbm, counts_hbm, tokens_ref, down_ref, up_ref, table_ref, *refs
):
    others = planes - 1
    sends, tokens_out = refs[:others], refs[others : others + PLANE - 2]
    entry_ref, adapter_ref, counts_ref, small_sem, tokens_sem, sem = refs[others + PLANE - 2 :]
    me = lax.axis_index("wide")
    column, plane = lax.rem(me, PLANE), lax.div(me, PLANE)
    run, up_run = down_ref.shape[2], up_ref.shape[2]
    small = [
        pltpu.make_async_copy(entry_hbm, entry_ref, small_sem.at[0]),
        pltpu.make_async_copy(adapter_hbm, adapter_ref, small_sem.at[1]),
        pltpu.make_async_copy(counts_hbm, counts_ref, small_sem.at[2]),
    ]
    for copy in small:
        copy.start()
    copies = []
    for k, out in enumerate(tokens_out):
        copies += slices(tokens_ref, column ^ (k + 2), run, out, tokens_sem.at[k])
    for copy in copies:
        copy.start()
    for copy in small:
        copy.wait()

    requests = counts_ref.shape[0]
    ends, total = [], 0
    for q in range(requests):
        total = total + counts_ref[q]
        ends.append(total)
    entries = [entry_ref[adapter_ref[q]] for q in range(requests)]

    def listed(p):
        ids = []
        for i in range(PLANE):
            block = p * PLANE + jnp.where(p % 2 == 0, i, PLANE - 1 - i)
            got = entries[0]
            for q in range(1, requests):
                got = jnp.where(ends[q - 1] <= block, entries[q], got)
            ids.append(got)
        place, held, count = [jnp.int32(0)], [ids[0]] * SLOTS, jnp.int32(1)
        for i in range(1, PLANE):
            found = count
            for j in range(i):
                found = jnp.where(ids[i] == ids[j], place[j], found)
            place.append(found)
            held = [jnp.where(found == s, ids[i], held[s]) for s in range(SLOTS)]
            count = jnp.maximum(count, found + 1)
        return held, place, count

    most = jnp.int32(1)
    for d in reversed(range(planes)):
        held, place, count = listed(plane ^ d)
        most = jnp.maximum(most, count)
        if d > 0:
            for s in range(sends[d - 1].shape[0]):
                out = sends[d - 1].at[s]
                for part, (ref, at) in enumerate(
                    ((down_ref, pl.ds(0, run)), (up_ref, pl.ds(run, up_run)))
                ):
                    copies.append(
                        pltpu.make_async_copy(ref.at[held[s]], out.at[:, at], sem.at[d - 1, s, part])
                    )
                    copies[-1].start()
        else:
            for s in range(SLOTS):
                table_ref[PLANE + s] = held[s]
    for k in range(PLANE):
        i = column ^ k
        table_ref[k] = pick(jnp.where(plane % 2 == 0, i, PLANE - 1 - i), place)
    table_ref[PLANE + SLOTS] = jnp.where(most > USUAL, 1, 0)
    for copy in copies:
        copy.wait()


def choose(planes, tokens, down, up, entry, adapter, counts):
    hbm = pl.BlockSpec(memory_space=pltpu.HBM)
    others = planes - 1
    rows = (2, down.shape[2] + up.shape[2], down.shape[3])
    sends = [
        jax.ShapeDtypeStruct((SLOTS if d == 1 else USUAL,) + rows, down.dtype) for d in range(1, planes)
    ]
    return pl.pallas_call(
        lambda *refs: choose_kernel(planes, *refs),
        out_shape=[jax.ShapeDtypeStruct((PLANE + SLOTS + 1,), jnp.int32)]
        + sends
        + [jax.ShapeDtypeStruct((2 * planes, BLK, down.shape[2]), tokens.dtype)] * (PLANE - 2),
        in_specs=[hbm] * 6,
        out_specs=[pl.BlockSpec(memory_space=pltpu.SMEM)]
        + [pl.BlockSpec(memory_space=pltpu.VMEM)] * (others + PLANE - 2),
        scratch_shapes=[
            pltpu.SMEM(entry.shape, jnp.int32),
            pltpu.SMEM(adapter.shape, jnp.int32),
            pltpu.SMEM(counts.shape, jnp.int32),
            pltpu.SemaphoreType.DMA((3,)),
            pltpu.SemaphoreType.DMA((PLANE - 2, 2 * planes)),
            pltpu.SemaphoreType.DMA((others, SLOTS, 2)),
        ],
        compiler_params=pltpu.CompilerParams(vmem_limit_bytes=57 * 2**20),
        name="choose",
    )(entry, adapter, counts, tokens, down, up)


def gather_kernel(planes, table_ref, tokens_ref, down_ref, up_ref, own_ref, pair_ref, tokens_sem, sem):
    column = lax.rem(lax.axis_index("wide"), PLANE)
    run, up_run = down_ref.shape[2], up_ref.shape[2]
    copies = []
    for core in range(2):
        at = lax.div(column, 2) * 2 + core
        copies += slices(tokens_ref, at, run, pair_ref.at[core], tokens_sem.at[core])
    for s in range(SLOTS):
        slot = table_ref[PLANE + s]
        out = own_ref.at[s]
        for part, (ref, rows) in enumerate(
            ((down_ref, pl.ds(0, run)), (up_ref, pl.ds(run, up_run)))
        ):
            copies.append(pltpu.make_async_copy(ref.at[slot], out.at[:, rows], sem.at[s, part]))
    for copy in copies:
        copy.start()
    for copy in copies:
        copy.wait()


def gather(planes, table, tokens, down, up):
    run = down.shape[2]
    hbm = pl.BlockSpec(memory_space=pltpu.HBM)
    rows = (2, run + up.shape[2], down.shape[3])
    return pl.pallas_call(
        lambda *refs: gather_kernel(planes, *refs),
        out_shape=[
            jax.ShapeDtypeStruct((SLOTS,) + rows, down.dtype),
        ]
        + [jax.ShapeDtypeStruct((2, 2 * planes, BLK, run), tokens.dtype)],
        in_specs=[pl.BlockSpec(memory_space=pltpu.SMEM)] + [hbm] * 3,
        out_specs=[pl.BlockSpec(memory_space=pltpu.VMEM)] * 2,
        scratch_shapes=[
            pltpu.SemaphoreType.DMA((2, 2 * planes)),
            pltpu.SemaphoreType.DMA((SLOTS, 2)),
        ],
        compiler_params=pltpu.CompilerParams(vmem_limit_bytes=57 * 2**20),
        cost_estimate=pl.CostEstimate(flops=10**10, bytes_accessed=0, transcendentals=0),
        name="gather",
    )(table, tokens, down, up)


def up_rows(factors, distances, place):
    rows = []
    for d in distances:
        slot = jnp.minimum(place, factors[d].shape[0] - 1)
        rows += [factors[d][slot, half] for half in range(2)]
    return rows


def shrink(planes, slots, run, blocks, near, far, places, rows, factors, held=(), ups=None, flops=None, kept=(), flag=False):
    vmem = pl.BlockSpec(memory_space=pltpu.VMEM)
    up_run, ranks = factors[0].shape[2] - run, factors[0].shape[3]

    def kernel(places_ref, *refs):
        row_refs, refs = refs[: len(rows)], refs[len(rows) :]
        factor_refs, refs = refs[: len(factors)], refs[len(factors) :]
        held_refs, outs = list(refs[: len(held)]), refs[len(held) + len(kept) :]
        me = lax.axis_index("wide")
        core, plane = lax.rem(me, 2), lax.div(me, PLANE)
        at = [places_ref[k] for k in blocks]
        views = [ref.at[:, :, pl.ds(run, up_run)] for ref in factor_refs]

        def rows_at(k, piece):
            return row_refs[0][core ^ k, piece] if k < 2 else row_refs[k - 1][piece]

        def sums_of(chosen, distances):
            total = jnp.zeros((len(chosen) * BLK, slots * ranks), jnp.float32)
            for d in distances:
                for half in range(2):
                    piece = half * planes + (plane ^ d)
                    total += jnp.dot(
                        jnp.concatenate([rows_at(blocks[i], piece) for i in chosen], axis=0),
                        jnp.concatenate(
                            [factor_refs[d][s, half, pl.ds(0, run)] for s in range(slots)], axis=1
                        ),
                        preferred_element_type=jnp.float32,
                    )
            parts = [total[j * BLK : (j + 1) * BLK] for j in range(len(chosen))]
            return {
                i: pick(at[i], [part[:, s * ranks : (s + 1) * ranks] for s in range(slots)])
                for i, part in zip(chosen, parts)
            }

        if flag:
            *outs, flag_ref = outs
            flag_ref[0] = places_ref[PLANE + SLOTS]
        every = range(len(blocks))
        mine = sums_of(every, far) if far else {}
        here = [i for i in every if blocks[i] in near]
        for i, part in (sums_of(here, (0,)) if here else {}).items():
            mine[i] = mine[i] + part if far else part
        for i in every:
            if i not in here:
                mine[i] = mine[i] + held_refs.pop(0)[...]
            outs[i][pl.ds(0, BLK)] = mine[i].astype(outs[i].dtype)
            for j, part in enumerate(up_rows(views, ups or (), at[i])):
                outs[i][pl.ds(BLK + j * up_run, up_run)] = part.astype(outs[i].dtype)

    height = BLK + len(ups or ()) * 2 * up_run
    exact = [ups is None or k == 0 for k in blocks]
    cost = None
    if flops is not None:
        cost = pl.CostEstimate(flops=flops, bytes_accessed=0, transcendentals=0)
    return pl.pallas_call(
        kernel,
        out_shape=[
            jax.ShapeDtypeStruct((height, ranks), jnp.float32 if full else rows[0].dtype)
            for full in exact
        ]
        + [jax.ShapeDtypeStruct((1,), jnp.int32)] * flag,
        in_specs=[pl.BlockSpec(memory_space=pltpu.SMEM)]
        + [vmem] * (len(rows) + len(factors) + len(held))
        + [pl.BlockSpec(memory_space=pl.ANY)] * len(kept),
        out_specs=[vmem] * len(blocks) + [pl.BlockSpec(memory_space=pltpu.SMEM)] * flag,
        compiler_params=pltpu.CompilerParams(vmem_limit_bytes=10 * 2**20),
        cost_estimate=cost,
        name="shrink",
    )(places, *rows, *factors, *held, *kept)


def expand(planes, up_run, sums):
    ranks = sums[0].shape[1]
    columns = 2 * planes * PLANE * up_run
    vmem = pl.BlockSpec(memory_space=pltpu.VMEM)
    span = 2 * up_run

    def kernel(*refs):
        sum_refs = refs[:PLANE]
        key_ref, value_ref, factor = refs[PLANE:]
        me = lax.axis_index("wide")
        column, plane = lax.rem(me, PLANE), lax.div(me, PLANE)
        total = jnp.zeros((BLK, ranks), jnp.float32)
        for k in range(PLANE):
            total += sum_refs[k][pl.ds(0, BLK)].astype(jnp.float32)
            for d in range(planes):
                rows = sum_refs[k][pl.ds(BLK + d * span, span)]
                factor[plane ^ d, :, column ^ k] = rows.astype(factor.dtype).reshape(2, up_run, ranks)
        low_rank = total.astype(jnp.bfloat16)
        is_key = lax.broadcasted_iota(jnp.int32, low_rank.shape, 1) < ranks // 2
        zero = jnp.zeros_like(low_rank)
        both = jnp.concatenate(
            [jnp.where(is_key, low_rank, zero), jnp.where(is_key, zero, low_rank)], axis=0
        )
        for half in range(2):
            for p in range(planes):
                delta = lax.dot_general(
                    both,
                    factor[p, half].reshape(PLANE * up_run, ranks),
                    (((1,), (1,)), ((), ())),
                    preferred_element_type=jnp.float32,
                ).astype(jnp.bfloat16)
                at = pl.ds((half * planes + p) * PLANE * up_run, PLANE * up_run)
                key_ref[:, at] = delta[:BLK]
                value_ref[:, at] = delta[BLK:]

    return pl.pallas_call(
        kernel,
        out_shape=[jax.ShapeDtypeStruct((BLK, columns), jnp.bfloat16)] * 2,
        in_specs=[vmem] * PLANE,
        out_specs=[vmem] * 2,
        scratch_shapes=[pltpu.VMEM((planes, 2, PLANE, up_run, ranks), jnp.bfloat16)],
        compiler_params=pltpu.CompilerParams(vmem_limit_bytes=4 * 2**20),
        name="expand",
    )(*sums)


def plane_body(
    tokens,
    adapter_down_weight,
    adapter_up_weight,
    adapter_entry,
    adapter_of_request,
    token_blocks_per_request,
):
    planes = lax.axis_size("wide") // PLANE
    places, *sends = choose(
        planes,
        tokens,
        adapter_down_weight,
        adapter_up_weight,
        adapter_entry,
        adapter_of_request,
        token_blocks_per_request,
    )
    factors, across = sends[: planes - 1], sends[planes - 1 :]
    own_factors, pair = gather(planes, places, tokens, adapter_down_weight, adapter_up_weight)
    sends = sends + [pair]
    run, up_run = adapter_down_weight.shape[2], adapter_up_weight.shape[2]
    whole, blocks = tuple(range(planes)), tuple(range(PLANE))
    factors = [own_factors] + [swap(factors[d - 1], d * PLANE) for d in whole[1:]]
    rows = [swap_cores(pair)] + [swap(across[k - 2], k) for k in range(2, PLANE)]
    *held, many = shrink(
        planes, SLOTS, run, (0, 1), (0, 1), (), places, rows[:1], factors[:1], flops=None, flag=True
    )

    def finish(sums):
        sums = [sums[0]] + [swap(sums[k], k) for k in range(1, PLANE)]
        return tuple(expand(planes, up_run, sums))

    def usual(places, factors, rows, held, kept):
        sums = shrink(
            planes, USUAL, run, blocks, (2, 3), whole[1:], places, rows, factors, held, whole
        )
        return finish(sums)

    def more(places, factors, rows, held, kept):
        third = [swap(factors[d ^ 1][:1], PLANE) for d in whole[2:]]
        factors = factors[:2] + [jnp.concatenate([factors[d], third[d - 2]]) for d in whole[2:]]
        sums = shrink(
            planes, SLOTS, run, blocks, (2, 3), whole[1:], places, rows, factors, held, whole, kept=kept
        )
        return finish(sums)

    return lax.switch(many[0], [usual, more], places, factors, rows, held, sends)


def solution(mesh):
    by_plane = mesh.shape["wide"] == 16 and mesh.shape["narrow"] == 1
    return jax.shard_map(
        plane_body if by_plane else direct_body,
        mesh=mesh,
        in_specs=(
            P(("groups", "wide"), "narrow"),
            P(None, "narrow", "wide", None),
            P(None, "narrow", "wide", None),
            P(),
            P("groups"),
            P("groups"),
        ),
        out_specs=(P(("groups", "wide"), "narrow"), P(("groups", "wide"), "narrow")),
        check_vma=False,
    )
```

```python
import jax
import jax.numpy as jnp
from jax import lax
from jax.experimental import pallas as pl
from jax.experimental.pallas import tpu as pltpu
from jax.sharding import PartitionSpec as P

BLK = 128
PLANE = 4
SLOTS = 3
USUAL = 2


def block_tables(
    adapter_entry,
    adapter_of_request,
    token_blocks_per_request,
    block_count,
    request_count,
    adapter_count,
):
    request_ends = jnp.cumsum(token_blocks_per_request)
    block_index = jnp.arange(block_count, dtype=jnp.int32)
    request = jnp.sum((request_ends[None, :] <= block_index[:, None]).astype(jnp.int32), axis=1)
    pick_table = (request[:, None] == jnp.arange(request_count, dtype=jnp.int32)[None, :]).astype(
        jnp.int32
    )
    adapter = jnp.sum(pick_table * adapter_of_request[None, :], axis=1)
    slot_table = (adapter[:, None] == jnp.arange(adapter_count, dtype=jnp.int32)[None, :]).astype(
        jnp.int32
    )
    return jnp.sum(slot_table * adapter_entry[None, :], axis=1)


def direct_body(
    tokens,
    adapter_down_weight,
    adapter_up_weight,
    adapter_entry,
    adapter_of_request,
    token_blocks_per_request,
):
    wide_count = lax.axis_size("wide")
    blocks_dev = tokens.shape[0] // BLK
    local_width = tokens.shape[1]
    paired_ranks = adapter_down_weight.shape[3]
    rank_count = paired_ranks // 2
    slot_ids = block_tables(
        adapter_entry,
        adapter_of_request,
        token_blocks_per_request,
        blocks_dev * wide_count,
        token_blocks_per_request.shape[0],
        adapter_entry.shape[0],
    )
    needed_adapters = slot_ids.reshape(wide_count, blocks_dev).T
    down_outgoing = adapter_down_weight[needed_adapters]
    up_outgoing = adapter_up_weight[needed_adapters]
    got_down, got_up = (
        lax.all_to_all(down_outgoing, "wide", split_axis=1, concat_axis=3, tiled=True),
        lax.all_to_all(up_outgoing, "wide", split_axis=1, concat_axis=3, tiled=True),
    )
    got_down = got_down.reshape(blocks_dev, local_width, paired_ranks)
    block_rows = tokens.reshape(blocks_dev, BLK, local_width)
    shrink = jnp.einsum("btd,bdr->btr", block_rows, got_down, preferred_element_type=jnp.float32)
    low_rank = lax.psum(shrink, "narrow").astype(jnp.bfloat16)
    got_up = got_up.reshape(blocks_dev, -1, paired_ranks)
    delta_key = jnp.einsum(
        "btr,bjr->btj",
        low_rank[..., :rank_count],
        got_up[..., :rank_count],
        preferred_element_type=jnp.float32,
    )
    delta_value = jnp.einsum(
        "btr,bjr->btj",
        low_rank[..., rank_count:],
        got_up[..., rank_count:],
        preferred_element_type=jnp.float32,
    )
    out_cols = got_up.shape[1]
    key_delta = delta_key.reshape(blocks_dev * BLK, out_cols).astype(jnp.bfloat16)
    value_delta = delta_value.reshape(blocks_dev * BLK, out_cols).astype(jnp.bfloat16)
    return (key_delta, value_delta)


def swap(value, step):
    count = lax.axis_size("wide")
    return lax.ppermute(value, "wide", [(i, i ^ step) for i in range(count)])


def swap_cores(value):
    count = lax.axis_size("wide")
    pairs = [[i, i + 1] for i in range(0, count, 2)]
    return lax.all_to_all(value, "wide", 0, 0, axis_index_groups=pairs, tiled=True)


def pick(index, values):
    got = values[0]
    for i in range(1, len(values)):
        got = jnp.where(index == i, values[i], got)
    return got


def slices(tokens_ref, column, run, out, sem):
    return [
        pltpu.make_async_copy(
            tokens_ref.at[:, pl.ds(pl.multiple_of((piece * PLANE + column) * run, run), run)],
            out.at[piece],
            sem.at[piece],
        )
        for piece in range(out.shape[0])
    ]


def choose_kernel(
    planes, entry_hbm, adapter_hbm, counts_hbm, tokens_ref, down_ref, up_ref, table_ref, *refs
):
    others = planes - 1
    sends, tokens_out = refs[:others], refs[others : others + PLANE - 2]
    entry_ref, adapter_ref, counts_ref, held_ref, small_sem, tokens_sem, sem = refs[others + PLANE - 2 :]
    me = lax.axis_index("wide")
    column, plane = lax.rem(me, PLANE), lax.div(me, PLANE)
    run, up_run = down_ref.shape[2], up_ref.shape[2]
    small = [
        pltpu.make_async_copy(entry_hbm, entry_ref, small_sem.at[0]),
        pltpu.make_async_copy(adapter_hbm, adapter_ref, small_sem.at[1]),
        pltpu.make_async_copy(counts_hbm, counts_ref, small_sem.at[2]),
    ]
    for copy in small:
        copy.start()
    copies = []
    for k, out in enumerate(tokens_out):
        copies += slices(tokens_ref, column ^ (k + 2), run, out, tokens_sem.at[k])
    for copy in copies:
        copy.start()
    for copy in small:
        copy.wait()

    requests = counts_ref.shape[0]
    ends, total = [], 0
    for q in range(requests):
        total = total + counts_ref[q]
        ends.append(total)
    entries = [entry_ref[adapter_ref[q]] for q in range(requests)]

    def listed(p):
        ids = []
        for i in range(PLANE):
            block = p * PLANE + jnp.where(p % 2 == 0, i, PLANE - 1 - i)
            got = entries[0]
            for q in range(1, requests):
                got = jnp.where(ends[q - 1] <= block, entries[q], got)
            ids.append(got)
        place, held, count = [jnp.int32(0)], [ids[0]] * SLOTS, jnp.int32(1)
        for i in range(1, PLANE):
            found = count
            for j in range(i):
                found = jnp.where(ids[i] == ids[j], place[j], found)
            place.append(found)
            held = [jnp.where(found == s, ids[i], held[s]) for s in range(SLOTS)]
            count = jnp.maximum(count, found + 1)
        return held, place, count

    most = jnp.int32(1)
    for d in (*range(2, planes), 1, 0):
        held, place, count = listed(plane ^ d)
        most = jnp.maximum(most, count)
        if d > 0:
            for s in range(sends[d - 1].shape[0]):
                out = sends[d - 1].at[s]
                for part, (ref, at) in enumerate(
                    ((down_ref, pl.ds(0, run)), (up_ref, pl.ds(run, up_run)))
                ):
                    copies.append(
                        pltpu.make_async_copy(ref.at[held[s]], out.at[:, at], sem.at[d - 1, s, part])
                    )
                    copies[-1].start()
        else:
            for s in range(SLOTS):
                held_ref[PLANE + s] = held[s]
    for k in range(PLANE):
        i = column ^ k
        held_ref[k] = pick(jnp.where(plane % 2 == 0, i, PLANE - 1 - i), place)
    held_ref[PLANE + SLOTS] = jnp.where(most > USUAL, 1, 0)
    copies.append(pltpu.make_async_copy(held_ref, table_ref, small_sem.at[3]))
    copies[-1].start()
    for copy in copies:
        copy.wait()


def choose(planes, tokens, down, up, entry, adapter, counts):
    hbm = pl.BlockSpec(memory_space=pltpu.HBM)
    others = planes - 1
    rows = (2, down.shape[2] + up.shape[2], down.shape[3])
    sends = [
        jax.ShapeDtypeStruct((SLOTS if d == 1 else USUAL,) + rows, down.dtype) for d in range(1, planes)
    ]
    return pl.pallas_call(
        lambda *refs: choose_kernel(planes, *refs),
        out_shape=[jax.ShapeDtypeStruct((PLANE + SLOTS + 1,), jnp.int32)]
        + sends
        + [jax.ShapeDtypeStruct((2 * planes, BLK, down.shape[2]), tokens.dtype)] * (PLANE - 2),
        in_specs=[hbm] * 6,
        out_specs=[pl.BlockSpec(memory_space=pl.ANY)]
        + [pl.BlockSpec(memory_space=pltpu.VMEM)] * (others + PLANE - 2),
        scratch_shapes=[
            pltpu.SMEM(entry.shape, jnp.int32),
            pltpu.SMEM(adapter.shape, jnp.int32),
            pltpu.SMEM(counts.shape, jnp.int32),
            pltpu.SMEM((PLANE + SLOTS + 1,), jnp.int32),
            pltpu.SemaphoreType.DMA((4,)),
            pltpu.SemaphoreType.DMA((PLANE - 2, 2 * planes)),
            pltpu.SemaphoreType.DMA((others, SLOTS, 2)),
        ],
        compiler_params=pltpu.CompilerParams(vmem_limit_bytes=57 * 2**20),
        name="choose",
    )(entry, adapter, counts, tokens, down, up)


def gather_kernel(planes, table_ref, tokens_ref, down_ref, up_ref, own_ref, pair_ref, tokens_sem, sem):
    column = lax.rem(lax.axis_index("wide"), PLANE)
    run, up_run = down_ref.shape[2], up_ref.shape[2]
    copies = []
    for core in range(2):
        at = lax.div(column, 2) * 2 + core
        copies += slices(tokens_ref, at, run, pair_ref.at[core], tokens_sem.at[core])
    for s in range(SLOTS):
        slot = table_ref[PLANE + s]
        out = own_ref.at[s]
        for part, (ref, rows) in enumerate(
            ((down_ref, pl.ds(0, run)), (up_ref, pl.ds(run, up_run)))
        ):
            copies.append(pltpu.make_async_copy(ref.at[slot], out.at[:, rows], sem.at[s, part]))
    for copy in copies:
        copy.start()
    for copy in copies:
        copy.wait()


def gather(planes, table, tokens, down, up):
    run = down.shape[2]
    hbm = pl.BlockSpec(memory_space=pltpu.HBM)
    rows = (2, run + up.shape[2], down.shape[3])
    return pl.pallas_call(
        lambda *refs: gather_kernel(planes, *refs),
        out_shape=[
            jax.ShapeDtypeStruct((SLOTS,) + rows, down.dtype),
        ]
        + [jax.ShapeDtypeStruct((2, 2 * planes, BLK, run), tokens.dtype)],
        in_specs=[pl.BlockSpec(memory_space=pltpu.SMEM)] + [hbm] * 3,
        out_specs=[pl.BlockSpec(memory_space=pltpu.VMEM)] * 2,
        scratch_shapes=[
            pltpu.SemaphoreType.DMA((2, 2 * planes)),
            pltpu.SemaphoreType.DMA((SLOTS, 2)),
        ],
        compiler_params=pltpu.CompilerParams(vmem_limit_bytes=57 * 2**20),
        name="gather",
    )(table, tokens, down, up)


def up_rows(factors, distances, place):
    rows = []
    for d in distances:
        slot = jnp.minimum(place, factors[d].shape[0] - 1)
        rows += [factors[d][slot, half] for half in range(2)]
    return rows


def shrink(
    planes,
    slots,
    run,
    blocks,
    near,
    first,
    far,
    places,
    rows,
    factors,
    held=(),
    ups=None,
    flops=None,
    kept=(),
    flag=False,
):
    vmem = pl.BlockSpec(memory_space=pltpu.VMEM)
    up_run, ranks = factors[0].shape[2] - run, factors[0].shape[3]

    used = sorted({*first, *far})

    def kernel(places_ref, *refs):
        row_refs, refs = refs[: len(rows)], refs[len(rows) :]
        factor_refs, refs = dict(zip(used, refs)), refs[len(used) :]
        held_refs, outs = list(refs[: len(held)]), refs[len(held) + len(kept) :]
        me = lax.axis_index("wide")
        core, plane = lax.rem(me, 2), lax.div(me, PLANE)
        at = [places_ref[k] for k in blocks]
        views = {d: ref.at[:, :, pl.ds(run, up_run)] for d, ref in factor_refs.items()}

        def rows_at(k, piece):
            return row_refs[0][core ^ k, piece] if k < 2 else row_refs[k - 1][piece]

        def sums_of(chosen, distances):
            total = jnp.zeros((len(chosen) * BLK, slots * ranks), jnp.float32)
            for d in distances:
                for half in range(2):
                    piece = half * planes + (plane ^ d)
                    total += jnp.dot(
                        jnp.concatenate([rows_at(blocks[i], piece) for i in chosen], axis=0),
                        jnp.concatenate(
                            [factor_refs[d][s, half, pl.ds(0, run)] for s in range(slots)], axis=1
                        ),
                        preferred_element_type=jnp.float32,
                    )
            parts = [total[j * BLK : (j + 1) * BLK] for j in range(len(chosen))]
            return {
                i: pick(at[i], [part[:, s * ranks : (s + 1) * ranks] for s in range(slots)])
                for i, part in zip(chosen, parts)
            }

        if flag:
            *outs, flag_ref = outs
            flag_ref[0] = places_ref[PLANE + SLOTS]
        every = range(len(blocks))
        mine = sums_of(every, far) if far else {}
        here = [i for i in every if blocks[i] in near]
        for i, part in (sums_of(here, first) if here else {}).items():
            mine[i] = mine[i] + part if far else part
        for i in every:
            if i not in here:
                mine[i] = mine[i] + held_refs.pop(0)[...]
            outs[i][pl.ds(0, BLK)] = mine[i].astype(outs[i].dtype)
            for j, part in enumerate(up_rows(views, ups or (), at[i])):
                outs[i][pl.ds(BLK + j * up_run, up_run)] = part.astype(outs[i].dtype)

    height = BLK + len(ups or ()) * 2 * up_run
    exact = [ups is None or k == 0 for k in blocks]
    cost = None
    if flops is not None:
        cost = pl.CostEstimate(flops=flops, bytes_accessed=0, transcendentals=0)
    return pl.pallas_call(
        kernel,
        out_shape=[
            jax.ShapeDtypeStruct((height, ranks), jnp.float32 if full else rows[0].dtype)
            for full in exact
        ]
        + [jax.ShapeDtypeStruct((1,), jnp.int32)] * flag,
        in_specs=[pl.BlockSpec(memory_space=pltpu.SMEM)]
        + [vmem] * (len(rows) + len(used) + len(held))
        + [pl.BlockSpec(memory_space=pl.ANY)] * len(kept),
        out_specs=[vmem] * len(blocks) + [pl.BlockSpec(memory_space=pltpu.SMEM)] * flag,
        compiler_params=pltpu.CompilerParams(vmem_limit_bytes=10 * 2**20),
        cost_estimate=cost,
        name="shrink",
    )(places, *rows, *[factors[d] for d in used], *held, *kept)


def expand(planes, up_run, sums):
    ranks = sums[0].shape[1]
    columns = 2 * planes * PLANE * up_run
    vmem = pl.BlockSpec(memory_space=pltpu.VMEM)
    span = 2 * up_run

    def kernel(*refs):
        sum_refs = refs[:PLANE]
        key_ref, value_ref, factor = refs[PLANE:]
        me = lax.axis_index("wide")
        column, plane = lax.rem(me, PLANE), lax.div(me, PLANE)
        total = jnp.zeros((BLK, ranks), jnp.float32)
        for k in range(PLANE):
            total += sum_refs[k][pl.ds(0, BLK)].astype(jnp.float32)
            for d in range(planes):
                rows = sum_refs[k][pl.ds(BLK + d * span, span)]
                factor[plane ^ d, :, column ^ k] = rows.astype(factor.dtype).reshape(2, up_run, ranks)
        low_rank = total.astype(jnp.bfloat16)
        is_key = lax.broadcasted_iota(jnp.int32, low_rank.shape, 1) < ranks // 2
        zero = jnp.zeros_like(low_rank)
        both = jnp.concatenate(
            [jnp.where(is_key, low_rank, zero), jnp.where(is_key, zero, low_rank)], axis=0
        )
        for half in range(2):
            for p in range(planes):
                delta = lax.dot_general(
                    both,
                    factor[p, half].reshape(PLANE * up_run, ranks),
                    (((1,), (1,)), ((), ())),
                    preferred_element_type=jnp.float32,
                ).astype(jnp.bfloat16)
                at = pl.ds((half * planes + p) * PLANE * up_run, PLANE * up_run)
                key_ref[:, at] = delta[:BLK]
                value_ref[:, at] = delta[BLK:]

    return pl.pallas_call(
        kernel,
        out_shape=[jax.ShapeDtypeStruct((BLK, columns), jnp.bfloat16)] * 2,
        in_specs=[vmem] * PLANE,
        out_specs=[vmem] * 2,
        scratch_shapes=[pltpu.VMEM((planes, 2, PLANE, up_run, ranks), jnp.bfloat16)],
        compiler_params=pltpu.CompilerParams(vmem_limit_bytes=4 * 2**20),
        name="expand",
    )(*sums)


def plane_body(
    tokens,
    adapter_down_weight,
    adapter_up_weight,
    adapter_entry,
    adapter_of_request,
    token_blocks_per_request,
):
    planes = lax.axis_size("wide") // PLANE
    places, *sends = choose(
        planes,
        tokens,
        adapter_down_weight,
        adapter_up_weight,
        adapter_entry,
        adapter_of_request,
        token_blocks_per_request,
    )
    factors, across = sends[: planes - 1], sends[planes - 1 :]
    own_factors, pair = gather(planes, places, tokens, adapter_down_weight, adapter_up_weight)
    sends = sends + [pair]
    run, up_run = adapter_down_weight.shape[2], adapter_up_weight.shape[2]
    whole, blocks = tuple(range(planes)), tuple(range(PLANE))
    factors = [own_factors] + [swap(factors[d - 1], d * PLANE) for d in whole[1:]]
    rows = [swap_cores(pair)] + [swap(across[k - 2], k) for k in range(2, PLANE)]
    early = (0, 2)
    *held, many = shrink(
        planes,
        USUAL,
        run,
        blocks[:2],
        blocks[:2],
        early,
        (),
        places,
        rows[:1],
        factors,
        flops=3*10**9,
        flag=True,
    )

    def finish(sums):
        sums = [sums[0]] + [swap(sums[k], k) for k in range(1, PLANE)]
        return tuple(expand(planes, up_run, sums))

    def usual(places, factors, rows, held, kept):
        args = (early, (1, 3), places, rows, factors)
        sums = shrink(planes, USUAL, run, blocks[1:], blocks[2:], *args, held[1:], whole)
        return finish([*shrink(planes, USUAL, run, blocks[:1], (), *args, held[:1], whole), *sums])

    def more(places, factors, rows, held, kept):
        third = [swap(factors[d ^ 1][:1], PLANE) for d in whole[2:]]
        factors = factors[:2] + [jnp.concatenate([factors[d], third[d - 2]]) for d in whole[2:]]
        sums = shrink(
            planes, SLOTS, run, blocks, blocks, whole, (), places, rows, factors, (), whole, kept=kept
        )
        return finish(sums)

    return lax.switch(many[0], [usual, more], places, factors, rows, held, sends)


def solution(mesh):
    by_plane = mesh.shape["wide"] == 16 and mesh.shape["narrow"] == 1
    return jax.shard_map(
        plane_body if by_plane else direct_body,
        mesh=mesh,
        in_specs=(
            P(("groups", "wide"), "narrow"),
            P(None, "narrow", "wide", None),
            P(None, "narrow", "wide", None),
            P(),
            P("groups"),
            P("groups"),
        ),
        out_specs=(P(("groups", "wide"), "narrow"), P(("groups", "wide"), "narrow")),
        check_vma=False,
    )
```

```python
import jax
import jax.numpy as jnp
from jax import lax
from jax.experimental import pallas as pl
from jax.experimental.pallas import tpu as pltpu
from jax.sharding import PartitionSpec as P

BLK = 128
PLANE = 4
SLOTS = 3
USUAL = 2


def block_tables(
    adapter_entry,
    adapter_of_request,
    token_blocks_per_request,
    block_count,
    request_count,
    adapter_count,
):
    request_ends = jnp.cumsum(token_blocks_per_request)
    block_index = jnp.arange(block_count, dtype=jnp.int32)
    request = jnp.sum((request_ends[None, :] <= block_index[:, None]).astype(jnp.int32), axis=1)
    pick_table = (request[:, None] == jnp.arange(request_count, dtype=jnp.int32)[None, :]).astype(
        jnp.int32
    )
    adapter = jnp.sum(pick_table * adapter_of_request[None, :], axis=1)
    slot_table = (adapter[:, None] == jnp.arange(adapter_count, dtype=jnp.int32)[None, :]).astype(
        jnp.int32
    )
    return jnp.sum(slot_table * adapter_entry[None, :], axis=1)


def direct_body(
    tokens,
    adapter_down_weight,
    adapter_up_weight,
    adapter_entry,
    adapter_of_request,
    token_blocks_per_request,
):
    wide_count = lax.axis_size("wide")
    blocks_dev = tokens.shape[0] // BLK
    local_width = tokens.shape[1]
    paired_ranks = adapter_down_weight.shape[3]
    rank_count = paired_ranks // 2
    slot_ids = block_tables(
        adapter_entry,
        adapter_of_request,
        token_blocks_per_request,
        blocks_dev * wide_count,
        token_blocks_per_request.shape[0],
        adapter_entry.shape[0],
    )
    needed_adapters = slot_ids.reshape(wide_count, blocks_dev).T
    down_outgoing = adapter_down_weight[needed_adapters]
    up_outgoing = adapter_up_weight[needed_adapters]
    got_down, got_up = (
        lax.all_to_all(down_outgoing, "wide", split_axis=1, concat_axis=3, tiled=True),
        lax.all_to_all(up_outgoing, "wide", split_axis=1, concat_axis=3, tiled=True),
    )
    got_down = got_down.reshape(blocks_dev, local_width, paired_ranks)
    block_rows = tokens.reshape(blocks_dev, BLK, local_width)
    shrink = jnp.einsum("btd,bdr->btr", block_rows, got_down, preferred_element_type=jnp.float32)
    low_rank = lax.psum(shrink, "narrow").astype(jnp.bfloat16)
    got_up = got_up.reshape(blocks_dev, -1, paired_ranks)
    delta_key = jnp.einsum(
        "btr,bjr->btj",
        low_rank[..., :rank_count],
        got_up[..., :rank_count],
        preferred_element_type=jnp.float32,
    )
    delta_value = jnp.einsum(
        "btr,bjr->btj",
        low_rank[..., rank_count:],
        got_up[..., rank_count:],
        preferred_element_type=jnp.float32,
    )
    out_cols = got_up.shape[1]
    key_delta = delta_key.reshape(blocks_dev * BLK, out_cols).astype(jnp.bfloat16)
    value_delta = delta_value.reshape(blocks_dev * BLK, out_cols).astype(jnp.bfloat16)
    return (key_delta, value_delta)


def swap(value, step):
    count = lax.axis_size("wide")
    return lax.ppermute(value, "wide", [(i, i ^ step) for i in range(count)])


def swap_cores(value):
    count = lax.axis_size("wide")
    pairs = [[i, i + 1] for i in range(0, count, 2)]
    return lax.all_to_all(value, "wide", 0, 0, axis_index_groups=pairs, tiled=True)


def pick(index, values):
    got = values[0]
    for i in range(1, len(values)):
        got = jnp.where(index == i, values[i], got)
    return got


def landed(out, sem):
    pltpu.make_async_copy(out, out, sem).wait()


def slices(tokens_ref, column, run, out, sem):
    return [
        pltpu.make_async_copy(
            tokens_ref.at[:, pl.ds(pl.multiple_of((piece * PLANE + column) * run, run), run)],
            out.at[piece],
            sem,
        )
        for piece in range(out.shape[0])
    ]


def choose_kernel(
    planes, entry_hbm, adapter_hbm, counts_hbm, tokens_ref, down_ref, up_ref, table_ref, *refs
):
    others = planes - 1
    sends, tokens_out = refs[:others], refs[others : others + PLANE - 2]
    entry_ref, adapter_ref, counts_ref, held_ref, small_sem, tokens_sem, sem = refs[others + PLANE - 2 :]
    me = lax.axis_index("wide")
    column, plane = lax.rem(me, PLANE), lax.div(me, PLANE)
    run, up_run = down_ref.shape[2], up_ref.shape[2]
    small = [
        pltpu.make_async_copy(entry_hbm, entry_ref, small_sem.at[0]),
        pltpu.make_async_copy(adapter_hbm, adapter_ref, small_sem.at[1]),
        pltpu.make_async_copy(counts_hbm, counts_ref, small_sem.at[2]),
    ]
    for copy in small:
        copy.start()
    for k, out in enumerate(tokens_out):
        for copy in slices(tokens_ref, column ^ (k + 2), run, out, tokens_sem.at[k]):
            copy.start()
    for copy in small:
        copy.wait()

    requests = counts_ref.shape[0]
    ends, total = [], 0
    for q in range(requests):
        total = total + counts_ref[q]
        ends.append(total)
    entries = [entry_ref[adapter_ref[q]] for q in range(requests)]

    def listed(p):
        ids = []
        for i in range(PLANE):
            block = p * PLANE + jnp.where(p % 2 == 0, i, PLANE - 1 - i)
            got = entries[0]
            for q in range(1, requests):
                got = jnp.where(ends[q - 1] <= block, entries[q], got)
            ids.append(got)
        place, held, count = [jnp.int32(0)], [ids[0]] * SLOTS, jnp.int32(1)
        for i in range(1, PLANE):
            found = count
            for j in range(i):
                found = jnp.where(ids[i] == ids[j], place[j], found)
            place.append(found)
            held = [jnp.where(found == s, ids[i], held[s]) for s in range(SLOTS)]
            count = jnp.maximum(count, found + 1)
        return held, place, count

    most = jnp.int32(1)
    for d in (*range(2, planes), 1, 0):
        held, place, count = listed(plane ^ d)
        most = jnp.maximum(most, count)
        if d > 0:
            for s in range(sends[d - 1].shape[0]):
                out = sends[d - 1].at[s]
                for ref, at in (down_ref, pl.ds(0, run)), (up_ref, pl.ds(run, up_run)):
                    pltpu.make_async_copy(ref.at[held[s]], out.at[:, at], sem.at[d - 1]).start()
        else:
            for s in range(SLOTS):
                held_ref[PLANE + s] = held[s]
    for k in range(PLANE):
        i = column ^ k
        held_ref[k] = pick(jnp.where(plane % 2 == 0, i, PLANE - 1 - i), place)
    held_ref[PLANE + SLOTS] = jnp.where(most > USUAL, 1, 0)
    table = pltpu.make_async_copy(held_ref, table_ref, small_sem.at[3])
    table.start()
    for k, out in enumerate(tokens_out):
        landed(out, tokens_sem.at[k])
    for d, out in enumerate(sends):
        landed(out, sem.at[d])
    table.wait()


def choose(planes, tokens, down, up, entry, adapter, counts):
    hbm = pl.BlockSpec(memory_space=pltpu.HBM)
    others = planes - 1
    rows = (2, down.shape[2] + up.shape[2], down.shape[3])
    sends = [
        jax.ShapeDtypeStruct((SLOTS if d == 1 else USUAL,) + rows, down.dtype) for d in range(1, planes)
    ]
    return pl.pallas_call(
        lambda *refs: choose_kernel(planes, *refs),
        out_shape=[jax.ShapeDtypeStruct((PLANE + SLOTS + 1,), jnp.int32)]
        + sends
        + [jax.ShapeDtypeStruct((2 * planes, BLK, down.shape[2]), tokens.dtype)] * (PLANE - 2),
        in_specs=[hbm] * 6,
        out_specs=[pl.BlockSpec(memory_space=pl.ANY)]
        + [pl.BlockSpec(memory_space=pltpu.VMEM)] * (others + PLANE - 2),
        scratch_shapes=[
            pltpu.SMEM(entry.shape, jnp.int32),
            pltpu.SMEM(adapter.shape, jnp.int32),
            pltpu.SMEM(counts.shape, jnp.int32),
            pltpu.SMEM((PLANE + SLOTS + 1,), jnp.int32),
            pltpu.SemaphoreType.DMA((4,)),
            pltpu.SemaphoreType.DMA((PLANE - 2,)),
            pltpu.SemaphoreType.DMA((others,)),
        ],
        compiler_params=pltpu.CompilerParams(vmem_limit_bytes=57 * 2**20),
        name="choose",
    )(entry, adapter, counts, tokens, down, up)


def gather_kernel(planes, table_ref, tokens_ref, down_ref, up_ref, own_ref, pair_ref, tokens_sem, sem):
    column = lax.rem(lax.axis_index("wide"), PLANE)
    run, up_run = down_ref.shape[2], up_ref.shape[2]
    for core in range(2):
        at = lax.div(column, 2) * 2 + core
        for copy in slices(tokens_ref, at, run, pair_ref.at[core], tokens_sem.at[core]):
            copy.start()
    for s in range(SLOTS):
        slot = table_ref[PLANE + s]
        for ref, rows in (down_ref, pl.ds(0, run)), (up_ref, pl.ds(run, up_run)):
            pltpu.make_async_copy(ref.at[slot], own_ref.at[s, :, rows], sem).start()
    for core in range(2):
        landed(pair_ref.at[core], tokens_sem.at[core])
    landed(own_ref, sem)


def gather(planes, table, tokens, down, up):
    run = down.shape[2]
    hbm = pl.BlockSpec(memory_space=pltpu.HBM)
    rows = (2, run + up.shape[2], down.shape[3])
    return pl.pallas_call(
        lambda *refs: gather_kernel(planes, *refs),
        out_shape=[
            jax.ShapeDtypeStruct((SLOTS,) + rows, down.dtype),
        ]
        + [jax.ShapeDtypeStruct((2, 2 * planes, BLK, run), tokens.dtype)],
        in_specs=[pl.BlockSpec(memory_space=pltpu.SMEM)] + [hbm] * 3,
        out_specs=[pl.BlockSpec(memory_space=pltpu.VMEM)] * 2,
        scratch_shapes=[
            pltpu.SemaphoreType.DMA((2,)),
            pltpu.SemaphoreType.DMA(()),
        ],
        compiler_params=pltpu.CompilerParams(vmem_limit_bytes=57 * 2**20),
        name="gather",
    )(table, tokens, down, up)


def up_rows(factors, distances, place):
    rows = []
    for d in distances:
        slot = jnp.minimum(place, factors[d].shape[0] - 1)
        rows += [factors[d][slot, half] for half in range(2)]
    return rows


def shrink(
    planes,
    slots,
    run,
    blocks,
    near,
    first,
    far,
    places,
    rows,
    factors,
    held=(),
    ups=None,
    flops=None,
    kept=(),
    flag=False,
):
    vmem, smem = pl.BlockSpec(memory_space=pltpu.VMEM), pl.BlockSpec(memory_space=pltpu.SMEM)
    up_run, ranks = factors[0].shape[2] - run, factors[0].shape[3]

    used = sorted({*first, *far})

    def kernel(places_ref, *refs):
        spread = len(places.shape) > 1
        row_refs, refs = refs[: len(rows)], refs[len(rows) :]
        factor_refs, refs = dict(zip(used, refs)), refs[len(used) :]
        held_refs, outs = list(refs[: len(held)]), refs[len(held) + len(kept) :]
        me = lax.axis_index("wide")
        core, plane = lax.rem(me, 2), lax.div(me, PLANE)
        at = [places_ref[k, pl.ds(0, 1)] if spread else places_ref[k] for k in blocks]
        views = {d: ref.at[:, :, pl.ds(run, up_run)] for d, ref in factor_refs.items()}

        def rows_of_up(place):
            if not spread:
                return up_rows(views, ups or (), place)
            return [
                pick(place, [views[d][s, half].astype(jnp.float32) for s in range(slots)])
                for d in ups or ()
                for half in range(2)
            ]

        def rows_at(k, piece):
            return row_refs[0][core ^ k, piece] if k < 2 else row_refs[k - 1][piece]

        def sums_of(chosen, distances):
            total = jnp.zeros((len(chosen) * BLK, slots * ranks), jnp.float32)
            for d in distances:
                for half in range(2):
                    piece = half * planes + (plane ^ d)
                    total += jnp.dot(
                        jnp.concatenate([rows_at(blocks[i], piece) for i in chosen], axis=0),
                        jnp.concatenate(
                            [factor_refs[d][s, half, pl.ds(0, run)] for s in range(slots)], axis=1
                        ),
                        preferred_element_type=jnp.float32,
                    )
            parts = [total[j * BLK : (j + 1) * BLK] for j in range(len(chosen))]
            return {
                i: pick(at[i], [part[:, s * ranks : (s + 1) * ranks] for s in range(slots)])
                for i, part in zip(chosen, parts)
            }

        if flag:
            *outs, spread_ref, flag_ref = outs
            flag_ref[0] = places_ref[PLANE + SLOTS]
            for k in range(PLANE):
                spread_ref[k] = jnp.full(spread_ref.shape[1:], places_ref[k], jnp.int32)
        every = range(len(blocks))
        mine = sums_of(every, far) if far else {}
        here = [i for i in every if blocks[i] in near]
        for i, part in (sums_of(here, first) if here else {}).items():
            mine[i] = mine[i] + part if far else part
        for i in every:
            if i not in here:
                mine[i] = mine[i] + held_refs.pop(0)[...]
            outs[i][pl.ds(0, BLK)] = mine[i].astype(outs[i].dtype)
            for j, part in enumerate(rows_of_up(at[i])):
                outs[i][pl.ds(BLK + j * up_run, up_run)] = part.astype(outs[i].dtype)

    height = BLK + len(ups or ()) * 2 * up_run
    exact = [ups is None or k == 0 for k in blocks]
    cost = None
    if flops is not None:
        cost = pl.CostEstimate(flops=flops, bytes_accessed=0, transcendentals=0)
    return pl.pallas_call(
        kernel,
        out_shape=[
            jax.ShapeDtypeStruct((height, ranks), jnp.float32 if full else rows[0].dtype)
            for full in exact
        ]
        + [jax.ShapeDtypeStruct((PLANE, 8, ranks), jnp.int32), jax.ShapeDtypeStruct((1,), jnp.int32)]
        * flag,
        in_specs=[vmem if len(places.shape) > 1 else smem]
        + [vmem] * (len(rows) + len(used) + len(held))
        + [pl.BlockSpec(memory_space=pl.ANY)] * len(kept),
        out_specs=[vmem] * len(blocks) + [vmem, smem] * flag,
        compiler_params=pltpu.CompilerParams(vmem_limit_bytes=10 * 2**20),
        cost_estimate=cost,
        name="shrink",
    )(places, *rows, *[factors[d] for d in used], *held, *kept)


def expand(planes, up_run, sums):
    ranks = sums[0].shape[1]
    columns = 2 * planes * PLANE * up_run
    vmem = pl.BlockSpec(memory_space=pltpu.VMEM)
    span = 2 * up_run
    order = (2, 3, 1, 0)

    def kernel(*refs):
        sum_refs = dict(zip(order, refs))
        key_ref, value_ref, factor = refs[PLANE:]
        me = lax.axis_index("wide")
        column, plane = lax.rem(me, PLANE), lax.div(me, PLANE)
        total = jnp.zeros((BLK, ranks), jnp.float32)
        for k in range(PLANE):
            total += sum_refs[k][pl.ds(0, BLK)].astype(jnp.float32)
            for d in range(planes):
                rows = sum_refs[k][pl.ds(BLK + d * span, span)]
                factor[plane ^ d, :, column ^ k] = rows.astype(factor.dtype).reshape(2, up_run, ranks)
        low_rank = total.astype(jnp.bfloat16)
        is_key = lax.broadcasted_iota(jnp.int32, low_rank.shape, 1) < ranks // 2
        zero = jnp.zeros_like(low_rank)
        both = jnp.concatenate(
            [jnp.where(is_key, low_rank, zero), jnp.where(is_key, zero, low_rank)], axis=0
        )
        for half in range(2):
            for p in range(planes):
                delta = lax.dot_general(
                    both,
                    factor[p, half].reshape(PLANE * up_run, ranks),
                    (((1,), (1,)), ((), ())),
                    preferred_element_type=jnp.float32,
                ).astype(jnp.bfloat16)
                at = pl.ds((half * planes + p) * PLANE * up_run, PLANE * up_run)
                key_ref[:, at] = delta[:BLK]
                value_ref[:, at] = delta[BLK:]

    return pl.pallas_call(
        kernel,
        out_shape=[jax.ShapeDtypeStruct((BLK, columns), jnp.bfloat16)] * 2,
        in_specs=[vmem] * PLANE,
        out_specs=[vmem] * 2,
        scratch_shapes=[pltpu.VMEM((planes, 2, PLANE, up_run, ranks), jnp.bfloat16)],
        compiler_params=pltpu.CompilerParams(vmem_limit_bytes=4 * 2**20),
        name="expand",
    )(*[sums[k] for k in order])


def plane_body(
    tokens,
    adapter_down_weight,
    adapter_up_weight,
    adapter_entry,
    adapter_of_request,
    token_blocks_per_request,
):
    planes = lax.axis_size("wide") // PLANE
    places, *sends = choose(
        planes,
        tokens,
        adapter_down_weight,
        adapter_up_weight,
        adapter_entry,
        adapter_of_request,
        token_blocks_per_request,
    )
    factors, across = sends[: planes - 1], sends[planes - 1 :]
    own_factors, pair = gather(planes, places, tokens, adapter_down_weight, adapter_up_weight)
    sends = sends + [pair]
    run, up_run = adapter_down_weight.shape[2], adapter_up_weight.shape[2]
    whole, blocks = tuple(range(planes)), tuple(range(PLANE))
    factors = [own_factors] + [swap(factors[d - 1], d * PLANE) for d in whole[1:]]
    rows = [swap_cores(pair)] + [swap(across[k - 2], k) for k in range(2, PLANE)]
    early = (0, 2)
    *held, spread, many = shrink(
        planes,
        USUAL,
        run,
        blocks[:2],
        blocks[:2],
        early,
        (),
        places,
        rows[:1],
        factors,
        flops=3*10**9,
        flag=True,
    )

    def finish(sums):
        sums = [sums[0]] + [swap(sums[k], k) for k in range(1, PLANE)]
        return tuple(expand(planes, up_run, sums))

    def usual(places, spread, factors, rows, held, kept):
        args = (early, (1, 3), spread, rows, factors)
        sums = shrink(planes, USUAL, run, blocks[1:], blocks[2:], *args, held[1:], whole)
        return finish([*shrink(planes, USUAL, run, blocks[:1], (), *args, held[:1], whole), *sums])

    def more(places, spread, factors, rows, held, kept):
        third = [swap(factors[d ^ 1][:1], PLANE) for d in whole[2:]]
        factors = factors[:2] + [jnp.concatenate([factors[d], third[d - 2]]) for d in whole[2:]]
        sums = shrink(
            planes, SLOTS, run, blocks, blocks, whole, (), places, rows, factors, (), whole, kept=kept
        )
        return finish(sums)

    return lax.switch(many[0], [usual, more], places, spread, factors, rows, held, sends)


def solution(mesh):
    by_plane = mesh.shape["wide"] == 16 and mesh.shape["narrow"] == 1
    return jax.shard_map(
        plane_body if by_plane else direct_body,
        mesh=mesh,
        in_specs=(
            P(("groups", "wide"), "narrow"),
            P(None, "narrow", "wide", None),
            P(None, "narrow", "wide", None),
            P(),
            P("groups"),
            P("groups"),
        ),
        out_specs=(P(("groups", "wide"), "narrow"), P(("groups", "wide"), "narrow")),
        check_vma=False,
    )
```

```python
import jax
import jax.numpy as jnp
from jax import lax
from jax.experimental import pallas as pl
from jax.experimental.pallas import tpu as pltpu
from jax.sharding import PartitionSpec as P

BLK = 128
PLANE = 4
SLOTS = 3
USUAL = 2


def block_tables(
    adapter_entry,
    adapter_of_request,
    token_blocks_per_request,
    block_count,
    request_count,
    adapter_count,
):
    request_ends = jnp.cumsum(token_blocks_per_request)
    block_index = jnp.arange(block_count, dtype=jnp.int32)
    request = jnp.sum((request_ends[None, :] <= block_index[:, None]).astype(jnp.int32), axis=1)
    pick_table = (request[:, None] == jnp.arange(request_count, dtype=jnp.int32)[None, :]).astype(
        jnp.int32
    )
    adapter = jnp.sum(pick_table * adapter_of_request[None, :], axis=1)
    slot_table = (adapter[:, None] == jnp.arange(adapter_count, dtype=jnp.int32)[None, :]).astype(
        jnp.int32
    )
    return jnp.sum(slot_table * adapter_entry[None, :], axis=1)


def direct_body(
    tokens,
    adapter_down_weight,
    adapter_up_weight,
    adapter_entry,
    adapter_of_request,
    token_blocks_per_request,
):
    wide_count = lax.axis_size("wide")
    blocks_dev = tokens.shape[0] // BLK
    local_width = tokens.shape[1]
    paired_ranks = adapter_down_weight.shape[3]
    rank_count = paired_ranks // 2
    slot_ids = block_tables(
        adapter_entry,
        adapter_of_request,
        token_blocks_per_request,
        blocks_dev * wide_count,
        token_blocks_per_request.shape[0],
        adapter_entry.shape[0],
    )
    needed_adapters = slot_ids.reshape(wide_count, blocks_dev).T
    down_outgoing = adapter_down_weight[needed_adapters]
    up_outgoing = adapter_up_weight[needed_adapters]
    got_down, got_up = (
        lax.all_to_all(down_outgoing, "wide", split_axis=1, concat_axis=3, tiled=True),
        lax.all_to_all(up_outgoing, "wide", split_axis=1, concat_axis=3, tiled=True),
    )
    got_down = got_down.reshape(blocks_dev, local_width, paired_ranks)
    block_rows = tokens.reshape(blocks_dev, BLK, local_width)
    shrink = jnp.einsum("btd,bdr->btr", block_rows, got_down, preferred_element_type=jnp.float32)
    low_rank = lax.psum(shrink, "narrow").astype(jnp.bfloat16)
    got_up = got_up.reshape(blocks_dev, -1, paired_ranks)
    delta_key = jnp.einsum(
        "btr,bjr->btj",
        low_rank[..., :rank_count],
        got_up[..., :rank_count],
        preferred_element_type=jnp.float32,
    )
    delta_value = jnp.einsum(
        "btr,bjr->btj",
        low_rank[..., rank_count:],
        got_up[..., rank_count:],
        preferred_element_type=jnp.float32,
    )
    out_cols = got_up.shape[1]
    key_delta = delta_key.reshape(blocks_dev * BLK, out_cols).astype(jnp.bfloat16)
    value_delta = delta_value.reshape(blocks_dev * BLK, out_cols).astype(jnp.bfloat16)
    return (key_delta, value_delta)


def swap(value, step):
    count = lax.axis_size("wide")
    return lax.ppermute(value, "wide", [(i, i ^ step) for i in range(count)])


def swap_cores(value):
    count = lax.axis_size("wide")
    pairs = [[i, i + 1] for i in range(0, count, 2)]
    return lax.all_to_all(value, "wide", 0, 0, axis_index_groups=pairs, tiled=True)


def pick(index, values):
    got = values[0]
    for i in range(1, len(values)):
        got = jnp.where(index == i, values[i], got)
    return got


def landed(out, sem):
    pltpu.make_async_copy(out, out, sem).wait()


def slices(tokens_ref, column, run, out, sem):
    return [
        pltpu.make_async_copy(
            tokens_ref.at[:, pl.ds(pl.multiple_of((piece * PLANE + column) * run, run), run)],
            out.at[piece],
            sem,
        )
        for piece in range(out.shape[0])
    ]


def choose_kernel(
    planes, entry_hbm, adapter_hbm, counts_hbm, tokens_ref, down_ref, up_ref, table_ref, *refs
):
    others = planes - 1
    sends, tokens_out = refs[:others], refs[others : others + PLANE - 2]
    entry_ref, adapter_ref, counts_ref, held_ref, small_sem, tokens_sem, sem = refs[others + PLANE - 2 :]
    me = lax.axis_index("wide")
    column, plane = lax.rem(me, PLANE), lax.div(me, PLANE)
    run, up_run = down_ref.shape[2], up_ref.shape[2]
    small = [
        pltpu.make_async_copy(entry_hbm, entry_ref, small_sem.at[0]),
        pltpu.make_async_copy(adapter_hbm, adapter_ref, small_sem.at[1]),
        pltpu.make_async_copy(counts_hbm, counts_ref, small_sem.at[2]),
    ]
    for copy in small:
        copy.start()
    for k, out in enumerate(tokens_out):
        for copy in slices(tokens_ref, column ^ (k + 2), run, out, tokens_sem.at[k]):
            copy.start()
    for copy in small:
        copy.wait()

    requests = counts_ref.shape[0]
    ends, total = [], 0
    for q in range(requests):
        total = total + counts_ref[q]
        ends.append(total)
    entries = [entry_ref[adapter_ref[q]] for q in range(requests)]

    def listed(p):
        ids = []
        for i in range(PLANE):
            block = p * PLANE + jnp.where(p % 2 == 0, i, PLANE - 1 - i)
            got = entries[0]
            for q in range(1, requests):
                got = jnp.where(ends[q - 1] <= block, entries[q], got)
            ids.append(got)
        place, held, count = [jnp.int32(0)], [ids[0]] * SLOTS, jnp.int32(1)
        for i in range(1, PLANE):
            found = count
            for j in range(i):
                found = jnp.where(ids[i] == ids[j], place[j], found)
            place.append(found)
            held = [jnp.where(found == s, ids[i], held[s]) for s in range(SLOTS)]
            count = jnp.maximum(count, found + 1)
        return held, place, count

    most = jnp.int32(1)
    for d in (*range(2, planes), 1, 0):
        held, place, count = listed(plane ^ d)
        most = jnp.maximum(most, count)
        if d > 0:
            for s in range(sends[d - 1].shape[0]):
                out = sends[d - 1].at[s]
                for ref, at in (down_ref, pl.ds(0, run)), (up_ref, pl.ds(run, up_run)):
                    pltpu.make_async_copy(ref.at[held[s]], out.at[:, at], sem.at[d - 1]).start()
        else:
            for s in range(SLOTS):
                held_ref[PLANE + s] = held[s]
    for k in range(PLANE):
        i = column ^ k
        held_ref[k] = pick(jnp.where(plane % 2 == 0, i, PLANE - 1 - i), place)
    held_ref[PLANE + SLOTS] = jnp.where(most > USUAL, 1, 0)
    table = pltpu.make_async_copy(held_ref, table_ref, small_sem.at[3])
    table.start()
    for k, out in enumerate(tokens_out):
        landed(out, tokens_sem.at[k])
    for d, out in enumerate(sends):
        landed(out, sem.at[d])
    table.wait()


def choose(planes, tokens, down, up, entry, adapter, counts):
    hbm = pl.BlockSpec(memory_space=pltpu.HBM)
    others = planes - 1
    rows = (2, down.shape[2] + up.shape[2], down.shape[3])
    sends = [
        jax.ShapeDtypeStruct((SLOTS if d == 1 else USUAL,) + rows, down.dtype) for d in range(1, planes)
    ]
    return pl.pallas_call(
        lambda *refs: choose_kernel(planes, *refs),
        out_shape=[jax.ShapeDtypeStruct((PLANE + SLOTS + 1,), jnp.int32)]
        + sends
        + [jax.ShapeDtypeStruct((2 * planes, BLK, down.shape[2]), tokens.dtype)] * (PLANE - 2),
        in_specs=[hbm] * 6,
        out_specs=[pl.BlockSpec(memory_space=pl.ANY)]
        + [pl.BlockSpec(memory_space=pltpu.VMEM)] * (others + PLANE - 2),
        scratch_shapes=[
            pltpu.SMEM(entry.shape, jnp.int32),
            pltpu.SMEM(adapter.shape, jnp.int32),
            pltpu.SMEM(counts.shape, jnp.int32),
            pltpu.SMEM((PLANE + SLOTS + 1,), jnp.int32),
            pltpu.SemaphoreType.DMA((4,)),
            pltpu.SemaphoreType.DMA((PLANE - 2,)),
            pltpu.SemaphoreType.DMA((others,)),
        ],
        compiler_params=pltpu.CompilerParams(vmem_limit_bytes=57 * 2**20),
        name="choose",
    )(entry, adapter, counts, tokens, down, up)


def gather_kernel(planes, table_ref, tokens_ref, down_ref, up_ref, own_ref, pair_ref, tokens_sem, sem):
    column = lax.rem(lax.axis_index("wide"), PLANE)
    run, up_run = down_ref.shape[2], up_ref.shape[2]
    for core in range(2):
        at = lax.div(column, 2) * 2 + core
        for copy in slices(tokens_ref, at, run, pair_ref.at[core], tokens_sem.at[core]):
            copy.start()
    for s in range(SLOTS):
        slot = table_ref[PLANE + s]
        for ref, rows in (down_ref, pl.ds(0, run)), (up_ref, pl.ds(run, up_run)):
            pltpu.make_async_copy(ref.at[slot], own_ref.at[s, :, rows], sem).start()
    for core in range(2):
        landed(pair_ref.at[core], tokens_sem.at[core])
    landed(own_ref, sem)


def gather(planes, table, tokens, down, up):
    run = down.shape[2]
    hbm = pl.BlockSpec(memory_space=pltpu.HBM)
    rows = (2, run + up.shape[2], down.shape[3])
    return pl.pallas_call(
        lambda *refs: gather_kernel(planes, *refs),
        out_shape=[
            jax.ShapeDtypeStruct((SLOTS,) + rows, down.dtype),
        ]
        + [jax.ShapeDtypeStruct((2, 2 * planes, BLK, run), tokens.dtype)],
        in_specs=[pl.BlockSpec(memory_space=pltpu.SMEM)] + [hbm] * 3,
        out_specs=[pl.BlockSpec(memory_space=pltpu.VMEM)] * 2,
        scratch_shapes=[
            pltpu.SemaphoreType.DMA((2,)),
            pltpu.SemaphoreType.DMA(()),
        ],
        compiler_params=pltpu.CompilerParams(vmem_limit_bytes=57 * 2**20),
        name="gather",
    )(table, tokens, down, up)


def up_rows(factors, distances, place):
    rows = []
    for d in distances:
        slot = jnp.minimum(place, factors[d].shape[0] - 1)
        rows += [factors[d][slot, half] for half in range(2)]
    return rows


def shrink(
    planes,
    slots,
    run,
    blocks,
    near,
    first,
    far,
    places,
    rows,
    factors,
    held=(),
    ups=None,
    flops=None,
    flag=False,
):
    vmem, smem = pl.BlockSpec(memory_space=pltpu.VMEM), pl.BlockSpec(memory_space=pltpu.SMEM)
    up_run, ranks = factors[0].shape[2] - run, factors[0].shape[3]

    used = sorted({*first, *far})

    def kernel(places_ref, *refs):
        spread = len(places.shape) > 1
        row_refs, refs = refs[: len(rows)], refs[len(rows) :]
        factor_refs, refs = dict(zip(used, refs)), refs[len(used) :]
        held_refs, outs = list(refs[: len(held)]), refs[len(held) :]
        me = lax.axis_index("wide")
        core, plane = lax.rem(me, 2), lax.div(me, PLANE)
        at = [places_ref[k, pl.ds(0, 1)] if spread else places_ref[k] for k in blocks]
        views = {d: ref.at[:, :, pl.ds(run, up_run)] for d, ref in factor_refs.items()}

        def rows_of_up(place):
            if not spread:
                return up_rows(views, ups or (), place)
            return [
                pick(place, [views[d][s, half].astype(jnp.float32) for s in range(slots)])
                for d in ups or ()
                for half in range(2)
            ]

        def rows_at(k, piece):
            return row_refs[0][core ^ k, piece] if k < 2 else row_refs[k - 1][piece]

        def sums_of(chosen, distances):
            total = jnp.zeros((len(chosen) * BLK, slots * ranks), jnp.float32)
            for d in distances:
                for half in range(2):
                    piece = half * planes + (plane ^ d)
                    total += jnp.dot(
                        jnp.concatenate([rows_at(blocks[i], piece) for i in chosen], axis=0),
                        jnp.concatenate(
                            [factor_refs[d][s, half, pl.ds(0, run)] for s in range(slots)], axis=1
                        ),
                        preferred_element_type=jnp.float32,
                    )
            parts = [total[j * BLK : (j + 1) * BLK] for j in range(len(chosen))]
            return {
                i: pick(at[i], [part[:, s * ranks : (s + 1) * ranks] for s in range(slots)])
                for i, part in zip(chosen, parts)
            }

        if flag:
            *outs, spread_ref, flag_ref = outs
            flag_ref[0] = places_ref[PLANE + SLOTS]
            for k in range(PLANE):
                spread_ref[k] = jnp.full(spread_ref.shape[1:], places_ref[k], jnp.int32)
        every = range(len(blocks))
        mine = sums_of(every, far) if far else {}
        here = [i for i in every if blocks[i] in near]
        for i, part in (sums_of(here, first) if here else {}).items():
            mine[i] = mine[i] + part if far else part
        for i in every:
            if i not in here:
                mine[i] = mine[i] + held_refs.pop(0)[...]
            outs[i][pl.ds(0, BLK)] = mine[i].astype(outs[i].dtype)
            for j, part in enumerate(rows_of_up(at[i])):
                outs[i][pl.ds(BLK + j * up_run, up_run)] = part.astype(outs[i].dtype)

    height = BLK + len(ups or ()) * 2 * up_run
    exact = [ups is None or k == 0 for k in blocks]
    cost = None
    if flops is not None:
        cost = pl.CostEstimate(flops=flops, bytes_accessed=0, transcendentals=0)
    return pl.pallas_call(
        kernel,
        out_shape=[
            jax.ShapeDtypeStruct((height, ranks), jnp.float32 if full else rows[0].dtype)
            for full in exact
        ]
        + [jax.ShapeDtypeStruct((PLANE, 8, ranks), jnp.int32), jax.ShapeDtypeStruct((1,), jnp.int32)]
        * flag,
        in_specs=[vmem if len(places.shape) > 1 else smem]
        + [vmem] * (len(rows) + len(used) + len(held)),
        out_specs=[vmem] * len(blocks) + [vmem, smem] * flag,
        compiler_params=pltpu.CompilerParams(vmem_limit_bytes=10 * 2**20),
        cost_estimate=cost,
        name="shrink",
    )(places, *rows, *[factors[d] for d in used], *held)


def amend(planes, run, places, rows, thirds, slots, sums, kept):
    vmem = pl.BlockSpec(memory_space=pltpu.VMEM)
    up_run, ranks = thirds[0].shape[2] - run, thirds[0].shape[3]

    def kernel(places_ref, *refs):
        row_refs, refs = refs[: len(rows)], refs[len(rows) :]
        third_refs, refs = refs[:planes], refs[planes:]
        sum_refs, outs = refs[:PLANE], refs[PLANE + len(kept) :]
        me = lax.axis_index("wide")
        core, plane = lax.rem(me, 2), lax.div(me, PLANE)
        total = jnp.zeros((PLANE * BLK, ranks), jnp.float32)
        for d in range(planes):
            for half in range(2):
                piece = half * planes + (plane ^ d)
                parts = [row_refs[0][core ^ k, piece] for k in range(2)]
                parts += [ref[piece] for ref in row_refs[1:]]
                total += jnp.dot(
                    jnp.concatenate(parts, axis=0),
                    third_refs[d][slots[d], half, pl.ds(0, run)],
                    preferred_element_type=jnp.float32,
                )
        for k in range(PLANE):
            anew = places_ref[k, pl.ds(0, 1)] == USUAL
            news = [(0, total[k * BLK : (k + 1) * BLK])]
            for d in range(planes):
                for half in range(2):
                    start = BLK + (2 * d + half) * up_run
                    news.append((start, third_refs[d][slots[d], half, pl.ds(run, up_run)]))
            for start, new in news:
                at = pl.ds(start, new.shape[0])
                old = sum_refs[k][at].astype(jnp.float32)
                outs[k][at] = jnp.where(anew, new.astype(jnp.float32), old).astype(outs[k].dtype)

    return pl.pallas_call(
        kernel,
        out_shape=[jax.ShapeDtypeStruct(value.shape, value.dtype) for value in sums],
        in_specs=[vmem] * (1 + len(rows) + planes + PLANE)
        + [pl.BlockSpec(memory_space=pl.ANY)] * len(kept),
        out_specs=[vmem] * PLANE,
        compiler_params=pltpu.CompilerParams(vmem_limit_bytes=10 * 2**20),
        name="amend",
    )(places, *rows, *thirds, *sums, *kept)


def expand(planes, up_run, sums):
    ranks = sums[0].shape[1]
    columns = 2 * planes * PLANE * up_run
    vmem = pl.BlockSpec(memory_space=pltpu.VMEM)
    span = 2 * up_run
    order = (2, 3, 1, 0)

    def kernel(*refs):
        sum_refs = dict(zip(order, refs))
        key_ref, value_ref, factor = refs[PLANE:]
        me = lax.axis_index("wide")
        column, plane = lax.rem(me, PLANE), lax.div(me, PLANE)
        total = jnp.zeros((BLK, ranks), jnp.float32)
        for k in range(PLANE):
            total += sum_refs[k][pl.ds(0, BLK)].astype(jnp.float32)
            for d in range(planes):
                rows = sum_refs[k][pl.ds(BLK + d * span, span)]
                factor[plane ^ d, :, column ^ k] = rows.astype(factor.dtype).reshape(2, up_run, ranks)
        low_rank = total.astype(jnp.bfloat16)
        is_key = lax.broadcasted_iota(jnp.int32, low_rank.shape, 1) < ranks // 2
        zero = jnp.zeros_like(low_rank)
        both = jnp.concatenate(
            [jnp.where(is_key, low_rank, zero), jnp.where(is_key, zero, low_rank)], axis=0
        )
        for half in range(2):
            for p in range(planes):
                delta = lax.dot_general(
                    both,
                    factor[p, half].reshape(PLANE * up_run, ranks),
                    (((1,), (1,)), ((), ())),
                    preferred_element_type=jnp.float32,
                ).astype(jnp.bfloat16)
                at = pl.ds((half * planes + p) * PLANE * up_run, PLANE * up_run)
                key_ref[:, at] = delta[:BLK]
                value_ref[:, at] = delta[BLK:]

    return pl.pallas_call(
        kernel,
        out_shape=[jax.ShapeDtypeStruct((BLK, columns), jnp.bfloat16)] * 2,
        in_specs=[vmem] * PLANE,
        out_specs=[vmem] * 2,
        scratch_shapes=[pltpu.VMEM((planes, 2, PLANE, up_run, ranks), jnp.bfloat16)],
        compiler_params=pltpu.CompilerParams(vmem_limit_bytes=4 * 2**20),
        name="expand",
    )(*[sums[k] for k in order])


def plane_body(
    tokens,
    adapter_down_weight,
    adapter_up_weight,
    adapter_entry,
    adapter_of_request,
    token_blocks_per_request,
):
    planes = lax.axis_size("wide") // PLANE
    places, *sends = choose(
        planes,
        tokens,
        adapter_down_weight,
        adapter_up_weight,
        adapter_entry,
        adapter_of_request,
        token_blocks_per_request,
    )
    factors, across = sends[: planes - 1], sends[planes - 1 :]
    own_factors, pair = gather(planes, places, tokens, adapter_down_weight, adapter_up_weight)
    sends = sends + [pair]
    run, up_run = adapter_down_weight.shape[2], adapter_up_weight.shape[2]
    whole, blocks = tuple(range(planes)), tuple(range(PLANE))
    factors = [own_factors] + [swap(factors[d - 1], d * PLANE) for d in whole[1:]]
    rows = [swap_cores(pair)] + [swap(across[k - 2], k) for k in range(2, PLANE)]
    early = (0, 2)
    *held, spread, many = shrink(
        planes,
        USUAL,
        run,
        blocks[:2],
        blocks[:2],
        early,
        (),
        places,
        rows[:1],
        factors,
        flops=3*10**9,
        flag=True,
    )

    def finish(sums):
        sums = [sums[0]] + [swap(sums[k], k) for k in range(1, PLANE)]
        return tuple(expand(planes, up_run, sums))

    def sums_of(spread, factors, rows, held):
        args = (early, (1, 3), spread, rows, factors)
        sums = shrink(planes, USUAL, run, blocks[1:], blocks[2:], *args, held[1:], whole)
        return [*shrink(planes, USUAL, run, blocks[:1], (), *args, held[:1], whole), *sums]

    def usual(spread, factors, rows, held, kept):
        return finish(sums_of(spread, factors, rows, held))

    def more(spread, factors, rows, held, kept):
        thirds = factors[:2] + [swap(factors[d ^ 1][:1], PLANE) for d in whole[2:]]
        slots = [USUAL if d < 2 else 0 for d in whole]
        sums = sums_of(spread, factors, rows, held)
        return finish(amend(planes, run, spread, rows, thirds, slots, sums, kept))

    return lax.switch(many[0], [usual, more], spread, factors, rows, held, sends)


def solution(mesh):
    by_plane = mesh.shape["wide"] == 16 and mesh.shape["narrow"] == 1
    return jax.shard_map(
        plane_body if by_plane else direct_body,
        mesh=mesh,
        in_specs=(
            P(("groups", "wide"), "narrow"),
            P(None, "narrow", "wide", None),
            P(None, "narrow", "wide", None),
            P(),
            P("groups"),
            P("groups"),
        ),
        out_specs=(P(("groups", "wide"), "narrow"), P(("groups", "wide"), "narrow")),
        check_vma=False,
    )
```

```python
import jax
import jax.numpy as jnp
from jax import lax
from jax.experimental import pallas as pl
from jax.experimental.pallas import tpu as pltpu
from jax.sharding import PartitionSpec as P

BLK = 128
PLANE = 4
SLOTS = 3
USUAL = 2


def block_tables(
    adapter_entry,
    adapter_of_request,
    token_blocks_per_request,
    block_count,
    request_count,
    adapter_count,
):
    request_ends = jnp.cumsum(token_blocks_per_request)
    block_index = jnp.arange(block_count, dtype=jnp.int32)
    request = jnp.sum((request_ends[None, :] <= block_index[:, None]).astype(jnp.int32), axis=1)
    pick_table = (request[:, None] == jnp.arange(request_count, dtype=jnp.int32)[None, :]).astype(
        jnp.int32
    )
    adapter = jnp.sum(pick_table * adapter_of_request[None, :], axis=1)
    slot_table = (adapter[:, None] == jnp.arange(adapter_count, dtype=jnp.int32)[None, :]).astype(
        jnp.int32
    )
    return jnp.sum(slot_table * adapter_entry[None, :], axis=1)


def direct_body(
    tokens,
    adapter_down_weight,
    adapter_up_weight,
    adapter_entry,
    adapter_of_request,
    token_blocks_per_request,
):
    wide_count = lax.axis_size("wide")
    blocks_dev = tokens.shape[0] // BLK
    local_width = tokens.shape[1]
    paired_ranks = adapter_down_weight.shape[3]
    rank_count = paired_ranks // 2
    slot_ids = block_tables(
        adapter_entry,
        adapter_of_request,
        token_blocks_per_request,
        blocks_dev * wide_count,
        token_blocks_per_request.shape[0],
        adapter_entry.shape[0],
    )
    needed_adapters = slot_ids.reshape(wide_count, blocks_dev).T
    down_outgoing = adapter_down_weight[needed_adapters]
    up_outgoing = adapter_up_weight[needed_adapters]
    got_down, got_up = (
        lax.all_to_all(down_outgoing, "wide", split_axis=1, concat_axis=3, tiled=True),
        lax.all_to_all(up_outgoing, "wide", split_axis=1, concat_axis=3, tiled=True),
    )
    got_down = got_down.reshape(blocks_dev, local_width, paired_ranks)
    block_rows = tokens.reshape(blocks_dev, BLK, local_width)
    shrink = jnp.einsum("btd,bdr->btr", block_rows, got_down, preferred_element_type=jnp.float32)
    low_rank = lax.psum(shrink, "narrow").astype(jnp.bfloat16)
    got_up = got_up.reshape(blocks_dev, -1, paired_ranks)
    delta_key = jnp.einsum(
        "btr,bjr->btj",
        low_rank[..., :rank_count],
        got_up[..., :rank_count],
        preferred_element_type=jnp.float32,
    )
    delta_value = jnp.einsum(
        "btr,bjr->btj",
        low_rank[..., rank_count:],
        got_up[..., rank_count:],
        preferred_element_type=jnp.float32,
    )
    out_cols = got_up.shape[1]
    key_delta = delta_key.reshape(blocks_dev * BLK, out_cols).astype(jnp.bfloat16)
    value_delta = delta_value.reshape(blocks_dev * BLK, out_cols).astype(jnp.bfloat16)
    return (key_delta, value_delta)


def swap(value, step):
    count = lax.axis_size("wide")
    return lax.ppermute(value, "wide", [(i, i ^ step) for i in range(count)])


def swap_cores(value):
    count = lax.axis_size("wide")
    pairs = [[i, i + 1] for i in range(0, count, 2)]
    return lax.all_to_all(value, "wide", 0, 0, axis_index_groups=pairs, tiled=True)


def pick(index, values):
    got = values[0]
    for i in range(1, len(values)):
        got = jnp.where(index == i, values[i], got)
    return got


def landed(out, sem):
    pltpu.make_async_copy(out, out, sem).wait()


def slices(tokens_ref, column, run, out, sem, first=0):
    return [
        pltpu.make_async_copy(
            tokens_ref.at[:, pl.ds(pl.multiple_of(((first + piece) * PLANE + column) * run, run), run)],
            out.at[piece],
            sem,
        )
        for piece in range(out.shape[0])
    ]


def choose_kernel(
    planes, entry_hbm, adapter_hbm, counts_hbm, tokens_ref, down_ref, up_ref, table_ref, *refs
):
    others = planes - 1
    sends, tokens_out = refs[:others], refs[others : others + 3]
    entry_ref, adapter_ref, counts_ref, held_ref, small_sem, tokens_sem, sem = refs[others + 3 :]
    me = lax.axis_index("wide")
    column, plane = lax.rem(me, PLANE), lax.div(me, PLANE)
    run, up_run = down_ref.shape[2], up_ref.shape[2]
    small = [
        pltpu.make_async_copy(entry_hbm, entry_ref, small_sem.at[0]),
        pltpu.make_async_copy(adapter_hbm, adapter_ref, small_sem.at[1]),
        pltpu.make_async_copy(counts_hbm, counts_ref, small_sem.at[2]),
    ]
    for copy in small:
        copy.start()
    for i, (k, first) in enumerate(((2, 0), (3, 0), (3, planes))):
        for copy in slices(tokens_ref, column ^ k, run, tokens_out[i], tokens_sem.at[i], first):
            copy.start()
    for copy in small:
        copy.wait()

    requests = counts_ref.shape[0]
    ends, total = [], 0
    for q in range(requests):
        total = total + counts_ref[q]
        ends.append(total)
    entries = [entry_ref[adapter_ref[q]] for q in range(requests)]

    def listed(p):
        ids = []
        for i in range(PLANE):
            block = p * PLANE + jnp.where(p % 2 == 0, i, PLANE - 1 - i)
            got = entries[0]
            for q in range(1, requests):
                got = jnp.where(ends[q - 1] <= block, entries[q], got)
            ids.append(got)
        place, held, count = [jnp.int32(0)], [ids[0]] * SLOTS, jnp.int32(1)
        for i in range(1, PLANE):
            found = count
            for j in range(i):
                found = jnp.where(ids[i] == ids[j], place[j], found)
            place.append(found)
            held = [jnp.where(found == s, ids[i], held[s]) for s in range(SLOTS)]
            count = jnp.maximum(count, found + 1)
        return held, place, count

    most = jnp.int32(1)
    for d in (*range(2, planes), 1, 0):
        held, place, count = listed(plane ^ d)
        most = jnp.maximum(most, count)
        if d > 0:
            for s in range(sends[d - 1].shape[0]):
                out = sends[d - 1].at[s]
                for ref, at in (down_ref, pl.ds(0, run)), (up_ref, pl.ds(run, up_run)):
                    pltpu.make_async_copy(ref.at[held[s]], out.at[:, at], sem.at[d - 1]).start()
        else:
            for s in range(SLOTS):
                held_ref[PLANE + s] = held[s]
    for k in range(PLANE):
        i = column ^ k
        held_ref[k] = pick(jnp.where(plane % 2 == 0, i, PLANE - 1 - i), place)
    held_ref[PLANE + SLOTS] = jnp.where(most > USUAL, 1, 0)
    table = pltpu.make_async_copy(held_ref, table_ref, small_sem.at[3])
    table.start()
    for k, out in enumerate(tokens_out):
        landed(out, tokens_sem.at[k])
    for d, out in enumerate(sends):
        landed(out, sem.at[d])
    table.wait()


def choose(planes, tokens, down, up, entry, adapter, counts):
    hbm = pl.BlockSpec(memory_space=pltpu.HBM)
    others = planes - 1
    rows = (2, down.shape[2] + up.shape[2], down.shape[3])
    sends = [
        jax.ShapeDtypeStruct((SLOTS if d == 1 else USUAL,) + rows, down.dtype) for d in range(1, planes)
    ]
    return pl.pallas_call(
        lambda *refs: choose_kernel(planes, *refs),
        out_shape=[jax.ShapeDtypeStruct((PLANE + SLOTS + 1,), jnp.int32)]
        + sends
        + [
            jax.ShapeDtypeStruct((count, BLK, down.shape[2]), tokens.dtype)
            for count in (2 * planes, planes, planes)
        ],
        in_specs=[hbm] * 6,
        out_specs=[pl.BlockSpec(memory_space=pl.ANY)]
        + [pl.BlockSpec(memory_space=pltpu.VMEM)] * (others + 3),
        scratch_shapes=[
            pltpu.SMEM(entry.shape, jnp.int32),
            pltpu.SMEM(adapter.shape, jnp.int32),
            pltpu.SMEM(counts.shape, jnp.int32),
            pltpu.SMEM((PLANE + SLOTS + 1,), jnp.int32),
            pltpu.SemaphoreType.DMA((4,)),
            pltpu.SemaphoreType.DMA((3,)),
            pltpu.SemaphoreType.DMA((others,)),
        ],
        compiler_params=pltpu.CompilerParams(vmem_limit_bytes=57 * 2**20),
        name="choose",
    )(entry, adapter, counts, tokens, down, up)


def gather_kernel(planes, table_ref, tokens_ref, down_ref, up_ref, own_ref, pair_ref, tokens_sem, sem):
    column = lax.rem(lax.axis_index("wide"), PLANE)
    run, up_run = down_ref.shape[2], up_ref.shape[2]
    for core in range(2):
        at = lax.div(column, 2) * 2 + core
        for copy in slices(tokens_ref, at, run, pair_ref.at[core], tokens_sem.at[core]):
            copy.start()
    for s in range(SLOTS):
        slot = table_ref[PLANE + s]
        for ref, rows in (down_ref, pl.ds(0, run)), (up_ref, pl.ds(run, up_run)):
            pltpu.make_async_copy(ref.at[slot], own_ref.at[s, :, rows], sem).start()
    for core in range(2):
        landed(pair_ref.at[core], tokens_sem.at[core])
    landed(own_ref, sem)


def gather(planes, table, tokens, down, up):
    run = down.shape[2]
    hbm = pl.BlockSpec(memory_space=pltpu.HBM)
    rows = (2, run + up.shape[2], down.shape[3])
    return pl.pallas_call(
        lambda *refs: gather_kernel(planes, *refs),
        out_shape=[
            jax.ShapeDtypeStruct((SLOTS,) + rows, down.dtype),
        ]
        + [jax.ShapeDtypeStruct((2, 2 * planes, BLK, run), tokens.dtype)],
        in_specs=[pl.BlockSpec(memory_space=pltpu.SMEM)] + [hbm] * 3,
        out_specs=[pl.BlockSpec(memory_space=pltpu.VMEM)] * 2,
        scratch_shapes=[
            pltpu.SemaphoreType.DMA((2,)),
            pltpu.SemaphoreType.DMA(()),
        ],
        compiler_params=pltpu.CompilerParams(vmem_limit_bytes=57 * 2**20),
        name="gather",
    )(table, tokens, down, up)


def up_rows(factors, distances, place):
    rows = []
    for d in distances:
        slot = jnp.minimum(place, factors[d].shape[0] - 1)
        rows += [factors[d][slot, half] for half in range(2)]
    return rows


def rows_of_block(row_refs, core, k, half, plane, planes):
    if k < 2:
        return row_refs[0][core ^ k, half * planes + plane]
    return row_refs[1][half * planes + plane] if k == 2 else row_refs[2 + half][plane]


def shrink(
    planes,
    slots,
    run,
    blocks,
    near,
    first,
    far,
    places,
    rows,
    factors,
    held=(),
    ups=None,
    flops=None,
    flag=False,
):
    vmem, smem = pl.BlockSpec(memory_space=pltpu.VMEM), pl.BlockSpec(memory_space=pltpu.SMEM)
    up_run, ranks = factors[0].shape[2] - run, factors[0].shape[3]

    used = sorted({*first, *far})

    def kernel(places_ref, *refs):
        spread = len(places.shape) > 1
        row_refs, refs = refs[: len(rows)], refs[len(rows) :]
        factor_refs, refs = dict(zip(used, refs)), refs[len(used) :]
        held_refs, outs = list(refs[: len(held)]), refs[len(held) :]
        me = lax.axis_index("wide")
        core, plane = lax.rem(me, 2), lax.div(me, PLANE)
        at = [places_ref[k, pl.ds(0, 1)] if spread else places_ref[k] for k in blocks]
        views = {d: ref.at[:, :, pl.ds(run, up_run)] for d, ref in factor_refs.items()}

        def rows_of_up(place):
            if not spread:
                return up_rows(views, ups or (), place)
            return [
                pick(place, [views[d][s, half].astype(jnp.float32) for s in range(slots)])
                for d in ups or ()
                for half in range(2)
            ]

        def rows_at(k, half, place):
            return rows_of_block(row_refs, core, k, half, place, planes)

        def sums_of(chosen, distances):
            total = jnp.zeros((len(chosen) * BLK, slots * ranks), jnp.float32)
            for d in distances:
                for half in range(2):
                    total += jnp.dot(
                        jnp.concatenate([rows_at(blocks[i], half, plane ^ d) for i in chosen], axis=0),
                        jnp.concatenate(
                            [factor_refs[d][s, half, pl.ds(0, run)] for s in range(slots)], axis=1
                        ),
                        preferred_element_type=jnp.float32,
                    )
            parts = [total[j * BLK : (j + 1) * BLK] for j in range(len(chosen))]
            return {
                i: pick(at[i], [part[:, s * ranks : (s + 1) * ranks] for s in range(slots)])
                for i, part in zip(chosen, parts)
            }

        if flag:
            *outs, spread_ref, flag_ref = outs
            flag_ref[0] = places_ref[PLANE + SLOTS]
            for k in range(PLANE):
                spread_ref[k] = jnp.full(spread_ref.shape[1:], places_ref[k], jnp.int32)
        every = range(len(blocks))
        mine = sums_of(every, far) if far else {}
        here = [i for i in every if blocks[i] in near]
        for i, part in (sums_of(here, first) if here else {}).items():
            mine[i] = mine[i] + part if far else part
        for i in every:
            if i not in here:
                mine[i] = mine[i] + held_refs.pop(0)[...]
            outs[i][pl.ds(0, BLK)] = mine[i].astype(outs[i].dtype)
            for j, part in enumerate(rows_of_up(at[i])):
                outs[i][pl.ds(BLK + j * up_run, up_run)] = part.astype(outs[i].dtype)

    height = BLK + len(ups or ()) * 2 * up_run
    exact = [ups is None or k == 0 for k in blocks]
    cost = None
    if flops is not None:
        cost = pl.CostEstimate(flops=flops, bytes_accessed=0, transcendentals=0)
    return pl.pallas_call(
        kernel,
        out_shape=[
            jax.ShapeDtypeStruct((height, ranks), jnp.float32 if full else rows[0].dtype)
            for full in exact
        ]
        + [jax.ShapeDtypeStruct((PLANE, 8, ranks), jnp.int32), jax.ShapeDtypeStruct((1,), jnp.int32)]
        * flag,
        in_specs=[vmem if len(places.shape) > 1 else smem]
        + [vmem] * (len(rows) + len(used) + len(held)),
        out_specs=[vmem] * len(blocks) + [vmem, smem] * flag,
        compiler_params=pltpu.CompilerParams(vmem_limit_bytes=10 * 2**20),
        cost_estimate=cost,
        name="shrink",
    )(places, *rows, *[factors[d] for d in used], *held)


def amend(planes, run, places, rows, thirds, slots, sums, kept):
    vmem = pl.BlockSpec(memory_space=pltpu.VMEM)
    up_run, ranks = thirds[0].shape[2] - run, thirds[0].shape[3]

    def kernel(places_ref, *refs):
        row_refs, refs = refs[: len(rows)], refs[len(rows) :]
        third_refs, refs = refs[:planes], refs[planes:]
        sum_refs, outs = refs[:PLANE], refs[PLANE + len(kept) :]
        me = lax.axis_index("wide")
        core, plane = lax.rem(me, 2), lax.div(me, PLANE)
        total = jnp.zeros((PLANE * BLK, ranks), jnp.float32)
        for d in range(planes):
            for half in range(2):
                parts = [
                    rows_of_block(row_refs, core, k, half, plane ^ d, planes) for k in range(PLANE)
                ]
                total += jnp.dot(
                    jnp.concatenate(parts, axis=0),
                    third_refs[d][slots[d], half, pl.ds(0, run)],
                    preferred_element_type=jnp.float32,
                )
        for k in range(PLANE):
            anew = places_ref[k, pl.ds(0, 1)] == USUAL
            news = [(0, total[k * BLK : (k + 1) * BLK])]
            for d in range(planes):
                for half in range(2):
                    start = BLK + (2 * d + half) * up_run
                    news.append((start, third_refs[d][slots[d], half, pl.ds(run, up_run)]))
            for start, new in news:
                at = pl.ds(start, new.shape[0])
                old = sum_refs[k][at].astype(jnp.float32)
                outs[k][at] = jnp.where(anew, new.astype(jnp.float32), old).astype(outs[k].dtype)

    return pl.pallas_call(
        kernel,
        out_shape=[jax.ShapeDtypeStruct(value.shape, value.dtype) for value in sums],
        in_specs=[vmem] * (1 + len(rows) + planes + PLANE)
        + [pl.BlockSpec(memory_space=pl.ANY)] * len(kept),
        out_specs=[vmem] * PLANE,
        compiler_params=pltpu.CompilerParams(vmem_limit_bytes=10 * 2**20),
        name="amend",
    )(places, *rows, *thirds, *sums, *kept)


def expand(planes, up_run, sums):
    ranks = sums[0].shape[1]
    columns = 2 * planes * PLANE * up_run
    vmem = pl.BlockSpec(memory_space=pltpu.VMEM)
    span = 2 * up_run
    order = (2, 3, 1, 0)

    def kernel(*refs):
        sum_refs = dict(zip(order, refs))
        key_ref, value_ref, factor = refs[PLANE:]
        me = lax.axis_index("wide")
        column, plane = lax.rem(me, PLANE), lax.div(me, PLANE)
        total = jnp.zeros((BLK, ranks), jnp.float32)
        for k in range(PLANE):
            total += sum_refs[k][pl.ds(0, BLK)].astype(jnp.float32)
            for d in range(planes):
                rows = sum_refs[k][pl.ds(BLK + d * span, span)]
                factor[plane ^ d, :, column ^ k] = rows.astype(factor.dtype).reshape(2, up_run, ranks)
        low_rank = total.astype(jnp.bfloat16)
        is_key = lax.broadcasted_iota(jnp.int32, low_rank.shape, 1) < ranks // 2
        zero = jnp.zeros_like(low_rank)
        both = jnp.concatenate(
            [jnp.where(is_key, low_rank, zero), jnp.where(is_key, zero, low_rank)], axis=0
        )
        for half in range(2):
            for p in range(planes):
                delta = lax.dot_general(
                    both,
                    factor[p, half].reshape(PLANE * up_run, ranks),
                    (((1,), (1,)), ((), ())),
                    preferred_element_type=jnp.float32,
                ).astype(jnp.bfloat16)
                at = pl.ds((half * planes + p) * PLANE * up_run, PLANE * up_run)
                key_ref[:, at] = delta[:BLK]
                value_ref[:, at] = delta[BLK:]

    return pl.pallas_call(
        kernel,
        out_shape=[jax.ShapeDtypeStruct((BLK, columns), jnp.bfloat16)] * 2,
        in_specs=[vmem] * PLANE,
        out_specs=[vmem] * 2,
        scratch_shapes=[pltpu.VMEM((planes, 2, PLANE, up_run, ranks), jnp.bfloat16)],
        compiler_params=pltpu.CompilerParams(vmem_limit_bytes=4 * 2**20),
        name="expand",
    )(*[sums[k] for k in order])


def plane_body(
    tokens,
    adapter_down_weight,
    adapter_up_weight,
    adapter_entry,
    adapter_of_request,
    token_blocks_per_request,
):
    planes = lax.axis_size("wide") // PLANE
    places, *sends = choose(
        planes,
        tokens,
        adapter_down_weight,
        adapter_up_weight,
        adapter_entry,
        adapter_of_request,
        token_blocks_per_request,
    )
    factors, across = sends[: planes - 1], sends[planes - 1 :]
    own_factors, pair = gather(planes, places, tokens, adapter_down_weight, adapter_up_weight)
    sends = sends + [pair]
    run, up_run = adapter_down_weight.shape[2], adapter_up_weight.shape[2]
    whole, blocks = tuple(range(planes)), tuple(range(PLANE))
    factors = [own_factors] + [swap(factors[d - 1], d * PLANE) for d in whole[1:]]
    rows = [swap_cores(pair)] + [swap(value, k) for value, k in zip(across, (2, 3, 3))]
    early = (0, 2)
    *held, spread, many = shrink(
        planes,
        USUAL,
        run,
        blocks[:2],
        blocks[:2],
        early,
        (),
        places,
        rows[:1],
        factors,
        flops=None,
        flag=True,
    )

    def finish(sums):
        sums = [sums[0]] + [swap(sums[k], k) for k in range(1, PLANE)]
        return tuple(expand(planes, up_run, sums))

    def sums_of(spread, factors, rows, held):
        args = (early, (1, 3), spread, rows, factors)
        sums = shrink(planes, USUAL, run, blocks[1:], blocks[2:], *args, held[1:], whole)
        return [*shrink(planes, USUAL, run, blocks[:1], (), *args, held[:1], whole), *sums]

    def usual(spread, factors, rows, held, kept):
        return finish(sums_of(spread, factors, rows, held))

    def more(spread, factors, rows, held, kept):
        thirds = factors[:2] + [swap(factors[d ^ 1][:1], PLANE) for d in whole[2:]]
        slots = [USUAL if d < 2 else 0 for d in whole]
        sums = sums_of(spread, factors, rows, held)
        return finish(amend(planes, run, spread, rows, thirds, slots, sums, kept))

    return lax.switch(many[0], [usual, more], spread, factors, rows, held, sends)


def solution(mesh):
    by_plane = mesh.shape["wide"] == 16 and mesh.shape["narrow"] == 1
    return jax.shard_map(
        plane_body if by_plane else direct_body,
        mesh=mesh,
        in_specs=(
            P(("groups", "wide"), "narrow"),
            P(None, "narrow", "wide", None),
            P(None, "narrow", "wide", None),
            P(),
            P("groups"),
            P("groups"),
        ),
        out_specs=(P(("groups", "wide"), "narrow"), P(("groups", "wide"), "narrow")),
        check_vma=False,
    )
```

```python
import jax
import jax.numpy as jnp
from jax import lax
from jax.experimental import pallas as pl
from jax.experimental.pallas import tpu as pltpu
from jax.sharding import PartitionSpec as P

BLK = 128
PLANE = 4
SLOTS = 3
USUAL = 2


def block_tables(
    adapter_entry,
    adapter_of_request,
    token_blocks_per_request,
    block_count,
    request_count,
    adapter_count,
):
    request_ends = jnp.cumsum(token_blocks_per_request)
    block_index = jnp.arange(block_count, dtype=jnp.int32)
    request = jnp.sum((request_ends[None, :] <= block_index[:, None]).astype(jnp.int32), axis=1)
    pick_table = (request[:, None] == jnp.arange(request_count, dtype=jnp.int32)[None, :]).astype(
        jnp.int32
    )
    adapter = jnp.sum(pick_table * adapter_of_request[None, :], axis=1)
    slot_table = (adapter[:, None] == jnp.arange(adapter_count, dtype=jnp.int32)[None, :]).astype(
        jnp.int32
    )
    return jnp.sum(slot_table * adapter_entry[None, :], axis=1)


def direct_body(
    tokens,
    adapter_down_weight,
    adapter_up_weight,
    adapter_entry,
    adapter_of_request,
    token_blocks_per_request,
):
    wide_count = lax.axis_size("wide")
    blocks_dev = tokens.shape[0] // BLK
    local_width = tokens.shape[1]
    paired_ranks = adapter_down_weight.shape[3]
    rank_count = paired_ranks // 2
    slot_ids = block_tables(
        adapter_entry,
        adapter_of_request,
        token_blocks_per_request,
        blocks_dev * wide_count,
        token_blocks_per_request.shape[0],
        adapter_entry.shape[0],
    )
    needed_adapters = slot_ids.reshape(wide_count, blocks_dev).T
    down_outgoing = adapter_down_weight[needed_adapters]
    up_outgoing = adapter_up_weight[needed_adapters]
    got_down, got_up = (
        lax.all_to_all(down_outgoing, "wide", split_axis=1, concat_axis=3, tiled=True),
        lax.all_to_all(up_outgoing, "wide", split_axis=1, concat_axis=3, tiled=True),
    )
    got_down = got_down.reshape(blocks_dev, local_width, paired_ranks)
    block_rows = tokens.reshape(blocks_dev, BLK, local_width)
    shrink = jnp.einsum("btd,bdr->btr", block_rows, got_down, preferred_element_type=jnp.float32)
    low_rank = lax.psum(shrink, "narrow").astype(jnp.bfloat16)
    got_up = got_up.reshape(blocks_dev, -1, paired_ranks)
    delta_key = jnp.einsum(
        "btr,bjr->btj",
        low_rank[..., :rank_count],
        got_up[..., :rank_count],
        preferred_element_type=jnp.float32,
    )
    delta_value = jnp.einsum(
        "btr,bjr->btj",
        low_rank[..., rank_count:],
        got_up[..., rank_count:],
        preferred_element_type=jnp.float32,
    )
    out_cols = got_up.shape[1]
    key_delta = delta_key.reshape(blocks_dev * BLK, out_cols).astype(jnp.bfloat16)
    value_delta = delta_value.reshape(blocks_dev * BLK, out_cols).astype(jnp.bfloat16)
    return (key_delta, value_delta)


def swap(value, step):
    count = lax.axis_size("wide")
    return lax.ppermute(value, "wide", [(i, i ^ step) for i in range(count)])


def swap_cores(value):
    count = lax.axis_size("wide")
    pairs = [[i, i + 1] for i in range(0, count, 2)]
    return lax.all_to_all(value, "wide", 0, 0, axis_index_groups=pairs, tiled=True)


def pick(index, values):
    got = values[0]
    for i in range(1, len(values)):
        got = jnp.where(index == i, values[i], got)
    return got


def landed(out, sem):
    pltpu.make_async_copy(out, out, sem).wait()


def slices(tokens_ref, column, run, out, sem, first=0):
    return [
        pltpu.make_async_copy(
            tokens_ref.at[:, pl.ds(pl.multiple_of(((first + piece) * PLANE + column) * run, run), run)],
            out.at[piece],
            sem,
        )
        for piece in range(out.shape[0])
    ]


def choose_kernel(
    planes, entry_hbm, adapter_hbm, counts_hbm, tokens_ref, down_ref, up_ref, table_ref, *refs
):
    others = planes - 1
    sends, tokens_out = refs[:others], refs[others : others + 3]
    entry_ref, adapter_ref, counts_ref, held_ref, small_sem, tokens_sem, sem = refs[others + 3 :]
    me = lax.axis_index("wide")
    column, plane = lax.rem(me, PLANE), lax.div(me, PLANE)
    run, up_run = down_ref.shape[2], up_ref.shape[2]
    small = [
        pltpu.make_async_copy(entry_hbm, entry_ref, small_sem.at[0]),
        pltpu.make_async_copy(adapter_hbm, adapter_ref, small_sem.at[1]),
        pltpu.make_async_copy(counts_hbm, counts_ref, small_sem.at[2]),
    ]
    for copy in small:
        copy.start()
    for i, (k, first) in enumerate(((2, 0), (3, 0), (3, planes))):
        for copy in slices(tokens_ref, column ^ k, run, tokens_out[i], tokens_sem.at[i], first):
            copy.start()
    for copy in small:
        copy.wait()

    requests = counts_ref.shape[0]
    ends, total = [], 0
    for q in range(requests):
        total = total + counts_ref[q]
        ends.append(total)
    entries = [entry_ref[adapter_ref[q]] for q in range(requests)]

    def listed(p):
        ids = []
        for i in range(PLANE):
            block = p * PLANE + jnp.where(p % 2 == 0, i, PLANE - 1 - i)
            got = entries[0]
            for q in range(1, requests):
                got = jnp.where(ends[q - 1] <= block, entries[q], got)
            ids.append(got)
        place, held, count = [jnp.int32(0)], [ids[0]] * SLOTS, jnp.int32(1)
        for i in range(1, PLANE):
            found = count
            for j in range(i):
                found = jnp.where(ids[i] == ids[j], place[j], found)
            place.append(found)
            held = [jnp.where(found == s, ids[i], held[s]) for s in range(SLOTS)]
            count = jnp.maximum(count, found + 1)
        return held, place, count

    most = jnp.int32(1)
    for d in (*range(2, planes), 1, 0):
        held, place, count = listed(plane ^ d)
        most = jnp.maximum(most, count)
        if d > 0:
            for s in range(sends[d - 1].shape[0]):
                out = sends[d - 1].at[s]
                for ref, at in (down_ref, pl.ds(0, run)), (up_ref, pl.ds(run, up_run)):
                    pltpu.make_async_copy(ref.at[held[s]], out.at[:, at], sem.at[d - 1]).start()
        else:
            for s in range(SLOTS):
                held_ref[PLANE + s] = held[s]
    for k in range(PLANE):
        i = column ^ k
        held_ref[k] = pick(jnp.where(plane % 2 == 0, i, PLANE - 1 - i), place)
    held_ref[PLANE + SLOTS] = jnp.where(most > USUAL, 1, 0)
    table = pltpu.make_async_copy(held_ref, table_ref, small_sem.at[3])
    table.start()
    for k, out in enumerate(tokens_out):
        landed(out, tokens_sem.at[k])
    for d, out in enumerate(sends):
        landed(out, sem.at[d])
    table.wait()


def choose(planes, tokens, down, up, entry, adapter, counts):
    hbm = pl.BlockSpec(memory_space=pltpu.HBM)
    others = planes - 1
    rows = (2, down.shape[2] + up.shape[2], down.shape[3])
    sends = [
        jax.ShapeDtypeStruct((SLOTS if d == 1 else USUAL,) + rows, down.dtype) for d in range(1, planes)
    ]
    return pl.pallas_call(
        lambda *refs: choose_kernel(planes, *refs),
        out_shape=[jax.ShapeDtypeStruct((PLANE + SLOTS + 1,), jnp.int32)]
        + sends
        + [
            jax.ShapeDtypeStruct((count, BLK, down.shape[2]), tokens.dtype)
            for count in (2 * planes, planes, planes)
        ],
        in_specs=[hbm] * 6,
        out_specs=[pl.BlockSpec(memory_space=pl.ANY)]
        + [pl.BlockSpec(memory_space=pltpu.VMEM)] * (others + 3),
        scratch_shapes=[
            pltpu.SMEM(entry.shape, jnp.int32),
            pltpu.SMEM(adapter.shape, jnp.int32),
            pltpu.SMEM(counts.shape, jnp.int32),
            pltpu.SMEM((PLANE + SLOTS + 1,), jnp.int32),
            pltpu.SemaphoreType.DMA((4,)),
            pltpu.SemaphoreType.DMA((3,)),
            pltpu.SemaphoreType.DMA((others,)),
        ],
        compiler_params=pltpu.CompilerParams(vmem_limit_bytes=57 * 2**20),
        name="choose",
    )(entry, adapter, counts, tokens, down, up)


def gather_kernel(planes, table_ref, tokens_ref, down_ref, up_ref, own_ref, pair_ref, tokens_sem, sem):
    column = lax.rem(lax.axis_index("wide"), PLANE)
    run, up_run = down_ref.shape[2], up_ref.shape[2]
    for core in range(2):
        at = lax.div(column, 2) * 2 + core
        for copy in slices(tokens_ref, at, run, pair_ref.at[core], tokens_sem.at[core]):
            copy.start()
    for s in range(SLOTS):
        slot = table_ref[PLANE + s]
        for ref, rows in (down_ref, pl.ds(0, run)), (up_ref, pl.ds(run, up_run)):
            pltpu.make_async_copy(ref.at[slot], own_ref.at[s, :, rows], sem).start()
    for core in range(2):
        landed(pair_ref.at[core], tokens_sem.at[core])
    landed(own_ref, sem)


def gather(planes, table, tokens, down, up):
    run = down.shape[2]
    hbm = pl.BlockSpec(memory_space=pltpu.HBM)
    rows = (2, run + up.shape[2], down.shape[3])
    return pl.pallas_call(
        lambda *refs: gather_kernel(planes, *refs),
        out_shape=[
            jax.ShapeDtypeStruct((SLOTS,) + rows, down.dtype),
        ]
        + [jax.ShapeDtypeStruct((2, 2 * planes, BLK, run), tokens.dtype)],
        in_specs=[pl.BlockSpec(memory_space=pltpu.SMEM)] + [hbm] * 3,
        out_specs=[pl.BlockSpec(memory_space=pltpu.VMEM)] * 2,
        scratch_shapes=[
            pltpu.SemaphoreType.DMA((2,)),
            pltpu.SemaphoreType.DMA(()),
        ],
        compiler_params=pltpu.CompilerParams(vmem_limit_bytes=57 * 2**20),
        name="gather",
    )(table, tokens, down, up)


def up_rows(factors, distances, place):
    rows = []
    for d in distances:
        slot = jnp.minimum(place, factors[d].shape[0] - 1)
        rows += [factors[d][slot, half] for half in range(2)]
    return rows


def rows_of_block(row_refs, core, k, half, plane, planes):
    if k < 2:
        return row_refs[0][core ^ k, half * planes + plane]
    return row_refs[1][half * planes + plane] if k == 2 else row_refs[2 + half][plane]


def shrink(
    planes,
    slots,
    run,
    blocks,
    near,
    first,
    far,
    places,
    rows,
    factors,
    held=(),
    ups=None,
    flops=None,
    flag=False,
):
    vmem, smem = pl.BlockSpec(memory_space=pltpu.VMEM), pl.BlockSpec(memory_space=pltpu.SMEM)
    up_run, ranks = factors[0].shape[2] - run, factors[0].shape[3]

    used = sorted({*first, *far})

    def kernel(places_ref, *refs):
        spread = len(places.shape) > 1
        row_refs, refs = refs[: len(rows)], refs[len(rows) :]
        factor_refs, refs = dict(zip(used, refs)), refs[len(used) :]
        held_refs, outs = list(refs[: len(held)]), refs[len(held) :]
        me = lax.axis_index("wide")
        core, plane = lax.rem(me, 2), lax.div(me, PLANE)
        at = [places_ref[k, pl.ds(0, 1)] if spread else places_ref[k] for k in blocks]
        views = {d: ref.at[:, :, pl.ds(run, up_run)] for d, ref in factor_refs.items()}

        def rows_of_up(place):
            if not spread:
                return up_rows(views, ups or (), place)
            return [
                pick(place, [views[d][s, half].astype(jnp.float32) for s in range(slots)])
                for d in ups or ()
                for half in range(2)
            ]

        def rows_at(k, half, place):
            return rows_of_block(row_refs, core, k, half, place, planes)

        def sums_of(chosen, distances):
            total = jnp.zeros((len(chosen) * BLK, slots * ranks), jnp.float32)
            for d in distances:
                for half in range(2):
                    total += jnp.dot(
                        jnp.concatenate([rows_at(blocks[i], half, plane ^ d) for i in chosen], axis=0),
                        jnp.concatenate(
                            [factor_refs[d][s, half, pl.ds(0, run)] for s in range(slots)], axis=1
                        ),
                        preferred_element_type=jnp.float32,
                    )
            parts = [total[j * BLK : (j + 1) * BLK] for j in range(len(chosen))]
            return {
                i: pick(at[i], [part[:, s * ranks : (s + 1) * ranks] for s in range(slots)])
                for i, part in zip(chosen, parts)
            }

        if flag:
            *outs, spread_ref, flag_ref = outs
            flag_ref[0] = places_ref[PLANE + SLOTS]
            for k in range(PLANE):
                spread_ref[k] = jnp.full(spread_ref.shape[1:], places_ref[k], jnp.int32)
        every = range(len(blocks))
        mine = sums_of(every, far) if far else {}
        here = [i for i in every if blocks[i] in near]
        for i, part in (sums_of(here, first) if here else {}).items():
            mine[i] = mine[i] + part if far else part
        for i in every:
            if i not in here:
                mine[i] = mine[i] + held_refs.pop(0)[...]
            outs[i][pl.ds(0, BLK)] = mine[i].astype(outs[i].dtype)
            for j, part in enumerate(rows_of_up(at[i])):
                outs[i][pl.ds(BLK + j * up_run, up_run)] = part.astype(outs[i].dtype)

    height = BLK + len(ups or ()) * 2 * up_run
    exact = [ups is None or k == 0 for k in blocks]
    cost = None
    if flops is not None:
        cost = pl.CostEstimate(flops=flops, bytes_accessed=0, transcendentals=0)
    return pl.pallas_call(
        kernel,
        out_shape=[
            jax.ShapeDtypeStruct((height, ranks), jnp.float32 if full else rows[0].dtype)
            for full in exact
        ]
        + [jax.ShapeDtypeStruct((PLANE, 8, ranks), jnp.int32), jax.ShapeDtypeStruct((1,), jnp.int32)]
        * flag,
        in_specs=[vmem if len(places.shape) > 1 else smem]
        + [vmem] * (len(rows) + len(used) + len(held)),
        out_specs=[vmem] * len(blocks) + [vmem, smem] * flag,
        compiler_params=pltpu.CompilerParams(vmem_limit_bytes=10 * 2**20),
        cost_estimate=cost,
        name="shrink",
    )(places, *rows, *[factors[d] for d in used], *held)


def third_sums(planes, run, distances, row_refs, third_refs, slots):
    me = lax.axis_index("wide")
    core, plane = lax.rem(me, 2), lax.div(me, PLANE)
    total = jnp.zeros((PLANE * BLK, third_refs[0].shape[3]), jnp.float32)
    for d, ref, slot in zip(distances, third_refs, slots):
        for half in range(2):
            parts = [rows_of_block(row_refs, core, k, half, plane ^ d, planes) for k in range(PLANE)]
            total += jnp.dot(
                jnp.concatenate(parts, axis=0),
                ref[slot, half, pl.ds(0, run)],
                preferred_element_type=jnp.float32,
            )
    return total


def amend_near(planes, run, rows, thirds, slots, kept):
    vmem = pl.BlockSpec(memory_space=pltpu.VMEM)

    def kernel(*refs):
        row_refs, third_refs, out = refs[: len(rows)], refs[len(rows) : len(rows) + len(thirds)], refs[-1]
        out[...] = third_sums(planes, run, range(len(thirds)), row_refs, third_refs, slots)

    return pl.pallas_call(
        kernel,
        out_shape=jax.ShapeDtypeStruct((PLANE * BLK, thirds[0].shape[3]), jnp.float32),
        in_specs=[vmem] * (len(rows) + len(thirds))
        + [pl.BlockSpec(memory_space=pl.ANY)] * len(kept),
        out_specs=vmem,
        compiler_params=pltpu.CompilerParams(vmem_limit_bytes=10 * 2**20),
        name="amend_near",
    )(*rows, *thirds, *kept)


def amend(planes, run, places, rows, thirds, slots, near, sums, kept):
    vmem = pl.BlockSpec(memory_space=pltpu.VMEM)
    up_run, ranks = thirds[0].shape[2] - run, thirds[0].shape[3]

    def kernel(places_ref, near_ref, *refs):
        row_refs, refs = refs[: len(rows)], refs[len(rows) :]
        third_refs, refs = refs[:planes], refs[planes:]
        sum_refs, outs = refs[:PLANE], refs[PLANE + len(kept) :]
        far = range(2, planes)
        total = third_sums(planes, run, far, row_refs, third_refs[2:], slots[2:]) + near_ref[...]
        for k in range(PLANE):
            anew = places_ref[k, pl.ds(0, 1)] == USUAL
            news = [(0, total[k * BLK : (k + 1) * BLK])]
            for d in range(planes):
                for half in range(2):
                    start = BLK + (2 * d + half) * up_run
                    news.append((start, third_refs[d][slots[d], half, pl.ds(run, up_run)]))
            for start, new in news:
                at = pl.ds(start, new.shape[0])
                old = sum_refs[k][at].astype(jnp.float32)
                outs[k][at] = jnp.where(anew, new.astype(jnp.float32), old).astype(outs[k].dtype)

    return pl.pallas_call(
        kernel,
        out_shape=[jax.ShapeDtypeStruct(value.shape, value.dtype) for value in sums],
        in_specs=[vmem] * (2 + len(rows) + planes + PLANE)
        + [pl.BlockSpec(memory_space=pl.ANY)] * len(kept),
        out_specs=[vmem] * PLANE,
        compiler_params=pltpu.CompilerParams(vmem_limit_bytes=10 * 2**20),
        name="amend",
    )(places, near, *rows, *thirds, *sums, *kept)


def expand(planes, up_run, sums):
    ranks = sums[0].shape[1]
    columns = 2 * planes * PLANE * up_run
    vmem = pl.BlockSpec(memory_space=pltpu.VMEM)
    span = 2 * up_run
    order = (2, 3, 1, 0)

    def kernel(*refs):
        sum_refs = dict(zip(order, refs))
        key_out, value_out, factor, key_ref, value_ref, sem = refs[PLANE:]
        me = lax.axis_index("wide")
        column, plane = lax.rem(me, PLANE), lax.div(me, PLANE)
        total = jnp.zeros((BLK, ranks), jnp.float32)
        for k in range(PLANE):
            total += sum_refs[k][pl.ds(0, BLK)].astype(jnp.float32)
            for d in range(planes):
                rows = sum_refs[k][pl.ds(BLK + d * span, span)]
                factor[plane ^ d, :, column ^ k] = rows.astype(factor.dtype).reshape(2, up_run, ranks)
        low_rank = total.astype(jnp.bfloat16)
        is_key = lax.broadcasted_iota(jnp.int32, low_rank.shape, 1) < ranks // 2
        zero = jnp.zeros_like(low_rank)
        both = jnp.concatenate(
            [jnp.where(is_key, low_rank, zero), jnp.where(is_key, zero, low_rank)], axis=0
        )
        copies = []
        for half in range(2):
            for p in range(planes):
                delta = lax.dot_general(
                    both,
                    factor[p, half].reshape(PLANE * up_run, ranks),
                    (((1,), (1,)), ((), ())),
                    preferred_element_type=jnp.float32,
                ).astype(jnp.bfloat16)
                at = pl.ds((half * planes + p) * PLANE * up_run, PLANE * up_run)
                key_ref[:, at] = delta[:BLK]
                value_ref[:, at] = delta[BLK:]
            at = pl.ds(half * (columns // 2), columns // 2)
            for i, (held, out) in enumerate(((key_ref, key_out), (value_ref, value_out))):
                copies.append(pltpu.make_async_copy(held.at[:, at], out.at[:, at], sem.at[half, i]))
                copies[-1].start()
        for copy in copies:
            copy.wait()

    return pl.pallas_call(
        kernel,
        out_shape=[jax.ShapeDtypeStruct((BLK, columns), jnp.bfloat16)] * 2,
        in_specs=[vmem] * PLANE,
        out_specs=[pl.BlockSpec(memory_space=pl.ANY)] * 2,
        scratch_shapes=[
            pltpu.VMEM((planes, 2, PLANE, up_run, ranks), jnp.bfloat16),
            pltpu.VMEM((BLK, columns), jnp.bfloat16),
            pltpu.VMEM((BLK, columns), jnp.bfloat16),
            pltpu.SemaphoreType.DMA((2, 2)),
        ],
        compiler_params=pltpu.CompilerParams(vmem_limit_bytes=4 * 2**20),
        name="expand",
    )(*[sums[k] for k in order])


def plane_body(
    tokens,
    adapter_down_weight,
    adapter_up_weight,
    adapter_entry,
    adapter_of_request,
    token_blocks_per_request,
):
    planes = lax.axis_size("wide") // PLANE
    places, *sends = choose(
        planes,
        tokens,
        adapter_down_weight,
        adapter_up_weight,
        adapter_entry,
        adapter_of_request,
        token_blocks_per_request,
    )
    factors, across = sends[: planes - 1], sends[planes - 1 :]
    own_factors, pair = gather(planes, places, tokens, adapter_down_weight, adapter_up_weight)
    sends = sends + [pair]
    run, up_run = adapter_down_weight.shape[2], adapter_up_weight.shape[2]
    whole, blocks = tuple(range(planes)), tuple(range(PLANE))
    factors = [own_factors] + [swap(factors[d - 1], d * PLANE) for d in whole[1:]]
    rows = [swap_cores(pair)] + [swap(value, k) for value, k in zip(across, (2, 3, 3))]
    early = (0, 2)
    *held, spread, many = shrink(
        planes,
        USUAL,
        run,
        blocks[:2],
        blocks[:2],
        early,
        (),
        places,
        rows[:1],
        factors,
        flops=None,
        flag=True,
    )

    def finish(sums):
        sums = [sums[0]] + [swap(sums[k], k) for k in range(1, PLANE)]
        return tuple(expand(planes, up_run, sums))

    def sums_of(spread, factors, rows, held):
        args = (early, (1, 3), spread, rows, factors)
        sums = shrink(planes, USUAL, run, blocks[1:], blocks[2:], *args, held[1:], whole)
        return [*shrink(planes, USUAL, run, blocks[:1], (), *args, held[:1], whole), *sums]

    def usual(spread, factors, rows, held, kept):
        return finish(sums_of(spread, factors, rows, held))

    def more(spread, factors, rows, held, kept):
        thirds = factors[:2] + [swap(factors[d ^ 1][:1], PLANE) for d in whole[2:]]
        slots = [USUAL if d < 2 else 0 for d in whole]
        sums = sums_of(spread, factors, rows, held)
        near = amend_near(planes, run, rows, thirds[:2], slots[:2], kept)
        return finish(amend(planes, run, spread, rows, thirds, slots, near, sums, kept))

    return lax.switch(many[0], [usual, more], spread, factors, rows, held, sends)


def solution(mesh):
    by_plane = mesh.shape["wide"] == 16 and mesh.shape["narrow"] == 1
    return jax.shard_map(
        plane_body if by_plane else direct_body,
        mesh=mesh,
        in_specs=(
            P(("groups", "wide"), "narrow"),
            P(None, "narrow", "wide", None),
            P(None, "narrow", "wide", None),
            P(),
            P("groups"),
            P("groups"),
        ),
        out_specs=(P(("groups", "wide"), "narrow"), P(("groups", "wide"), "narrow")),
        check_vma=False,
    )
```

```python
import jax
import jax.numpy as jnp
from jax import lax
from jax.experimental import pallas as pl
from jax.experimental.pallas import tpu as pltpu
from jax.sharding import PartitionSpec as P

BLK = 128
PLANE = 4
SLOTS = 3
USUAL = 2


def block_tables(
    adapter_entry,
    adapter_of_request,
    token_blocks_per_request,
    block_count,
    request_count,
    adapter_count,
):
    request_ends = jnp.cumsum(token_blocks_per_request)
    block_index = jnp.arange(block_count, dtype=jnp.int32)
    request = jnp.sum((request_ends[None, :] <= block_index[:, None]).astype(jnp.int32), axis=1)
    pick_table = (request[:, None] == jnp.arange(request_count, dtype=jnp.int32)[None, :]).astype(
        jnp.int32
    )
    adapter = jnp.sum(pick_table * adapter_of_request[None, :], axis=1)
    slot_table = (adapter[:, None] == jnp.arange(adapter_count, dtype=jnp.int32)[None, :]).astype(
        jnp.int32
    )
    return jnp.sum(slot_table * adapter_entry[None, :], axis=1)


def direct_body(
    tokens,
    adapter_down_weight,
    adapter_up_weight,
    adapter_entry,
    adapter_of_request,
    token_blocks_per_request,
):
    wide_count = lax.axis_size("wide")
    blocks_dev = tokens.shape[0] // BLK
    local_width = tokens.shape[1]
    paired_ranks = adapter_down_weight.shape[3]
    rank_count = paired_ranks // 2
    slot_ids = block_tables(
        adapter_entry,
        adapter_of_request,
        token_blocks_per_request,
        blocks_dev * wide_count,
        token_blocks_per_request.shape[0],
        adapter_entry.shape[0],
    )
    needed_adapters = slot_ids.reshape(wide_count, blocks_dev).T
    down_outgoing = adapter_down_weight[needed_adapters]
    up_outgoing = adapter_up_weight[needed_adapters]
    got_down, got_up = (
        lax.all_to_all(down_outgoing, "wide", split_axis=1, concat_axis=3, tiled=True),
        lax.all_to_all(up_outgoing, "wide", split_axis=1, concat_axis=3, tiled=True),
    )
    got_down = got_down.reshape(blocks_dev, local_width, paired_ranks)
    block_rows = tokens.reshape(blocks_dev, BLK, local_width)
    shrink = jnp.einsum("btd,bdr->btr", block_rows, got_down, preferred_element_type=jnp.float32)
    low_rank = lax.psum(shrink, "narrow").astype(jnp.bfloat16)
    got_up = got_up.reshape(blocks_dev, -1, paired_ranks)
    delta_key = jnp.einsum(
        "btr,bjr->btj",
        low_rank[..., :rank_count],
        got_up[..., :rank_count],
        preferred_element_type=jnp.float32,
    )
    delta_value = jnp.einsum(
        "btr,bjr->btj",
        low_rank[..., rank_count:],
        got_up[..., rank_count:],
        preferred_element_type=jnp.float32,
    )
    out_cols = got_up.shape[1]
    key_delta = delta_key.reshape(blocks_dev * BLK, out_cols).astype(jnp.bfloat16)
    value_delta = delta_value.reshape(blocks_dev * BLK, out_cols).astype(jnp.bfloat16)
    return (key_delta, value_delta)


def swap(value, step):
    count = lax.axis_size("wide")
    return lax.ppermute(value, "wide", [(i, i ^ step) for i in range(count)])


def swap_cores(value):
    count = lax.axis_size("wide")
    pairs = [[i, i + 1] for i in range(0, count, 2)]
    return lax.all_to_all(value, "wide", 0, 0, axis_index_groups=pairs, tiled=True)


def pick(index, values):
    got = values[0]
    for i in range(1, len(values)):
        got = jnp.where(index == i, values[i], got)
    return got


def landed(out, sem):
    pltpu.make_async_copy(out, out, sem).wait()


def slices(tokens_ref, column, run, out, sem, first=0):
    return [
        pltpu.make_async_copy(
            tokens_ref.at[:, pl.ds(pl.multiple_of(((first + piece) * PLANE + column) * run, run), run)],
            out.at[piece],
            sem,
        )
        for piece in range(out.shape[0])
    ]


def choose_kernel(
    planes, entry_hbm, adapter_hbm, counts_hbm, tokens_ref, down_ref, up_ref, table_ref, *refs
):
    others = planes - 1
    sends, tokens_out = refs[:others], refs[others : others + 3]
    entry_ref, adapter_ref, counts_ref, held_ref, small_sem, tokens_sem, sem = refs[others + 3 :]
    me = lax.axis_index("wide")
    column, plane = lax.rem(me, PLANE), lax.div(me, PLANE)
    run, up_run = down_ref.shape[2], up_ref.shape[2]
    small = [
        pltpu.make_async_copy(entry_hbm, entry_ref, small_sem.at[0]),
        pltpu.make_async_copy(adapter_hbm, adapter_ref, small_sem.at[1]),
        pltpu.make_async_copy(counts_hbm, counts_ref, small_sem.at[2]),
    ]
    for copy in small:
        copy.start()
    for i, (k, first) in enumerate(((2, 0), (3, 0), (3, planes))):
        for copy in slices(tokens_ref, column ^ k, run, tokens_out[i], tokens_sem.at[i], first):
            copy.start()
    for copy in small:
        copy.wait()

    requests = counts_ref.shape[0]
    ends, total = [], 0
    for q in range(requests):
        total = total + counts_ref[q]
        ends.append(total)
    entries = [entry_ref[adapter_ref[q]] for q in range(requests)]

    def listed(p):
        ids = []
        for i in range(PLANE):
            block = p * PLANE + jnp.where(p % 2 == 0, i, PLANE - 1 - i)
            got = entries[0]
            for q in range(1, requests):
                got = jnp.where(ends[q - 1] <= block, entries[q], got)
            ids.append(got)
        place, held, count = [jnp.int32(0)], [ids[0]] * SLOTS, jnp.int32(1)
        for i in range(1, PLANE):
            found = count
            for j in range(i):
                found = jnp.where(ids[i] == ids[j], place[j], found)
            place.append(found)
            held = [jnp.where(found == s, ids[i], held[s]) for s in range(SLOTS)]
            count = jnp.maximum(count, found + 1)
        return held, place, count

    most = jnp.int32(1)
    for d in (*range(2, planes), 1, 0):
        held, place, count = listed(plane ^ d)
        most = jnp.maximum(most, count)
        if d > 0:
            for s in range(sends[d - 1].shape[0]):
                out = sends[d - 1].at[s]
                for ref, at in (down_ref, pl.ds(0, run)), (up_ref, pl.ds(run, up_run)):
                    pltpu.make_async_copy(ref.at[held[s]], out.at[:, at], sem.at[d - 1]).start()
        else:
            for s in range(SLOTS):
                held_ref[PLANE + s] = held[s]
    for k in range(PLANE):
        i = column ^ k
        held_ref[k] = pick(jnp.where(plane % 2 == 0, i, PLANE - 1 - i), place)
    held_ref[PLANE + SLOTS] = jnp.where(most > USUAL, 1, 0)
    table = pltpu.make_async_copy(held_ref, table_ref, small_sem.at[3])
    table.start()
    for k, out in enumerate(tokens_out):
        landed(out, tokens_sem.at[k])
    for d, out in enumerate(sends):
        landed(out, sem.at[d])
    table.wait()


def choose(planes, tokens, down, up, entry, adapter, counts):
    hbm = pl.BlockSpec(memory_space=pltpu.HBM)
    others = planes - 1
    rows = (2, down.shape[2] + up.shape[2], down.shape[3])
    sends = [
        jax.ShapeDtypeStruct((SLOTS if d == 1 else USUAL,) + rows, down.dtype) for d in range(1, planes)
    ]
    return pl.pallas_call(
        lambda *refs: choose_kernel(planes, *refs),
        out_shape=[jax.ShapeDtypeStruct((PLANE + SLOTS + 1,), jnp.int32)]
        + sends
        + [
            jax.ShapeDtypeStruct((count, BLK, down.shape[2]), tokens.dtype)
            for count in (2 * planes, planes, planes)
        ],
        in_specs=[hbm] * 6,
        out_specs=[pl.BlockSpec(memory_space=pl.ANY)]
        + [pl.BlockSpec(memory_space=pltpu.VMEM)] * (others + 3),
        scratch_shapes=[
            pltpu.SMEM(entry.shape, jnp.int32),
            pltpu.SMEM(adapter.shape, jnp.int32),
            pltpu.SMEM(counts.shape, jnp.int32),
            pltpu.SMEM((PLANE + SLOTS + 1,), jnp.int32),
            pltpu.SemaphoreType.DMA((4,)),
            pltpu.SemaphoreType.DMA((3,)),
            pltpu.SemaphoreType.DMA((others,)),
        ],
        compiler_params=pltpu.CompilerParams(vmem_limit_bytes=57 * 2**20),
        name="choose",
    )(entry, adapter, counts, tokens, down, up)


def gather_kernel(planes, table_ref, tokens_ref, down_ref, up_ref, own_ref, pair_ref, tokens_sem, sem):
    column = lax.rem(lax.axis_index("wide"), PLANE)
    run, up_run = down_ref.shape[2], up_ref.shape[2]
    for core in range(2):
        at = lax.div(column, 2) * 2 + core
        for copy in slices(tokens_ref, at, run, pair_ref.at[core], tokens_sem.at[core]):
            copy.start()
    for s in range(SLOTS):
        slot = table_ref[PLANE + s]
        for ref, rows in (down_ref, pl.ds(0, run)), (up_ref, pl.ds(run, up_run)):
            pltpu.make_async_copy(ref.at[slot], own_ref.at[s, :, rows], sem).start()
    for core in range(2):
        landed(pair_ref.at[core], tokens_sem.at[core])
    landed(own_ref, sem)


def gather(planes, table, tokens, down, up):
    run = down.shape[2]
    hbm = pl.BlockSpec(memory_space=pltpu.HBM)
    rows = (2, run + up.shape[2], down.shape[3])
    return pl.pallas_call(
        lambda *refs: gather_kernel(planes, *refs),
        out_shape=[
            jax.ShapeDtypeStruct((SLOTS,) + rows, down.dtype),
        ]
        + [jax.ShapeDtypeStruct((2, 2 * planes, BLK, run), tokens.dtype)],
        in_specs=[pl.BlockSpec(memory_space=pltpu.SMEM)] + [hbm] * 3,
        out_specs=[pl.BlockSpec(memory_space=pltpu.VMEM)] * 2,
        scratch_shapes=[
            pltpu.SemaphoreType.DMA((2,)),
            pltpu.SemaphoreType.DMA(()),
        ],
        compiler_params=pltpu.CompilerParams(vmem_limit_bytes=57 * 2**20),
        name="gather",
    )(table, tokens, down, up)


def up_rows(factors, distances, place):
    rows = []
    for d in distances:
        slot = jnp.minimum(place, factors[d].shape[0] - 1)
        rows += [factors[d][slot, half] for half in range(2)]
    return rows


def rows_of_block(row_refs, core, k, half, plane, planes):
    if k < 2:
        return row_refs[0][core ^ k, half * planes + plane]
    return row_refs[1][half * planes + plane] if k == 2 else row_refs[2 + half][plane]


def shrink(
    planes,
    slots,
    run,
    blocks,
    near,
    first,
    far,
    places,
    rows,
    factors,
    held=(),
    ups=None,
    flops=None,
    flag=False,
):
    vmem, smem = pl.BlockSpec(memory_space=pltpu.VMEM), pl.BlockSpec(memory_space=pltpu.SMEM)
    up_run, ranks = factors[0].shape[2] - run, factors[0].shape[3]

    used = sorted({*first, *far})

    def kernel(places_ref, *refs):
        spread = len(places.shape) > 1
        row_refs, refs = refs[: len(rows)], refs[len(rows) :]
        factor_refs, refs = dict(zip(used, refs)), refs[len(used) :]
        held_refs, outs = list(refs[: len(held)]), refs[len(held) :]
        me = lax.axis_index("wide")
        core, plane = lax.rem(me, 2), lax.div(me, PLANE)
        at = [places_ref[k, pl.ds(0, 1)] if spread else places_ref[k] for k in blocks]
        views = {d: ref.at[:, :, pl.ds(run, up_run)] for d, ref in factor_refs.items()}

        def rows_of_up(place):
            if not spread:
                return up_rows(views, ups or (), place)
            return [
                pick(place, [views[d][s, half].astype(jnp.float32) for s in range(slots)])
                for d in ups or ()
                for half in range(2)
            ]

        def rows_at(k, half, place):
            return rows_of_block(row_refs, core, k, half, place, planes)

        def sums_of(chosen, distances):
            total = jnp.zeros((len(chosen) * BLK, slots * ranks), jnp.float32)
            for d in distances:
                for half in range(2):
                    total += jnp.dot(
                        jnp.concatenate([rows_at(blocks[i], half, plane ^ d) for i in chosen], axis=0),
                        jnp.concatenate(
                            [factor_refs[d][s, half, pl.ds(0, run)] for s in range(slots)], axis=1
                        ),
                        preferred_element_type=jnp.float32,
                    )
            parts = [total[j * BLK : (j + 1) * BLK] for j in range(len(chosen))]
            return {
                i: pick(at[i], [part[:, s * ranks : (s + 1) * ranks] for s in range(slots)])
                for i, part in zip(chosen, parts)
            }

        if flag:
            *outs, spread_ref, flag_ref = outs
            flag_ref[0] = places_ref[PLANE + SLOTS]
            for k in range(PLANE):
                spread_ref[k] = jnp.full(spread_ref.shape[1:], places_ref[k], jnp.int32)
        every = range(len(blocks))
        mine = sums_of(every, far) if far else {}
        here = [i for i in every if blocks[i] in near]
        for i, part in (sums_of(here, first) if here else {}).items():
            mine[i] = mine[i] + part if far else part
        for i in every:
            if i not in here:
                mine[i] = mine[i] + held_refs.pop(0)[...]
            outs[i][pl.ds(0, BLK)] = mine[i].astype(outs[i].dtype)
            for j, part in enumerate(rows_of_up(at[i])):
                outs[i][pl.ds(BLK + j * up_run, up_run)] = part.astype(outs[i].dtype)

    height = BLK + len(ups or ()) * 2 * up_run
    exact = [ups is None or k == 0 for k in blocks]
    cost = None
    if flops is not None:
        cost = pl.CostEstimate(flops=flops, bytes_accessed=0, transcendentals=0)
    return pl.pallas_call(
        kernel,
        out_shape=[
            jax.ShapeDtypeStruct((height, ranks), jnp.float32 if full else rows[0].dtype)
            for full in exact
        ]
        + [jax.ShapeDtypeStruct((PLANE, 8, ranks), jnp.int32), jax.ShapeDtypeStruct((1,), jnp.int32)]
        * flag,
        in_specs=[vmem if len(places.shape) > 1 else smem]
        + [vmem] * (len(rows) + len(used) + len(held)),
        out_specs=[vmem] * len(blocks) + [vmem, smem] * flag,
        compiler_params=pltpu.CompilerParams(vmem_limit_bytes=10 * 2**20),
        cost_estimate=cost,
        name="shrink",
    )(places, *rows, *[factors[d] for d in used], *held)


def amend(planes, run, places, rows, thirds, slots, sums, kept):
    vmem = pl.BlockSpec(memory_space=pltpu.VMEM)
    up_run, ranks = thirds[0].shape[2] - run, thirds[0].shape[3]

    def kernel(places_ref, *refs):
        row_refs, refs = refs[: len(rows)], refs[len(rows) :]
        third_refs, refs = refs[:planes], refs[planes:]
        sum_refs, outs = refs[:PLANE], refs[PLANE + len(kept) :]
        me = lax.axis_index("wide")
        core, plane = lax.rem(me, 2), lax.div(me, PLANE)
        total = jnp.zeros((PLANE * BLK, ranks), jnp.float32)
        for d in range(planes):
            for half in range(2):
                parts = [
                    rows_of_block(row_refs, core, k, half, plane ^ d, planes) for k in range(PLANE)
                ]
                total += jnp.dot(
                    jnp.concatenate(parts, axis=0),
                    third_refs[d][slots[d], half, pl.ds(0, run)],
                    preferred_element_type=jnp.float32,
                )
        for k in range(PLANE):
            anew = places_ref[k, pl.ds(0, 1)] == USUAL
            news = [(0, total[k * BLK : (k + 1) * BLK])]
            for d in range(planes):
                for half in range(2):
                    start = BLK + (2 * d + half) * up_run
                    news.append((start, third_refs[d][slots[d], half, pl.ds(run, up_run)]))
            for start, new in news:
                at = pl.ds(start, new.shape[0])
                old = sum_refs[k][at].astype(jnp.float32)
                outs[k][at] = jnp.where(anew, new.astype(jnp.float32), old).astype(outs[k].dtype)

    return pl.pallas_call(
        kernel,
        out_shape=[jax.ShapeDtypeStruct(value.shape, value.dtype) for value in sums],
        in_specs=[vmem] * (1 + len(rows) + planes + PLANE)
        + [pl.BlockSpec(memory_space=pl.ANY)] * len(kept),
        out_specs=[vmem] * PLANE,
        compiler_params=pltpu.CompilerParams(vmem_limit_bytes=10 * 2**20),
        name="amend",
    )(places, *rows, *thirds, *sums, *kept)


def expand(planes, up_run, sums):
    ranks = sums[0].shape[1]
    columns = 2 * planes * PLANE * up_run
    vmem = pl.BlockSpec(memory_space=pltpu.VMEM)
    span = 2 * up_run
    order = (2, 3, 1, 0)

    def kernel(*refs):
        sum_refs = dict(zip(order, refs))
        key_out, value_out, factor, key_ref, value_ref, sem = refs[PLANE:]
        me = lax.axis_index("wide")
        column, plane = lax.rem(me, PLANE), lax.div(me, PLANE)
        total = jnp.zeros((BLK, ranks), jnp.float32)
        for k in range(PLANE):
            total += sum_refs[k][pl.ds(0, BLK)].astype(jnp.float32)
            for d in range(planes):
                rows = sum_refs[k][pl.ds(BLK + d * span, span)]
                factor[plane ^ d, :, column ^ k] = rows.astype(factor.dtype).reshape(2, up_run, ranks)
        low_rank = total.astype(jnp.bfloat16)
        is_key = lax.broadcasted_iota(jnp.int32, low_rank.shape, 1) < ranks // 2
        zero = jnp.zeros_like(low_rank)
        both = jnp.concatenate(
            [jnp.where(is_key, low_rank, zero), jnp.where(is_key, zero, low_rank)], axis=0
        )
        copies = []
        for half in range(2):
            for p in range(planes):
                delta = lax.dot_general(
                    both,
                    factor[p, half].reshape(PLANE * up_run, ranks),
                    (((1,), (1,)), ((), ())),
                    preferred_element_type=jnp.float32,
                ).astype(jnp.bfloat16)
                at = pl.ds((half * planes + p) * PLANE * up_run, PLANE * up_run)
                key_ref[:, at] = delta[:BLK]
                value_ref[:, at] = delta[BLK:]
            at = pl.ds(half * (columns // 2), columns // 2)
            for i, (held, out) in enumerate(((key_ref, key_out), (value_ref, value_out))):
                copies.append(pltpu.make_async_copy(held.at[:, at], out.at[:, at], sem.at[half, i]))
                copies[-1].start()
        for copy in copies:
            copy.wait()

    return pl.pallas_call(
        kernel,
        out_shape=[jax.ShapeDtypeStruct((BLK, columns), jnp.bfloat16)] * 2,
        in_specs=[vmem] * PLANE,
        out_specs=[pl.BlockSpec(memory_space=pl.ANY)] * 2,
        scratch_shapes=[
            pltpu.VMEM((planes, 2, PLANE, up_run, ranks), jnp.bfloat16),
            pltpu.VMEM((BLK, columns), jnp.bfloat16),
            pltpu.VMEM((BLK, columns), jnp.bfloat16),
            pltpu.SemaphoreType.DMA((2, 2)),
        ],
        compiler_params=pltpu.CompilerParams(vmem_limit_bytes=4 * 2**20),
        name="expand",
    )(*[sums[k] for k in order])


def plane_body(
    tokens,
    adapter_down_weight,
    adapter_up_weight,
    adapter_entry,
    adapter_of_request,
    token_blocks_per_request,
):
    planes = lax.axis_size("wide") // PLANE
    places, *sends = choose(
        planes,
        tokens,
        adapter_down_weight,
        adapter_up_weight,
        adapter_entry,
        adapter_of_request,
        token_blocks_per_request,
    )
    factors, across = sends[: planes - 1], sends[planes - 1 :]
    own_factors, pair = gather(planes, places, tokens, adapter_down_weight, adapter_up_weight)
    sends = sends + [pair]
    run, up_run = adapter_down_weight.shape[2], adapter_up_weight.shape[2]
    whole, blocks = tuple(range(planes)), tuple(range(PLANE))
    factors = [own_factors] + [swap(factors[d - 1], d * PLANE) for d in whole[1:]]
    rows = [swap_cores(pair)] + [swap(value, k) for value, k in zip(across, (2, 3, 3))]
    early = (0, 2)
    *held, spread, many = shrink(
        planes,
        USUAL,
        run,
        blocks[:2],
        blocks[:2],
        early,
        (),
        places,
        rows[:1],
        factors,
        flops=None,
        flag=True,
    )

    def finish(sums):
        sums = [sums[0]] + [swap(sums[k], k) for k in range(1, PLANE)]
        return tuple(expand(planes, up_run, sums))

    def sums_of(spread, factors, rows, held):
        args = (early, (1, 3), spread, rows, factors)
        sums = shrink(planes, USUAL, run, blocks[1:], blocks[2:], *args, held[1:], whole)
        return [*shrink(planes, USUAL, run, blocks[:1], (), *args, held[:1], whole), *sums]

    def usual(spread, factors, rows, held, kept):
        return finish(sums_of(spread, factors, rows, held))

    def more(spread, factors, rows, held, kept):
        thirds = factors[:2] + [swap(factors[d ^ 1][:1], PLANE) for d in whole[2:]]
        slots = [USUAL if d < 2 else 0 for d in whole]
        sums = sums_of(spread, factors, rows, held)
        return finish(amend(planes, run, spread, rows, thirds, slots, sums, kept))

    return lax.switch(many[0], [usual, more], spread, factors, rows, held, sends)


def solution(mesh):
    by_plane = mesh.shape["wide"] == 16 and mesh.shape["narrow"] == 1
    return jax.shard_map(
        plane_body if by_plane else direct_body,
        mesh=mesh,
        in_specs=(
            P(("groups", "wide"), "narrow"),
            P(None, "narrow", "wide", None),
            P(None, "narrow", "wide", None),
            P(),
            P("groups"),
            P("groups"),
        ),
        out_specs=(P(("groups", "wide"), "narrow"), P(("groups", "wide"), "narrow")),
        check_vma=False,
    )
```
